32 devices in a mesh: dp: 8 (over y, x, core), tensor: 4 (over z).
Axes of the slice: x: 2, y: 2, z: 4, core: 2. Of those that a mesh axis runs over, the one named last changes fastest.
Arguments:
- inputs: bfloat16 [2, 8, 1024, 768], P(None, 'dp'), may hold values from -6 to 6
- memory: bfloat16 [2, 8, 1024, 768], P(None, 'dp'), may hold values from -6 to 6
- cotangent: bfloat16 [2, 8, 1024, 768], P(None, 'dp', 'tensor'), may hold values from -6 to 6
- dec_len: int32 [2, 8], P(None, 'dp'), may hold values from 128 to 1024, as said below
- mem_len: int32 [2, 8], P(None, 'dp'), may hold values from 128 to 1024, as said below
- self_qkv: bfloat16 [3, 768, 768], P(None, None, 'tensor'), may hold values from -0.21875 to 0.21875
- self_out: bfloat16 [768, 768], P('tensor'), may hold values from -0.875 to 0.875
- cross_q: bfloat16 [768, 768], P(None, 'tensor'), may hold values from -0.21875 to 0.21875
- cross_kv: bfloat16 [2, 768, 768], P(None, None, 'tensor'), may hold values from -0.21875 to 0.21875
- cross_out: bfloat16 [768, 768], P('tensor'), may hold values from -0.875 to 0.875
- ffn_in: bfloat16 [768, 3072], P(None, 'tensor'), may hold values from -0.21875 to 0.21875
- ffn_out: bfloat16 [3072, 768], P('tensor'), may hold values from -0.109375 to 0.109375
- ln_gain: float32 [3, 768], replicated, may hold values from 0.5 to 1.5
- ln_bias: float32 [3, 768], replicated, may hold values from -3 to 3
Outputs:
- out: bfloat16 [2, 8, 1024, 768], P(None, 'dp', 'tensor')
- d_inputs: float32 [2, 8, 1024, 768], P(None, 'dp', 'tensor')
- d_memory: float32 [2, 8, 1024, 768], P(None, 'dp', 'tensor')
- d_self_qkv: float32 [3, 768, 768], P(None, None, 'tensor')
- d_self_out: float32 [768, 768], P('tensor')
- d_cross_q: float32 [768, 768], P(None, 'tensor')
- d_cross_kv: float32 [2, 768, 768], P(None, None, 'tensor')
- d_cross_out: float32 [768, 768], P('tensor')
- d_ffn_in: float32 [768, 3072], P(None, 'tensor')
- d_ffn_out: float32 [3072, 768], P('tensor')
- d_gain: float32 [3, 768], replicated
- d_bias: float32 [3, 768], replicated
The draws below stay inside these ranges and needn't reach their ends.
Inputs may be any that keep to these rules, and one draw needn't show every extreme that they name: `dec_len`: in every micro-batch some sequence has all 1024 positions valid. `mem_len`: in every micro-batch some memory has all 1024 positions valid.
All inputs are finite; a program needn't handle non-finite values.
Results may differ from the reference program's by a relative error of at most 0.019.
Values may be sent and summed in bfloat16 or wider, within the bound.
No kernel may reach another device: no remote copies, remote signals or barrier semaphores. Data moves between devices by JAX's collectives and lax.ppermute only.
A program may use at most 192 MiB of HBM per device.

```python
from functools import partial
import jax
import jax.numpy as jnp
from jax import lax

D = 768
HEAD = 64
FF = 3072
L = 1024
M = 1024
MB = 2
BATCH = 8


def ragged(key, longest):
    first_key, second_key = jax.random.split(key)
    lengths = jax.random.randint(first_key, (MB, BATCH), longest // 8, longest + 1)
    chosen = jax.random.randint(second_key, (MB, 1), 0, BATCH)
    spots = jnp.arange(BATCH)[None, :]
    return jnp.where(spots == chosen, longest, lengths).astype(jnp.int32)


def draw_dec_len(key, part):
    key = jax.random.fold_in(key, 5)
    return ragged(key, L)


def draw_mem_len(key, part):
    key = jax.random.fold_in(key, 9)
    return ragged(key, M)


def levels(stream_key, shape, shards, smallest, high):
    def one(axis_at, blocks):
        heights = jax.random.uniform(jax.random.fold_in(jax.random.fold_in(stream_key, 6), axis_at), (blocks,), jnp.float32, smallest / len(shards), high / len(shards))
        return jnp.repeat(jnp.exp(heights), shape[axis_at] // blocks).reshape((-1,) + (1,) * (len(shape) - axis_at - 1))

    factor_of = one(*shards[0])
    for cut in shards[1:]:
        factor_of = factor_of * one(*cut)
    return factor_of


def noise(stream_key, shape, scale, limit, shards=(), kind=jnp.bfloat16):
    entries = jax.random.normal(stream_key, shape, jnp.float32) * scale
    if len(shards) > 0:
        entries = levels(stream_key, shape, shards, -0.22, 0.18) * entries
    return jnp.clip(entries, min=-limit, max=limit).astype(kind)


def setup_inputs(seed: int = 0) -> dict:
    keys = jax.random.split(jax.random.key(seed), 15)
    inputs = noise(keys[0], (MB, BATCH, L, D), 1.0, 6.0, ((1, 8),))
    memory = noise(keys[1], (MB, BATCH, M, D), 1.0, 6.0, ((1, 8),))
    cotangent = noise(keys[2], (MB, BATCH, L, D), 1.0, 6.0, ((1, 8), (2, 4)))
    dec_len = draw_dec_len(jax.random.fold_in(keys[14], 71), 0)
    mem_len = draw_mem_len(jax.random.fold_in(keys[14], 71), 0)
    self_qkv = noise(keys[5], (3, D, D), D ** -0.5, 0.21875, ((2, 4),))
    self_out = noise(keys[6], (D, D), (D // 16) ** -0.5, 0.875, ((0, 4),))
    cross_q = noise(keys[7], (D, D), D ** -0.5, 0.21875, ((1, 4),))
    cross_kv = noise(keys[8], (2, D, D), D ** -0.5, 0.21875, ((2, 4),))
    cross_out = noise(keys[9], (D, D), (D // 16) ** -0.5, 0.875, ((0, 4),))
    ffn_in = noise(keys[10], (D, FF), D ** -0.5, 0.21875, ((1, 4),))
    ffn_out = noise(keys[11], (FF, D), FF ** -0.5, 0.109375, ((0, 4),))
    ln_gain = jnp.clip(1.0 + 0.1 * jax.random.normal(keys[12], (3, D), jnp.float32), 0.5, 1.5)
    ln_bias = noise(keys[13], (3, D), 0.5, 3.0, (), jnp.float32)
    return dict(inputs=inputs, memory=memory, cotangent=cotangent, dec_len=dec_len, mem_len=mem_len, self_qkv=self_qkv, self_out=self_out, cross_q=cross_q, cross_kv=cross_kv, cross_out=cross_out, ffn_in=ffn_in, ffn_out=ffn_out, ln_gain=ln_gain, ln_bias=ln_bias)


EPS = 1e-05

@jax.custom_vjp
def low(v):
    return lax.optimization_barrier(v.astype(jnp.bfloat16)).astype(jnp.float32)

@jax.custom_vjp
def low_back(v):
    return v

def low_keep(v):
    return (low(v), None)

def low_pass(kept, grad):
    return (grad,)

def back_keep(v):
    return (v, None)

def back_low(kept, grad):
    return (low(grad),)
low.defvjp(low_keep, low_pass)
low_back.defvjp(back_keep, back_low)

def round_both(value):
    return low_back(low(value))

def product(left, right):
    return jnp.matmul(left, right, precision=lax.Precision.HIGHEST)

def norm_rows(resid, gain, shift):
    center = resid - lax.optimization_barrier(jnp.mean(resid, -1, keepdims=True))
    spread = lax.optimization_barrier(jnp.mean(center * center, -1, keepdims=True))
    return center * lax.rsqrt(spread + EPS) * gain + shift

def attend(query, keys_in, values_in, allowed):
    query_rows = query.shape[0]
    query_h = query.reshape(query_rows, -1, HEAD)
    keys_h = keys_in.reshape(keys_in.shape[0], -1, HEAD)
    values_h = values_in.reshape(values_in.shape[0], -1, HEAD)
    scores = jnp.einsum('qhd,khd->hqk', query_h, keys_h, precision=lax.Precision.HIGHEST) * HEAD ** (-0.5)
    scores = low_back(scores)
    scores = jnp.where(allowed[None], scores, -1e+30)
    row_peak = lax.optimization_barrier(jnp.max(scores, -1, keepdims=True))
    exp_scores = jnp.exp(scores - row_peak)
    softmax_w = low(exp_scores / lax.optimization_barrier(jnp.sum(exp_scores, -1, keepdims=True)))
    mixed = jnp.einsum('hqk,khd->qhd', softmax_w, values_h, precision=lax.Precision.HIGHEST)
    return round_both(mixed.reshape(query_rows, -1))

def decoder_layer(params, x_seq, mem_seq, dec_one, mem_one):
    w_qkv, w_self, w_query, w_kv, w_cross, w_up, w_down, gains, shifts = params
    positions = jnp.arange(L, dtype=jnp.int32)
    mask_self = (positions[None, :] <= positions[:, None]) & (positions[None, :] < dec_one)
    mask_cross = jnp.broadcast_to(jnp.arange(M, dtype=jnp.int32)[None, :] < mem_one, (L, M))
    query_s = round_both(product(x_seq, w_qkv[0]))
    keys_s = round_both(product(x_seq, w_qkv[1]))
    values_s = round_both(product(x_seq, w_qkv[2]))
    branch_one = low_back(product(attend(query_s, keys_s, values_s, mask_self), w_self))
    normed_one = norm_rows(x_seq + branch_one, gains[0], shifts[0])
    query_c = round_both(product(low(normed_one), w_query))
    keys_c = round_both(product(mem_seq, w_kv[0]))
    values_c = round_both(product(mem_seq, w_kv[1]))
    branch_two = low_back(product(attend(query_c, keys_c, values_c, mask_cross), w_cross))
    normed_two = norm_rows(normed_one + branch_two, gains[1], shifts[1])
    hidden_pre = low_back(product(low(normed_two), w_up))
    hidden_act = low(jax.nn.gelu(hidden_pre, approximate=False))
    branch_three = low_back(product(hidden_act, w_down))
    return norm_rows(normed_two + branch_three, gains[2], shifts[2])

def reference(inputs, memory, cotangent, dec_len, mem_len, self_qkv, self_out, cross_q, cross_kv, cross_out, ffn_in, ffn_out, ln_gain, ln_bias):
    params = (self_qkv.astype(jnp.float32), self_out.astype(jnp.float32), cross_q.astype(jnp.float32), cross_kv.astype(jnp.float32), cross_out.astype(jnp.float32), ffn_in.astype(jnp.float32), ffn_out.astype(jnp.float32), ln_gain.astype(jnp.float32), ln_bias.astype(jnp.float32))
    seq_total = MB * BATCH
    inputs_all = inputs.astype(jnp.float32).reshape(seq_total, L, D)
    memory_all = memory.astype(jnp.float32).reshape(seq_total, M, D)
    lengths_dec = dec_len.reshape(seq_total).astype(jnp.int32)
    lengths_mem = mem_len.reshape(seq_total).astype(jnp.int32)

    def forward(weights_all, inputs_f, memory_f):
        step_fn = jax.checkpoint(partial(decoder_layer, weights_all))

        def one_item(seq_item):
            return step_fn(seq_item[0], seq_item[1], seq_item[2], seq_item[3])
        return lax.map(one_item, (inputs_f, memory_f, lengths_dec, lengths_mem))
    outputs_all, pullback = jax.vjp(forward, params, inputs_all, memory_all)
    grad_params, grad_inputs, grad_memory = pullback(cotangent.astype(jnp.float32).reshape(seq_total, L, D))
    return (outputs_all.astype(jnp.bfloat16).reshape(MB, BATCH, L, D), grad_inputs.reshape(MB, BATCH, L, D), grad_memory.reshape(MB, BATCH, M, D), grad_params[0], grad_params[1], grad_params[2], grad_params[3], grad_params[4], grad_params[5], grad_params[6], grad_params[7], grad_params[8])
```

```python
import functools

import jax
import jax.numpy as jnp
from jax import lax
from jax.experimental import pallas as pl
from jax.experimental.pallas import tpu as pltpu
from jax.sharding import PartitionSpec as P

HEAD = 64
EPS = 1e-05
NEG = -1e30
LOW = jnp.bfloat16
F32 = jnp.float32
OWN_BLOCKS = ((0, 3), (1, 2))
MIB = 1024 * 1024


def dot_nn(left, right):
    return lax.dot_general(left, right, (((1,), (0,)), ((), ())), preferred_element_type=F32)


def dot_nt(left, right):
    return lax.dot_general(left, right, (((1,), (1,)), ((), ())), preferred_element_type=F32)


def dot_tn(left, right):
    return lax.dot_general(left, right, (((0,), (0,)), ((), ())), preferred_element_type=F32)


def cost(flops, size, trans=0):
    return pl.CostEstimate(flops=int(flops), bytes_accessed=int(size), transcendentals=int(trans))


def whole(shape):
    return pl.BlockSpec(shape, lambda *_: (0,) * len(shape), pipeline_mode=pl.Buffered(1))


def attend_forward(causal, info, query, keys_in, values_in):
    rows, width = query.shape
    key_rows = keys_in.shape[0]
    block = rows // 2
    pair = 2 * HEAD

    def kernel(info_ref, q_ref, k_ref, v_ref, o_ref, lse_ref):
        length = info_ref[1]

        def part(spot, block_id, extent):
            lane = lax.broadcasted_iota(jnp.int32, (block, pair), 1)
            limit = jnp.full((block, 1), length, jnp.int32)
            if causal:
                row = block_id * block + lax.broadcasted_iota(jnp.int32, (block, 1), 0)
                limit = jnp.minimum(limit, row + 1)
            allowed = lax.broadcasted_iota(jnp.int32, (block, extent), 1) < limit
            span = pl.ds(spot * block, block)
            q = q_ref[span, :]
            out, logs = None, None
            for side in range(2):
                mine = (lane >= HEAD) if side else (lane < HEAD)
                q_side = jnp.where(mine, q, 0).astype(LOW) * LOW(HEAD ** (-0.5))
                scores = jnp.where(allowed, dot_nt(q_side, k_ref[:extent, :]), NEG)
                peak = jnp.max(scores, -1, keepdims=True)
                weights = jnp.exp(scores - peak)
                total = jnp.sum(weights, -1, keepdims=True)
                mixed = dot_nn(weights.astype(LOW), v_ref[:extent, :]) / total
                log_total = peak + jnp.log(total)
                if side:
                    out = jnp.where(mine, mixed, out)
                    logs = jnp.where(mine, log_total, logs)
                else:
                    out, logs = mixed, jnp.broadcast_to(log_total, (block, pair))
            o_ref[span, :] = out.astype(LOW)
            lse_ref[span, :] = logs

        if causal:
            for variant in range(2):

                @pl.when(info_ref[0] == variant)
                def _():
                    for spot in range(2):
                        block_id = OWN_BLOCKS[variant][spot]
                        part(spot, block_id, (block_id + 1) * block)
        else:
            for spot in range(2):
                part(spot, 0, key_rows)

    column = pl.BlockSpec((rows, pair), lambda p, *_: (0, p))
    key_column = pl.BlockSpec((key_rows, pair), lambda p, *_: (0, p))
    share = 0.625 if causal else 1.0
    elements = width // HEAD * rows * key_rows * share
    return pl.pallas_call(
        kernel,
        out_shape=(
            jax.ShapeDtypeStruct((rows, width), LOW),
            jax.ShapeDtypeStruct((rows, width), F32),
        ),
        grid_spec=pltpu.PrefetchScalarGridSpec(
            num_scalar_prefetch=1,
            grid=(width // pair,),
            in_specs=[column, key_column, key_column],
            out_specs=[column, column],
        ),
        compiler_params=pltpu.CompilerParams(vmem_limit_bytes=48 * MIB),
        cost_estimate=cost(elements * 1024, 10 * MIB, elements),
    )(info, query, keys_in, values_in)


def attend_backward(causal, info, query, keys_in, values_in, out, logs, grad_out):
    rows, width = query.shape
    key_rows = keys_in.shape[0]
    block = rows // 2
    pair = 2 * HEAD

    def kernel(
        info_ref, q_ref, k_ref, v_ref, o_ref, lse_ref, g_ref,
        dq_ref, dk_ref, dv_ref, dks_ref, dvs_ref, dk_acc, dv_acc,
    ):
        length = info_ref[1]
        dk_acc[...] = jnp.zeros_like(dk_acc)
        dv_acc[...] = jnp.zeros_like(dv_acc)

        def part(spot, block_id, extent):
            lane = lax.broadcasted_iota(jnp.int32, (block, pair), 1)
            limit = jnp.full((block, 1), length, jnp.int32)
            if causal:
                row = block_id * block + lax.broadcasted_iota(jnp.int32, (block, 1), 0)
                limit = jnp.minimum(limit, row + 1)
            allowed = lax.broadcasted_iota(jnp.int32, (block, extent), 1) < limit
            span = pl.ds(spot * block, block)
            q = q_ref[span, :]
            g = g_ref[span, :]
            along = g.astype(F32) * o_ref[span, :].astype(F32)
            dq = None
            for side in range(2):
                mine = (lane >= HEAD) if side else (lane < HEAD)
                q_side = jnp.where(mine, q, 0).astype(LOW) * LOW(HEAD ** (-0.5))
                g_side = jnp.where(mine, g, 0).astype(LOW)
                inner = jnp.sum(jnp.where(mine, along, 0.0), -1, keepdims=True)
                log_total = lse_ref[span, side * HEAD : side * HEAD + 1]
                scores = jnp.where(allowed, dot_nt(q_side, k_ref[:extent, :]), NEG)
                weights = jnp.exp(scores - log_total)
                dv_acc[:extent, :] += dot_tn(weights.astype(LOW), g_side)
                grad_w = dot_nt(g_side, v_ref[:extent, :])
                grad_s = (weights * (grad_w - inner)).astype(LOW)
                dk_acc[:extent, :] += dot_tn(grad_s, q_side)
                part_q = dot_nn(grad_s, k_ref[:extent, :])
                dq = jnp.where(mine, part_q, dq) if side else part_q
            dq_ref[span, :] = (dq * HEAD ** (-0.5)).astype(LOW)

        for variant in range(2):

            @pl.when(info_ref[0] == variant)
            def _():
                for spot in range(2):
                    block_id = OWN_BLOCKS[variant][spot]
                    part(spot, block_id, (block_id + 1) * block if causal else key_rows)
                for spot in range(2):
                    keep = slice(OWN_BLOCKS[variant][spot] * block, (OWN_BLOCKS[variant][spot] + 1) * block)
                    give = slice(OWN_BLOCKS[1 - variant][spot] * block, (OWN_BLOCKS[1 - variant][spot] + 1) * block)
                    span = slice(spot * block, (spot + 1) * block)
                    dk_ref[span, :] = dk_acc[keep, :].astype(LOW)
                    dv_ref[span, :] = dv_acc[keep, :].astype(LOW)
                    dks_ref[span, :] = dk_acc[give, :].astype(LOW)
                    dvs_ref[span, :] = dv_acc[give, :].astype(LOW)

    column = pl.BlockSpec((rows, pair), lambda p, *_: (0, p))
    key_column = pl.BlockSpec((key_rows, pair), lambda p, *_: (0, p))
    share = 0.625 if causal else 1.0
    elements = width // HEAD * rows * key_rows * share
    return pl.pallas_call(
        kernel,
        out_shape=(jax.ShapeDtypeStruct((rows, width), LOW),) * 5,
        grid_spec=pltpu.PrefetchScalarGridSpec(
            num_scalar_prefetch=1,
            grid=(width // pair,),
            in_specs=[column, key_column, key_column, column, column, column],
            out_specs=[column] * 5,
            scratch_shapes=[pltpu.VMEM((key_rows, pair), F32), pltpu.VMEM((key_rows, pair), F32)],
        ),
        compiler_params=pltpu.CompilerParams(vmem_limit_bytes=48 * MIB),
        cost_estimate=cost(elements * 2560, 10 * MIB, elements),
    )(info, query, keys_in, values_in, out, logs, grad_out)


def normalize(resid):
    center = resid - jnp.mean(resid, -1, keepdims=True)
    rstd = lax.rsqrt(jnp.mean(center * center, -1, keepdims=True) + EPS)
    return center * rstd, rstd


def norm_back(grad, gain, normed, rstd):
    dn = grad * gain
    mean_dn = jnp.mean(dn, -1, keepdims=True)
    mean_dnn = jnp.mean(dn * normed, -1, keepdims=True)
    return rstd * (dn - mean_dn - normed * mean_dnn)


def row_sum(value):
    return jnp.sum(value, 0, keepdims=True)


def first_norm(attn, x_rows, w_out, w_query, gain, shift):
    rows, width = attn.shape
    block = min(256, rows)

    def kernel(o_ref, x_ref, wo_ref, wq_ref, g_ref, s_ref, n_ref, r_ref, h_ref, q_ref):
        normed, rstd = normalize(x_ref[...].astype(F32) + dot_nn(o_ref[...], wo_ref[...]))
        n_ref[...] = normed
        r_ref[...] = jnp.broadcast_to(rstd, r_ref.shape)
        low = (normed * g_ref[0:1, :] + s_ref[0:1, :]).astype(LOW)
        h_ref[...] = low
        q_ref[...] = dot_nt(low, wq_ref[...]).astype(LOW)

    row = pl.BlockSpec((block, width), lambda b: (b, 0))
    thin = pl.BlockSpec((block, 128), lambda b: (b, 0))
    return pl.pallas_call(
        kernel,
        grid=(rows // block,),
        out_shape=(
            jax.ShapeDtypeStruct((rows, width), F32),
            jax.ShapeDtypeStruct((rows, 128), F32),
            jax.ShapeDtypeStruct((rows, width), LOW),
            jax.ShapeDtypeStruct((rows, width), LOW),
        ),
        in_specs=[row, row, whole(w_out.shape), whole(w_query.shape), whole(gain.shape), whole(shift.shape)],
        out_specs=[row, thin, row, row],
        compiler_params=pltpu.CompilerParams(vmem_limit_bytes=40 * MIB),
        cost_estimate=cost(4 * rows * width * width, 8 * MIB),
    )(attn, x_rows, w_out, w_query, gain, shift)


def gelu_parts(u):
    t = 1.0 / (1.0 + (0.3275911 * 0.7071067811865476) * jnp.abs(u))
    bell = jnp.exp(-0.5 * u * u)
    poly = t * (0.254829592 + t * (-0.284496736 + t * (1.421413741 + t * (-1.453152027 + t * 1.061405429))))
    tail = 0.5 * poly * bell
    return jnp.where(u < 0, tail, 1.0 - tail), bell * 0.3989422804014327


def middle(normed_one, attn, grad_y, w_out, w_up, w_down, gain, shift):
    rows, width = attn.shape
    hidden = w_up.shape[0]
    block = min(128, rows)
    step = min(768, hidden)

    def kernel(
        n0_ref, o_ref, y_ref, wo_ref, up_ref, dn_ref, g_ref, s_ref,
        out_ref, a_ref, du_ref, db3_ref, h2_ref, db2_ref, do_ref, dr2_ref, sums_ref, slope_ref,
    ):
        @pl.when(pl.program_id(0) == 0)
        def _():
            sums_ref[...] = jnp.zeros_like(sums_ref)

        h1 = n0_ref[...] * g_ref[0:1, :] + s_ref[0:1, :]
        n1, rstd1 = normalize(h1 + dot_nn(o_ref[...], wo_ref[...]))
        h2 = n1 * g_ref[1:2, :] + s_ref[1:2, :]
        h2_low = h2.astype(LOW)
        h2_ref[...] = h2_low
        branch = None
        for start in range(0, hidden, step):
            span = slice(start, start + step)
            u = dot_nt(h2_low, up_ref[span, :])
            share, density = gelu_parts(u)
            slope_ref[:, span] = share + u * density
            a = (u * share).astype(LOW)
            a_ref[:, span] = a
            term = dot_nn(a, dn_ref[span, :])
            branch = term if branch is None else branch + term
        n2, rstd2 = normalize(h2 + branch)
        out_ref[...] = (n2 * g_ref[2:3, :] + s_ref[2:3, :]).astype(LOW)
        g = y_ref[...].astype(F32)
        sums_ref[2:3, :] += row_sum(g * n2)
        sums_ref[5:6, :] += row_sum(g)
        dr3 = norm_back(g, g_ref[2:3, :], n2, rstd2)
        db3 = dr3.astype(LOW)
        db3_ref[...] = db3
        dh2 = dr3
        for start in range(0, hidden, step):
            span = slice(start, start + step)
            du = (dot_nt(db3, dn_ref[span, :]) * slope_ref[:, span]).astype(LOW)
            du_ref[:, span] = du
            dh2 = dh2 + dot_nn(du, up_ref[span, :])
        sums_ref[1:2, :] += row_sum(dh2 * n1)
        sums_ref[4:5, :] += row_sum(dh2)
        dr2 = norm_back(dh2, g_ref[1:2, :], n1, rstd1)
        dr2_ref[...] = dr2
        db2 = dr2.astype(LOW)
        db2_ref[...] = db2
        do_ref[...] = dot_nt(db2, wo_ref[...]).astype(LOW)

    row = pl.BlockSpec((block, width), lambda b: (b, 0))
    broad = pl.BlockSpec((block, hidden), lambda b: (b, 0))
    low_row = jax.ShapeDtypeStruct((rows, width), LOW)
    low_broad = jax.ShapeDtypeStruct((rows, hidden), LOW)
    return pl.pallas_call(
        kernel,
        grid=(rows // block,),
        out_shape=(
            low_row, low_broad, low_broad, low_row, low_row, low_row, low_row,
            jax.ShapeDtypeStruct((rows, width), F32),
            jax.ShapeDtypeStruct((8, width), F32),
        ),
        in_specs=[
            row, row, row, whole(w_out.shape), whole(w_up.shape), whole(w_down.shape),
            whole(gain.shape), whole(shift.shape),
        ],
        out_specs=[
            row, broad, broad, row, row, row, row, row,
            pl.BlockSpec((8, width), lambda b: (0, 0)),
        ],
        scratch_shapes=[pltpu.VMEM((block, hidden), F32)],
        compiler_params=pltpu.CompilerParams(vmem_limit_bytes=50 * MIB),
        cost_estimate=cost(rows * width * (8 * hidden + 4 * width), 24 * MIB, rows * hidden),
    )(normed_one, attn, grad_y, w_out, w_up, w_down, gain, shift)


def first_norm_back(grad_resid, grad_query, normed_one, rstd_one, w_query, w_out, gain):
    rows, width = grad_resid.shape
    block = min(256, rows)

    def kernel(dr2_ref, dq_ref, n_ref, r_ref, wq_ref, wo_ref, g_ref, dr1_ref, db1_ref, do_ref, sums_ref):
        @pl.when(pl.program_id(0) == 0)
        def _():
            sums_ref[...] = jnp.zeros_like(sums_ref)

        normed = n_ref[...]
        dh1 = dr2_ref[...] + dot_nn(dq_ref[...], wq_ref[...])
        sums_ref[0:1, :] += row_sum(dh1 * normed)
        sums_ref[3:4, :] += row_sum(dh1)
        dr1 = norm_back(dh1, g_ref[0:1, :], normed, r_ref[:, 0:1])
        dr1_ref[...] = dr1
        db1 = dr1.astype(LOW)
        db1_ref[...] = db1
        do_ref[...] = dot_nt(db1, wo_ref[...]).astype(LOW)

    row = pl.BlockSpec((block, width), lambda b: (b, 0))
    thin = pl.BlockSpec((block, 128), lambda b: (b, 0))
    low_row = jax.ShapeDtypeStruct((rows, width), LOW)
    return pl.pallas_call(
        kernel,
        grid=(rows // block,),
        out_shape=(
            jax.ShapeDtypeStruct((rows, width), F32), low_row, low_row,
            jax.ShapeDtypeStruct((8, width), F32),
        ),
        in_specs=[row, row, row, thin, whole(w_query.shape), whole(w_out.shape), whole(gain.shape)],
        out_specs=[row, row, row, pl.BlockSpec((8, width), lambda b: (0, 0))],
        compiler_params=pltpu.CompilerParams(vmem_limit_bytes=40 * MIB),
        cost_estimate=cost(4 * rows * width * width, 8 * MIB),
    )(grad_resid, grad_query, normed_one, rstd_one, w_query, w_out, gain)


def swap(value, axis, bit, size):
    return lax.ppermute(value, axis, [(d, d ^ bit) for d in range(size)])


def ordered(own, other, bit, axis):
    low = jnp.where(bit, other, own)
    high = jnp.where(bit, own, other)
    return jnp.concatenate([low, high], axis)


class Place:
    def __init__(self):
        self.dp = lax.axis_size("dp")
        self.tensor = lax.axis_size("tensor")
        index = lax.axis_index("dp")
        self.z = lax.axis_index("tensor")
        self.core = index & 1
        self.bits = {2: (index >> 1) & 1, 4: (index >> 2) & 1}


def gather_weights(place, shard, order):
    count, rows, width = shard.shape
    half, quarter = width // 2, rows // 4
    first, second = order
    at_row = (2 * place.bits[first] + place.bits[second]) * quarter
    piece = lax.dynamic_slice(
        shard, (0, at_row, place.core * half), (count, quarter, half)
    )
    got = jnp.stack([swap(piece, "tensor", r, place.tensor) for r in range(1, place.tensor)], 1)
    got = ordered(got, swap(got, "dp", second, place.dp), place.bits[second] == 1, 2)
    got = ordered(got, swap(got, "dp", first, place.dp), place.bits[first] == 1, 2)
    got = ordered(got, swap(got, "dp", 1, place.dp), place.core == 1, 3)
    return jnp.concatenate([shard[:, None], got], 1)


def reduce_grads(place, pairs, order):
    width = pairs[0][1].shape[1]
    half = width // 2
    slots = place.tensor
    rows = pairs[0][0].shape[1] // slots
    first, second = order

    def product(at):
        return jnp.stack(
            [dot_tn(g, lax.dynamic_slice_in_dim(a, at, half, 1)) for g, a in pairs]
        ).reshape(len(pairs), slots, rows, half)

    give = product((1 - place.core) * half).astype(LOW)
    total = product(place.core * half) + swap(give, "dp", 1, place.dp).astype(F32)
    for bit in order:
        rows = rows // 2
        mine = place.bits[bit]
        give = lax.dynamic_slice_in_dim(total, (1 - mine) * rows, rows, 2).astype(LOW)
        keep = lax.dynamic_slice_in_dim(total, mine * rows, rows, 2)
        total = keep + swap(give, "dp", bit, place.dp).astype(F32)
    low = total.astype(LOW)
    piece = total[:, 0]
    for r in range(1, slots):
        piece = piece + swap(low[:, r], "tensor", r, slots).astype(F32)
    bit = 8
    while bit < place.dp:
        piece = piece + swap(piece.astype(LOW), "dp", bit, place.dp).astype(F32)
        bit *= 2
    piece = piece.astype(LOW)
    piece = ordered(piece, swap(piece, "dp", second, place.dp), place.bits[second] == 1, 1)
    piece = ordered(piece, swap(piece, "dp", first, place.dp), place.bits[first] == 1, 1)
    piece = ordered(piece, swap(piece, "dp", 1, place.dp), place.core == 1, 2)
    return piece.astype(F32)


def local(
    inputs, memory, cotangent, dec_len, mem_len,
    self_qkv, self_out, cross_q, cross_kv, cross_out, ffn_in, ffn_out, ln_gain, ln_bias,
):
    place = Place()
    dp, slots = place.dp, place.tensor
    both = ("dp", "tensor")
    width = inputs.shape[3]
    length = inputs.shape[2]
    block = length // slots
    micro = place.z // 2
    owner = place.core == (place.z & 1)
    fetch_perm = [
        (d * slots + t, (d ^ 1) * slots + t)
        for d in range(dp)
        for t in range(slots)
        if d % 2 == t % 2
    ]
    spread = []
    for call in range(2):
        spread.append(
            [
                ((g + hh) * slots + s, (g + s % 2) * slots + OWN_BLOCKS[hh][(call + s // 2) % 2])
                for g in range(0, dp, 2)
                for s in range(slots)
                for hh in range(2)
            ]
        )
    collect = [[(dst, src) for src, dst in perm] for perm in spread]

    def fetch(value):
        mine = lax.dynamic_index_in_dim(value, micro, 0, False)[0]
        return jnp.where(owner, mine, lax.ppermute(mine, both, fetch_perm))

    def own_rows(value):
        return jnp.concatenate(
            [
                lax.dynamic_slice_in_dim(value, place.core * block, block, 0),
                lax.dynamic_slice_in_dim(value, (3 - place.core) * block, block, 0),
            ],
            0,
        )

    def send_rows(value):
        got = [
            lax.ppermute(
                lax.dynamic_slice_in_dim(value, ((call + micro) % 2) * block, block, 0), both, spread[call]
            )
            for call in range(2)
        ]
        near = place.z // 2 == 0
        return jnp.stack([jnp.where(near, got[0], got[1]), jnp.where(near, got[1], got[0])])[:, None]

    def collect_rows(value):
        got = [
            lax.ppermute(
                lax.dynamic_index_in_dim(value, (place.z // 2 + call) % 2, 0, False)[0], both, collect[call]
            )
            for call in range(2)
        ]
        return jnp.concatenate(
            [jnp.where(micro == 0, got[0], got[1]), jnp.where(micro == 0, got[1], got[0])], 0
        )

    def flat(weights):
        return weights.reshape(-1, width)

    lens = fetch(jnp.stack([dec_len, mem_len], -1))
    core = place.core.astype(jnp.int32)
    info_self = jnp.stack([core, lens[0]])
    info_cross = jnp.stack([core, lens[1]])

    x_all = fetch(inputs)
    w_qkv = gather_weights(place, jnp.swapaxes(self_qkv, 1, 2), (2, 4))
    w_mid = gather_weights(
        place,
        jnp.concatenate(
            [self_out[None], cross_q.T[None], jnp.swapaxes(cross_kv, 1, 2), cross_out[None]], 0
        ),
        (4, 2),
    )
    mem_all = fetch(memory)
    w_up = flat(gather_weights(place, ffn_in.T[None], (2, 4)))
    w_down = flat(gather_weights(place, ffn_out[None], (4, 2)))
    grad_y = collect_rows(cotangent)

    x_own = own_rows(x_all)
    mem_own = own_rows(mem_all)
    wq, wk, wv = (flat(w_qkv[t]) for t in range(3))
    w_so, w_cq, w_ck, w_cv, w_co = (flat(w_mid[t]) for t in range(5))

    query_s = dot_nt(x_own, wq).astype(LOW)
    key_s = dot_nt(x_all, wk).astype(LOW)
    value_s = dot_nt(x_all, wv).astype(LOW)
    attn_s, logs_s = attend_forward(True, info_self, query_s, key_s, value_s)
    normed_one, rstd_one, h1_low, query_c = first_norm(attn_s, x_own, w_so, w_cq, ln_gain, ln_bias)
    key_c = dot_nt(mem_all, w_ck).astype(LOW)
    value_c = dot_nt(mem_all, w_cv).astype(LOW)
    attn_c, logs_c = attend_forward(False, info_cross, query_c, key_c, value_c)
    (out_rows, act, grad_pre, grad_b3, h2_low, grad_b2, grad_oc, grad_r2, sums_late) = middle(
        normed_one, attn_c, grad_y, w_co, w_up, w_down, ln_gain, ln_bias
    )
    out = send_rows(out_rows)
    d_down = reduce_grads(place, [(act, grad_b3)], (2, 4))
    d_up = reduce_grads(place, [(grad_pre, h2_low)], (4, 2))

    dq_c, dk_c, dv_c, dk_cs, dv_cs = attend_backward(
        False, info_cross, query_c, key_c, value_c, attn_c, logs_c, grad_oc
    )
    dk_c = (dk_c.astype(F32) + swap(dk_cs, "dp", 1, dp).astype(F32)).astype(LOW)
    dv_c = (dv_c.astype(F32) + swap(dv_cs, "dp", 1, dp).astype(F32)).astype(LOW)
    grad_r1, grad_b1, grad_os, sums_first = first_norm_back(
        grad_r2, dq_c, normed_one, rstd_one, w_cq, w_so, ln_gain
    )
    d_mem = send_rows((dot_nn(dk_c, w_ck) + dot_nn(dv_c, w_cv)).astype(LOW)).astype(F32)
    d_mid = reduce_grads(
        place,
        [(attn_s, grad_b1), (dq_c, h1_low), (dk_c, mem_own), (dv_c, mem_own), (attn_c, grad_b2)],
        (2, 4),
    )

    sums = sums_late + sums_first
    bit = 1
    while bit < dp:
        sums = sums + swap(sums, "dp", bit, dp)
        bit *= 2
    bit = 1
    while bit < slots:
        sums = sums + swap(sums, "tensor", bit, slots)
        bit *= 2

    dq_s, dk_s, dv_s, dk_ss, dv_ss = attend_backward(
        True, info_self, query_s, key_s, value_s, attn_s, logs_s, grad_os
    )
    dk_s = (dk_s.astype(F32) + swap(dk_ss, "dp", 1, dp).astype(F32)).astype(LOW)
    dv_s = (dv_s.astype(F32) + swap(dv_ss, "dp", 1, dp).astype(F32)).astype(LOW)
    d_x = send_rows(
        (grad_r1 + dot_nn(dq_s, wq) + dot_nn(dk_s, wk) + dot_nn(dv_s, wv)).astype(LOW)
    ).astype(F32)
    d_qkv = reduce_grads(place, [(dq_s, x_own), (dk_s, x_own), (dv_s, x_own)], (4, 2))

    return (
        out,
        d_x,
        d_mem,
        jnp.swapaxes(d_qkv, 1, 2),
        d_mid[0],
        d_mid[1].T,
        jnp.swapaxes(d_mid[2:4], 1, 2),
        d_mid[4],
        d_up[0].T,
        d_down[0],
        sums[0:3],
        sums[3:6],
    )


def solution(mesh):
    rows = P(None, "dp", "tensor", None)
    in_specs = (
        P(None, "dp", None, None),
        P(None, "dp", None, None),
        rows,
        P(None, "dp"),
        P(None, "dp"),
        P(None, None, "tensor"),
        P("tensor", None),
        P(None, "tensor"),
        P(None, None, "tensor"),
        P("tensor", None),
        P(None, "tensor"),
        P("tensor", None),
        P(),
        P(),
    )
    out_specs = (
        rows,
        rows,
        rows,
        P(None, None, "tensor"),
        P("tensor", None),
        P(None, "tensor"),
        P(None, None, "tensor"),
        P("tensor", None),
        P(None, "tensor"),
        P("tensor", None),
        P(),
        P(),
    )
    return jax.shard_map(local, mesh=mesh, in_specs=in_specs, out_specs=out_specs, check_vma=False)
```

```python
import functools

import jax
import jax.numpy as jnp
from jax import lax
from jax.experimental import pallas as pl
from jax.experimental.pallas import tpu as pltpu
from jax.sharding import PartitionSpec as P

HEAD = 64
EPS = 1e-05
NEG = -1e30
LOW = jnp.bfloat16
F32 = jnp.float32
OWN_BLOCKS = ((0, 3), (1, 2))
MIB = 1024 * 1024


def dot_nn(left, right):
    return lax.dot_general(left, right, (((1,), (0,)), ((), ())), preferred_element_type=F32)


def dot_nt(left, right):
    return lax.dot_general(left, right, (((1,), (1,)), ((), ())), preferred_element_type=F32)


def dot_tn(left, right):
    return lax.dot_general(left, right, (((0,), (0,)), ((), ())), preferred_element_type=F32)


def cost(flops, size, trans=0):
    return pl.CostEstimate(flops=int(flops), bytes_accessed=int(size), transcendentals=int(trans))


def whole(shape):
    return pl.BlockSpec(shape, lambda *_: (0,) * len(shape), pipeline_mode=pl.Buffered(1))


def attend_forward(causal, info, query, keys_in, values_in):
    rows, width = query.shape
    key_rows = keys_in.shape[0]
    block = rows // 2
    pair = 2 * HEAD

    def kernel(info_ref, q_ref, k_ref, v_ref, o_ref, lse_ref):
        length = info_ref[1]

        def part(spot, block_id, extent):
            lane = lax.broadcasted_iota(jnp.int32, (block, pair), 1)
            limit = jnp.full((block, 1), length, jnp.int32)
            if causal:
                row = block_id * block + lax.broadcasted_iota(jnp.int32, (block, 1), 0)
                limit = jnp.minimum(limit, row + 1)
            allowed = lax.broadcasted_iota(jnp.int32, (block, extent), 1) < limit
            span = pl.ds(spot * block, block)
            q = q_ref[span, :]
            out, logs = None, None
            for side in range(2):
                mine = (lane >= HEAD) if side else (lane < HEAD)
                q_side = jnp.where(mine, q, 0).astype(LOW) * LOW(HEAD ** (-0.5))
                scores = jnp.where(allowed, dot_nt(q_side, k_ref[:extent, :]), NEG)
                peak = jnp.max(scores, -1, keepdims=True)
                weights = jnp.exp(scores - peak)
                total = jnp.sum(weights, -1, keepdims=True)
                mixed = dot_nn(weights.astype(LOW), v_ref[:extent, :]) / total
                log_total = peak + jnp.log(total)
                if side:
                    out = jnp.where(mine, mixed, out)
                    logs = jnp.where(mine, log_total, logs)
                else:
                    out, logs = mixed, jnp.broadcast_to(log_total, (block, pair))
            o_ref[span, :] = out.astype(LOW)
            lse_ref[span, :] = logs

        if causal:
            for variant in range(2):

                @pl.when(info_ref[0] == variant)
                def _():
                    for spot in range(2):
                        block_id = OWN_BLOCKS[variant][spot]
                        part(spot, block_id, (block_id + 1) * block)
        else:
            for spot in range(2):
                part(spot, 0, key_rows)

    column = pl.BlockSpec((rows, pair), lambda p, *_: (0, p))
    key_column = pl.BlockSpec((key_rows, pair), lambda p, *_: (0, p))
    share = 0.625 if causal else 1.0
    elements = width // HEAD * rows * key_rows * share
    return pl.pallas_call(
        kernel,
        out_shape=(
            jax.ShapeDtypeStruct((rows, width), LOW),
            jax.ShapeDtypeStruct((rows, width), F32),
        ),
        grid_spec=pltpu.PrefetchScalarGridSpec(
            num_scalar_prefetch=1,
            grid=(width // pair,),
            in_specs=[column, key_column, key_column],
            out_specs=[column, column],
        ),
        compiler_params=pltpu.CompilerParams(vmem_limit_bytes=48 * MIB),
        cost_estimate=cost(elements * 1024, 10 * MIB, elements),
    )(info, query, keys_in, values_in)


def attend_backward(causal, share_of, info, query, keys_in, values_in, out, logs, grad_out):
    rows, width = query.shape[0], query.shape[1] // share_of[1]
    skip = share_of[0] * width // (2 * HEAD)
    key_rows = keys_in.shape[0]
    block = rows // 2
    pair = 2 * HEAD

    def kernel(
        info_ref, q_ref, k_ref, v_ref, o_ref, lse_ref, g_ref,
        dq_ref, own_ref, give_ref, dk_acc, dv_acc,
    ):
        length = info_ref[1]
        dk_acc[...] = jnp.zeros_like(dk_acc)
        dv_acc[...] = jnp.zeros_like(dv_acc)

        def part(spot, block_id, extent):
            lane = lax.broadcasted_iota(jnp.int32, (block, pair), 1)
            limit = jnp.full((block, 1), length, jnp.int32)
            if causal:
                row = block_id * block + lax.broadcasted_iota(jnp.int32, (block, 1), 0)
                limit = jnp.minimum(limit, row + 1)
            allowed = lax.broadcasted_iota(jnp.int32, (block, extent), 1) < limit
            span = pl.ds(spot * block, block)
            q = q_ref[span, :]
            g = g_ref[span, :]
            along = g.astype(F32) * o_ref[span, :].astype(F32)
            dq = None
            for side in range(2):
                mine = (lane >= HEAD) if side else (lane < HEAD)
                q_side = jnp.where(mine, q, 0).astype(LOW) * LOW(HEAD ** (-0.5))
                g_side = jnp.where(mine, g, 0).astype(LOW)
                inner = jnp.sum(jnp.where(mine, along, 0.0), -1, keepdims=True)
                log_total = lse_ref[span, side * HEAD : side * HEAD + 1]
                scores = jnp.where(allowed, dot_nt(q_side, k_ref[:extent, :]), NEG)
                weights = jnp.exp(scores - log_total)
                dv_acc[:extent, :] += dot_tn(weights.astype(LOW), g_side)
                grad_w = dot_nt(g_side, v_ref[:extent, :])
                grad_s = (weights * (grad_w - inner)).astype(LOW)
                dk_acc[:extent, :] += dot_tn(grad_s, q_side)
                part_q = dot_nn(grad_s, k_ref[:extent, :])
                dq = jnp.where(mine, part_q, dq) if side else part_q
            dq_ref[span, :] = (dq * HEAD ** (-0.5)).astype(LOW)

        for variant in range(2):

            @pl.when(info_ref[0] == variant)
            def _():
                for spot in range(2):
                    block_id = OWN_BLOCKS[variant][spot]
                    part(spot, block_id, (block_id + 1) * block if causal else key_rows)
                for spot in range(2):
                    keep = slice(OWN_BLOCKS[variant][spot] * block, (OWN_BLOCKS[variant][spot] + 1) * block)
                    give = slice(OWN_BLOCKS[1 - variant][spot] * block, (OWN_BLOCKS[1 - variant][spot] + 1) * block)
                    span = slice(spot * block, (spot + 1) * block)
                    own_ref[0, span, :] = dk_acc[keep, :].astype(LOW)
                    own_ref[1, span, :] = dv_acc[keep, :].astype(LOW)
                    give_ref[0, span, :] = dk_acc[give, :].astype(LOW)
                    give_ref[1, span, :] = dv_acc[give, :].astype(LOW)

    column = pl.BlockSpec((rows, pair), lambda p, *_: (0, p + skip))
    key_column = pl.BlockSpec((key_rows, pair), lambda p, *_: (0, p + skip))
    single = pl.BlockSpec((rows, pair), lambda p, *_: (0, p))
    double = pl.BlockSpec((2, rows, pair), lambda p, *_: (0, 0, p))
    share = 0.625 if causal else 1.0
    elements = width // HEAD * rows * key_rows * share
    return pl.pallas_call(
        kernel,
        out_shape=(jax.ShapeDtypeStruct((rows, width), LOW),)
        + (jax.ShapeDtypeStruct((2, rows, width), LOW),) * 2,
        grid_spec=pltpu.PrefetchScalarGridSpec(
            num_scalar_prefetch=1,
            grid=(width // pair,),
            in_specs=[column, key_column, key_column, column, column, column],
            out_specs=[single, double, double],
            scratch_shapes=[pltpu.VMEM((key_rows, pair), F32), pltpu.VMEM((key_rows, pair), F32)],
        ),
        compiler_params=pltpu.CompilerParams(vmem_limit_bytes=48 * MIB),
        cost_estimate=cost(elements * 2560, 10 * MIB, elements),
    )(info, query, keys_in, values_in, out, logs, grad_out)


def normalize(resid):
    center = resid - jnp.mean(resid, -1, keepdims=True)
    rstd = lax.rsqrt(jnp.mean(center * center, -1, keepdims=True) + EPS)
    return center * rstd, rstd


def norm_back(grad, gain, normed, rstd):
    dn = grad * gain
    mean_dn = jnp.mean(dn, -1, keepdims=True)
    mean_dnn = jnp.mean(dn * normed, -1, keepdims=True)
    return rstd * (dn - mean_dn - normed * mean_dnn)


def row_sum(value):
    return jnp.sum(value, 0, keepdims=True)


def first_norm(attn, x_rows, w_out, w_query, gain, shift):
    rows, width = attn.shape
    block = min(256, rows)

    def kernel(o_ref, x_ref, wo_ref, wq_ref, g_ref, s_ref, n_ref, r_ref, h_ref, q_ref):
        normed, rstd = normalize(x_ref[...].astype(F32) + dot_nn(o_ref[...], wo_ref[...]))
        n_ref[...] = normed
        r_ref[...] = jnp.broadcast_to(rstd, r_ref.shape)
        low = (normed * g_ref[0:1, :] + s_ref[0:1, :]).astype(LOW)
        h_ref[...] = low
        q_ref[...] = dot_nt(low, wq_ref[...]).astype(LOW)

    row = pl.BlockSpec((block, width), lambda b: (b, 0))
    thin = pl.BlockSpec((block, 128), lambda b: (b, 0))
    return pl.pallas_call(
        kernel,
        grid=(rows // block,),
        out_shape=(
            jax.ShapeDtypeStruct((rows, width), F32),
            jax.ShapeDtypeStruct((rows, 128), F32),
            jax.ShapeDtypeStruct((rows, width), LOW),
            jax.ShapeDtypeStruct((rows, width), LOW),
        ),
        in_specs=[row, row, whole(w_out.shape), whole(w_query.shape), whole(gain.shape), whole(shift.shape)],
        out_specs=[row, thin, row, row],
        compiler_params=pltpu.CompilerParams(vmem_limit_bytes=40 * MIB),
        cost_estimate=cost(4 * rows * width * width, 8 * MIB),
    )(attn, x_rows, w_out, w_query, gain, shift)


def gelu_parts(u):
    t = 1.0 / (1.0 + (0.3275911 * 0.7071067811865476) * jnp.abs(u))
    bell = jnp.exp(-0.5 * u * u)
    poly = t * (0.254829592 + t * (-0.284496736 + t * (1.421413741 + t * (-1.453152027 + t * 1.061405429))))
    tail = 0.5 * poly * bell
    return jnp.where(u < 0, tail, 1.0 - tail), bell * 0.3989422804014327


def middle(normed_one, attn, grad_y, w_out, w_ffn, gain, shift):
    rows, width = attn.shape
    parts, _, part, _ = w_ffn.shape
    hidden = parts * part
    block = min(128, rows)
    step = min(768, hidden)

    def kernel(
        n0_ref, o_ref, y_ref, wo_ref, w_ref, g_ref, s_ref,
        out_ref, a_ref, du_ref, db3_ref, h2_ref, db2_ref, do_ref, dr2_ref, sums_ref, slope_ref,
    ):
        @pl.when(pl.program_id(0) == 0)
        def _():
            sums_ref[...] = jnp.zeros_like(sums_ref)

        def weight(which, start):
            return w_ref[start // part : (start + step) // part, which].reshape(step, width)

        h1 = n0_ref[...] * g_ref[0:1, :] + s_ref[0:1, :]
        n1, rstd1 = normalize(h1 + dot_nn(o_ref[...], wo_ref[...]))
        h2 = n1 * g_ref[1:2, :] + s_ref[1:2, :]
        h2_low = h2.astype(LOW)
        h2_ref[...] = h2_low
        branch = None
        for start in range(0, hidden, step):
            span = slice(start, start + step)
            u = dot_nt(h2_low, weight(0, start))
            share, density = gelu_parts(u)
            slope_ref[:, span] = share + u * density
            a = (u * share).astype(LOW)
            a_ref[:, span] = a
            term = dot_nn(a, weight(1, start))
            branch = term if branch is None else branch + term
        n2, rstd2 = normalize(h2 + branch)
        out_ref[...] = (n2 * g_ref[2:3, :] + s_ref[2:3, :]).astype(LOW)
        g = y_ref[...].astype(F32)
        sums_ref[2:3, :] += row_sum(g * n2)
        sums_ref[5:6, :] += row_sum(g)
        dr3 = norm_back(g, g_ref[2:3, :], n2, rstd2)
        db3 = dr3.astype(LOW)
        db3_ref[...] = db3
        dh2 = dr3
        for start in range(0, hidden, step):
            span = slice(start, start + step)
            du = (dot_nt(db3, weight(1, start)) * slope_ref[:, span]).astype(LOW)
            du_ref[:, span] = du
            dh2 = dh2 + dot_nn(du, weight(0, start))
        sums_ref[1:2, :] += row_sum(dh2 * n1)
        sums_ref[4:5, :] += row_sum(dh2)
        dr2 = norm_back(dh2, g_ref[1:2, :], n1, rstd1)
        dr2_ref[...] = dr2
        db2 = dr2.astype(LOW)
        db2_ref[...] = db2
        do_ref[...] = dot_nt(db2, wo_ref[...]).astype(LOW)

    row = pl.BlockSpec((block, width), lambda b: (b, 0))
    broad = pl.BlockSpec((block, hidden), lambda b: (b, 0))
    low_row = jax.ShapeDtypeStruct((rows, width), LOW)
    low_broad = jax.ShapeDtypeStruct((rows, hidden), LOW)
    return pl.pallas_call(
        kernel,
        grid=(rows // block,),
        out_shape=(
            low_row, low_broad, low_broad, low_row, low_row, low_row, low_row,
            jax.ShapeDtypeStruct((rows, width), F32),
            jax.ShapeDtypeStruct((8, width), F32),
        ),
        in_specs=[
            row, row, row, whole(w_out.shape), whole(w_ffn.shape), whole(gain.shape),
            whole(shift.shape),
        ],
        out_specs=[
            row, broad, broad, row, row, row, row, row,
            pl.BlockSpec((8, width), lambda b: (0, 0)),
        ],
        scratch_shapes=[pltpu.VMEM((block, hidden), F32)],
        compiler_params=pltpu.CompilerParams(vmem_limit_bytes=50 * MIB),
        cost_estimate=cost(rows * width * (8 * hidden + 4 * width), 24 * MIB, rows * hidden),
    )(normed_one, attn, grad_y, w_out, w_ffn, gain, shift)


def first_norm_back(grad_resid, grad_query, normed_one, rstd_one, w_query, w_out, gain):
    rows, width = grad_resid.shape
    block = min(256, rows)

    def kernel(dr2_ref, dq_ref, n_ref, r_ref, wq_ref, wo_ref, g_ref, dr1_ref, db1_ref, do_ref, sums_ref):
        @pl.when(pl.program_id(0) == 0)
        def _():
            sums_ref[...] = jnp.zeros_like(sums_ref)

        normed = n_ref[...]
        dh1 = dr2_ref[...] + dot_nn(dq_ref[...], wq_ref[...])
        sums_ref[0:1, :] += row_sum(dh1 * normed)
        sums_ref[3:4, :] += row_sum(dh1)
        dr1 = norm_back(dh1, g_ref[0:1, :], normed, r_ref[:, 0:1])
        dr1_ref[...] = dr1
        db1 = dr1.astype(LOW)
        db1_ref[...] = db1
        do_ref[...] = dot_nt(db1, wo_ref[...]).astype(LOW)

    row = pl.BlockSpec((block, width), lambda b: (b, 0))
    thin = pl.BlockSpec((block, 128), lambda b: (b, 0))
    low_row = jax.ShapeDtypeStruct((rows, width), LOW)
    return pl.pallas_call(
        kernel,
        grid=(rows // block,),
        out_shape=(
            jax.ShapeDtypeStruct((rows, width), F32), low_row, low_row,
            jax.ShapeDtypeStruct((8, width), F32),
        ),
        in_specs=[row, row, row, thin, whole(w_query.shape), whole(w_out.shape), whole(gain.shape)],
        out_specs=[row, row, row, pl.BlockSpec((8, width), lambda b: (0, 0))],
        compiler_params=pltpu.CompilerParams(vmem_limit_bytes=40 * MIB),
        cost_estimate=cost(4 * rows * width * width, 8 * MIB),
    )(grad_resid, grad_query, normed_one, rstd_one, w_query, w_out, gain)


def swap(value, axis, bit, size):
    return lax.ppermute(value, axis, [(d, d ^ bit) for d in range(size)])


def ordered(own, other, bit, axis):
    low = jnp.where(bit, other, own)
    high = jnp.where(bit, own, other)
    return jnp.concatenate([low, high], axis)


class Place:
    def __init__(self):
        self.dp = lax.axis_size("dp")
        self.tensor = lax.axis_size("tensor")
        index = lax.axis_index("dp")
        self.z = lax.axis_index("tensor")
        self.core = index & 1
        self.chip = (index >> 1) & 3


def after(value, *deps):
    return lax.optimization_barrier((value, deps))[0]


def beside(always, work, *operands):
    def nothing(*operands):
        return jax.tree.map(lambda leaf: jnp.zeros(leaf.shape, leaf.dtype), jax.eval_shape(work, *operands))

    return lax.optimization_barrier(
        lax.cond(always, work, nothing, *lax.optimization_barrier(operands))
    )


def piece_of(place, shard):
    count, rows, width = shard.shape
    return lax.dynamic_slice(
        shard,
        (0, place.chip * (rows // 4), place.core * (width // 2)),
        (count, rows // 4, width // 2),
    )


def from_tensor(place, piece, far, *deps):
    near = swap(after(jnp.stack([piece, far]), *deps), "tensor", 1, place.tensor)
    return jnp.stack([near[0], far, near[1]])


def from_chips(place, got, *deps):
    others = [swap(got, "dp", 2 * r, place.dp) for r in range(1, 4)]
    if deps:
        others = after(others, *deps)
    return [got, *others]


def assemble(place, shard, mine, theirs):
    count, rows, width = shard.shape
    quarter, half, slots = rows // 4, width // 2, mine.shape[1] + 1

    def kernel(info_ref, shard_ref, mine_ref, theirs_ref, *out_refs):
        def fill(left, right):
            for t, out_ref in enumerate(out_refs):
                out_ref[0] = shard_ref[t]
                for r in range(1, slots):
                    out_ref[r, :, :half] = left[0, r - 1, t]
                    out_ref[r, :, half:] = right[0, r - 1, t]

        @pl.when(info_ref[0] == 0)
        def _():
            fill(mine_ref, theirs_ref)

        @pl.when(info_ref[0] == 1)
        def _():
            fill(theirs_ref, mine_ref)

    def spot(p, info):
        return (p ^ info[1], 0, 0, 0, 0)

    part = pl.BlockSpec((1, slots - 1, count, quarter, half), spot)
    outs = pl.pallas_call(
        kernel,
        out_shape=(jax.ShapeDtypeStruct((slots, rows, width), LOW),) * count,
        grid_spec=pltpu.PrefetchScalarGridSpec(
            num_scalar_prefetch=1,
            grid=(4,),
            in_specs=[pl.BlockSpec((count, quarter, width), lambda p, info: (0, p, 0)), part, part],
            out_specs=[pl.BlockSpec((slots, quarter, width), lambda p, info: (0, p, 0))] * count,
        ),
        compiler_params=pltpu.CompilerParams(vmem_limit_bytes=32 * MIB),
        cost_estimate=cost(0, 4 * count * slots * rows * width),
    )(jnp.stack([place.core, place.chip]).astype(jnp.int32), shard, mine, theirs)
    return [out.reshape(slots * rows, width) for out in outs]


def weight_grads(place, pairs):
    count = len(pairs)
    n, columns = pairs[0][0].shape
    width = pairs[0][1].shape[1]
    half = width // 2
    block = min(768, columns)
    steps = columns // block
    chunk = min(256, block)

    def kernel(info_ref, *refs):
        sides, (keep_ref, give_ref) = refs[: 2 * count], refs[2 * count :]
        keep = pl.multiple_of(info_ref[0] * half, 128)
        give = pl.multiple_of((1 - info_ref[0]) * half, 128)
        for t in range(count):

            @pl.when(pl.program_id(0) // steps == t)
            def _():
                g_ref, a_ref = sides[2 * t], sides[2 * t + 1]
                for start in range(0, block, chunk):
                    at = slice(start, start + chunk)
                    left = g_ref[:, at]
                    keep_ref[0, at, :] = dot_tn(left, a_ref[:, pl.ds(keep, half)]).astype(LOW)
                    give_ref[0, at, :] = dot_tn(left, a_ref[:, pl.ds(give, half)]).astype(LOW)

    def rows_spec(t):
        return pl.BlockSpec(
            (n, block), lambda g, info: (0, jnp.clip(g - t * steps, 0, steps - 1))
        )

    out = pl.BlockSpec((1, block, half), lambda g, info: (g // steps, g % steps, 0))
    in_specs, operands = [], []
    for t, (g, a) in enumerate(pairs):
        in_specs += [rows_spec(t), pl.BlockSpec((n, width), lambda g, info: (0, 0))]
        operands += [g, a]
    return pl.pallas_call(
        kernel,
        out_shape=(jax.ShapeDtypeStruct((count, columns, half), LOW),) * 2,
        grid_spec=pltpu.PrefetchScalarGridSpec(
            num_scalar_prefetch=1,
            grid=(count * steps,),
            in_specs=in_specs,
            out_specs=[out, out],
        ),
        compiler_params=pltpu.CompilerParams(vmem_limit_bytes=48 * MIB),
        cost_estimate=cost(2 * count * n * columns * width, 4 * count * columns * width),
    )(jnp.stack([place.core]).astype(jnp.int32), *operands)


def chip_parts(place, keep, other):
    count, rows, half = keep.shape
    slots = place.tensor
    quarter = rows // slots // 4

    def kernel(info_ref, keep_ref, other_ref, *part_refs):
        for r, part_ref in enumerate(part_refs):
            for z in range(slots):
                at = pl.multiple_of(4 * z * quarter + (info_ref[0] ^ r) * quarter, 16)
                span = pl.ds(at, quarter)
                total = keep_ref[0, span, :].astype(F32) + other_ref[0, span, :].astype(F32)
                part_ref[0, z] = total.astype(LOW)

    row = pl.BlockSpec((1, rows, half), lambda t, info: (t, 0, 0))
    part = pl.BlockSpec((1, slots, quarter, half), lambda t, info: (t, 0, 0, 0))
    return pl.pallas_call(
        kernel,
        out_shape=(jax.ShapeDtypeStruct((count, slots, quarter, half), LOW),) * 4,
        grid_spec=pltpu.PrefetchScalarGridSpec(
            num_scalar_prefetch=1, grid=(count,), in_specs=[row, row], out_specs=[part] * 4
        ),
        compiler_params=pltpu.CompilerParams(vmem_limit_bytes=32 * MIB),
        cost_estimate=cost(0, 6 * count * rows * half),
    )(jnp.stack([place.chip]).astype(jnp.int32), keep, other)


def swap_chips(place, parts):
    return [swap(parts[r], "dp", 2 * r, place.dp) for r in range(1, 4)]


def add_all(own, others):
    own = own.astype(F32)
    for other in others:
        own = own + other.astype(F32)
    return own


def near_parts(place, total, natural):
    def slot(r):
        if natural:
            return lax.dynamic_index_in_dim(total, place.z ^ r, 1, False)
        return total[:, r]

    stay, leave = jnp.stack([slot(0), slot(2)]), jnp.stack([slot(1), slot(3)])
    return stay, leave.astype(LOW)


def add_far(place, total, other):
    piece = total[0] + other.astype(F32)
    bit = 8
    while bit < place.dp:
        piece = piece + swap(piece.astype(LOW), "dp", bit, place.dp).astype(F32)
        bit *= 2
    return piece.astype(LOW)


def regather(place, piece):
    own = jnp.stack(from_chips(place, piece))
    return own, swap(own, "dp", 1, place.dp)


def finish(place, own, other, groups):
    _, count, quarter, half = own.shape
    rows, width = 4 * quarter, 2 * half

    def kernel(info_ref, own_ref, other_ref, *out_refs):
        core, chip = info_ref[0], info_ref[1]
        t = 0
        for group, out_ref in zip(groups, out_refs, strict=True):
            for g in range(group):
                for p in range(4):
                    at = slice(p * quarter, (p + 1) * quarter)
                    mine, theirs = own_ref[p ^ chip, t].astype(F32), other_ref[p ^ chip, t].astype(F32)
                    out_ref[g, at, :half] = jnp.where(core == 0, mine, theirs)
                    out_ref[g, at, half:] = jnp.where(core == 0, theirs, mine)
                t += 1

    shapes = [(group, rows, width) for group in groups]
    return pl.pallas_call(
        kernel,
        out_shape=[jax.ShapeDtypeStruct(shape, F32) for shape in shapes],
        grid_spec=pltpu.PrefetchScalarGridSpec(
            num_scalar_prefetch=1,
            grid=(1,),
            in_specs=[whole(own.shape), whole(own.shape)],
            out_specs=[whole(shape) for shape in shapes],
        ),
        compiler_params=pltpu.CompilerParams(vmem_limit_bytes=48 * MIB),
        cost_estimate=cost(0, 6 * count * rows * width),
    )(jnp.stack([place.core, place.chip]).astype(jnp.int32), own, other)


def finish_ffn(parts):
    _, _, quarter, half = parts.shape
    rows, width = 4 * quarter, 2 * half

    def kernel(parts_ref, down_ref, up_ref):
        for side in range(2):
            columns = slice(side * half, (side + 1) * half)
            for q in range(4):
                at = slice(q * quarter, (q + 1) * quarter)
                down_ref[at, columns] = parts_ref[2 * q + side, 0].astype(F32)
            full = jnp.concatenate([parts_ref[2 * q + side, 1] for q in range(4)], 0)
            up_ref[columns, :] = full.astype(F32).T

    return pl.pallas_call(
        kernel,
        out_shape=(jax.ShapeDtypeStruct((rows, width), F32), jax.ShapeDtypeStruct((width, rows), F32)),
        compiler_params=pltpu.CompilerParams(vmem_limit_bytes=32 * MIB),
        cost_estimate=cost(0, 12 * rows * width),
    )(parts)


def local(
    inputs, memory, cotangent, dec_len, mem_len,
    self_qkv, self_out, cross_q, cross_kv, cross_out, ffn_in, ffn_out, ln_gain, ln_bias,
):
    place = Place()
    dp, slots = place.dp, place.tensor
    axes = ("dp", "tensor")
    width = inputs.shape[3]
    length = inputs.shape[2]
    block = length // slots
    micro = place.z // 2
    owner = place.core == (place.z & 1)
    fetch_perm = [
        (d * slots + t, (d ^ 1) * slots + t)
        for d in range(dp)
        for t in range(slots)
        if d % 2 == t % 2
    ]
    spread = []
    for call in range(2):
        spread.append(
            [
                ((g + hh) * slots + s, (g + s % 2) * slots + OWN_BLOCKS[hh][(call + s // 2) % 2])
                for g in range(0, dp, 2)
                for s in range(slots)
                for hh in range(2)
            ]
        )
    collect = [[(dst, src) for src, dst in perm] for perm in spread]

    def fetch(value):
        mine = lax.dynamic_index_in_dim(value, micro, 0, False)[0]
        return jnp.where(owner, mine, lax.ppermute(mine, axes, fetch_perm))

    def own_rows(value):
        return jnp.concatenate(
            [
                lax.dynamic_slice_in_dim(value, place.core * block, block, 0),
                lax.dynamic_slice_in_dim(value, (3 - place.core) * block, block, 0),
            ],
            0,
        )

    def start_rows(value):
        return [
            lax.ppermute(
                lax.dynamic_slice_in_dim(value, ((call + micro) % 2) * block, block, 0), axes, spread[call]
            )
            for call in range(2)
        ]

    def end_rows(got):
        near = place.z // 2 == 0
        return jnp.stack([jnp.where(near, got[0], got[1]), jnp.where(near, got[1], got[0])])[:, None]

    def collect_rows(value):
        return [
            lax.ppermute(
                lax.dynamic_index_in_dim(value, (place.z // 2 + call) % 2, 0, False)[0], axes, collect[call]
            )
            for call in range(2)
        ]


    def flat(weights):
        return weights.reshape(-1, width)

    index = lax.axis_index("dp")
    at_ffn = ffn_out.shape[0] // dp
    piece_ffn = jnp.stack(
        [
            lax.dynamic_slice_in_dim(ffn_in, index * at_ffn, at_ffn, 1).T,
            lax.dynamic_slice_in_dim(ffn_out, index * at_ffn, at_ffn, 0),
        ]
    )
    shard_qkv = jnp.swapaxes(self_qkv, 1, 2)
    shard_mid = jnp.concatenate(
        [self_out[None], cross_q.T[None], jnp.swapaxes(cross_kv, 1, 2), cross_out[None]], 0
    )
    pieces = jnp.concatenate([piece_of(place, shard_qkv), piece_of(place, shard_mid)], 0)
    pieces = after(pieces, piece_ffn)
    far = swap(pieces, "tensor", 2, slots)
    lens = fetch(jnp.stack([dec_len, mem_len], -1))
    core = place.core.astype(jnp.int32)
    always = lens[0] > 0
    info_self = jnp.stack([core, lens[0]])
    info_cross = jnp.stack([core, lens[1]])
    x_all = fetch(inputs)
    mem_all = fetch(memory)
    got = after(from_tensor(place, pieces, far), x_all, mem_all, lens)
    w_ffn = lax.all_gather(after(piece_ffn, got), ("tensor", "dp"), axis=0)
    got_qkv = jnp.stack(from_chips(place, got[:, :3]))
    wq, wk, wv = assemble(place, shard_qkv, got_qkv, swap(got_qkv, "dp", 1, dp))

    x_own = own_rows(x_all)

    def self_forward(got, rows, x_own, x_all, wq, wk, wv, info):
        query = dot_nt(x_own, wq).astype(LOW)
        key = dot_nt(x_all, wk).astype(LOW)
        value = dot_nt(x_all, wv).astype(LOW)
        return (
            swap_chips(place, [got] * 4),
            collect_rows(rows),
            (query, key, value),
            attend_forward(True, info, query, key, value),
        )

    others, got_y, (query_s, key_s, value_s), (attn_s, logs_s) = beside(
        always, self_forward, got[:, 3:], cotangent, x_own, x_all, wq, wk, wv, info_self
    )
    got_mid = jnp.stack([got[:, 3:], *others])
    w_so, w_cq, w_ck, w_cv, w_co = assemble(
        place, shard_mid, got_mid, swap(got_mid, "dp", 1, dp)
    )
    grad_y = jnp.concatenate(
        [jnp.where(micro == 0, got_y[0], got_y[1]), jnp.where(micro == 0, got_y[1], got_y[0])], 0
    )
    mem_own = own_rows(mem_all)
    normed_one, rstd_one, h1_low, query_c = first_norm(
        attn_s, x_own, w_so, w_cq, ln_gain, ln_bias
    )
    key_c = dot_nt(mem_all, w_ck).astype(LOW)
    value_c = dot_nt(mem_all, w_cv).astype(LOW)
    attn_c, logs_c = attend_forward(False, info_cross, query_c, key_c, value_c)
    (out_rows, act, grad_pre, grad_b3, h2_low, grad_b2, grad_oc, grad_r2, sums_late) = middle(
        normed_one, attn_c, grad_y, w_co, w_ffn, ln_gain, ln_bias
    )

    keep_down, give_down = weight_grads(place, [(act, grad_b3)])

    def up_grads(give, *pair):
        return swap(give, "dp", 1, dp), weight_grads(place, [pair])

    other_down, (keep_up, give_up) = beside(always, up_grads, give_down, grad_pre, h2_low)
    other_up = swap(give_up, "dp", 1, dp)
    parts_down = chip_parts(place, keep_down, other_down)
    parts_up = chip_parts(place, keep_up, other_up)
    parts_ffn = [jnp.concatenate(pair, 0) for pair in zip(parts_down, parts_up, strict=True)]

    def cross_back(part_x, part_y, rows, *operands):
        return (
            swap(part_x, "dp", 2, dp),
            swap(part_y, "dp", 4, dp),
            start_rows(rows),
            attend_backward(False, (0, 1), *operands),
        )

    ffn_x, ffn_y, got_out, (dq_c, own_c, give_c) = beside(
        always, cross_back, parts_ffn[1], parts_ffn[2], out_rows,
        info_cross, query_c, key_c, value_c, attn_c, logs_c, grad_oc,
    )
    out = end_rows(got_out)
    own_c = (own_c.astype(F32) + swap(give_c, "dp", 1, dp).astype(F32)).astype(LOW)
    dk_c, dv_c = own_c[0], own_c[1]
    grad_r1, grad_b1, grad_os, sums_first = first_norm_back(
        grad_r2, dq_c, normed_one, rstd_one, w_cq, w_so, ln_gain
    )
    d_mem = (dot_nn(dk_c, w_ck) + dot_nn(dv_c, w_cv)).astype(LOW)

    def mid_grads(part, rows, *sides):
        return (
            swap(part, "dp", 6, dp),
            start_rows(rows),
            weight_grads(place, [(sides[2 * t], sides[2 * t + 1]) for t in range(5)]),
        )

    ffn_xy, got_mem, (keep_mid, give_mid) = beside(
        always, mid_grads, parts_ffn[3], d_mem,
        attn_s, grad_b1, dq_c, h1_low, dk_c, mem_own, dv_c, mem_own, attn_c, grad_b2,
    )
    total_ffn = add_all(parts_ffn[0], [ffn_x, ffn_y, ffn_xy])
    near_ffn = near_parts(place, total_ffn, True)
    parts_mid = chip_parts(place, keep_mid, swap(give_mid, "dp", 1, dp))
    sums = sums_late + sums_first
    back_operands = (info_self, query_s, key_s, value_s, attn_s, logs_s, grad_os)

    def self_back_first(part_x, part_y, sums, leave, *operands):
        return (
            swap(part_x, "dp", 2, dp),
            swap(part_y, "dp", 4, dp),
            swap(sums, "dp", 2, dp),
            swap(leave, "tensor", 1, slots),
            attend_backward(True, (0, 2), *operands),
        )

    def self_back_second(part_xy, sums, leave, give, *operands):
        return (
            swap(part_xy, "dp", 6, dp),
            swap(sums, "dp", 4, dp),
            swap(leave, "tensor", 2, slots),
            swap(give, "dp", 1, dp),
            attend_backward(True, (1, 2), *operands),
        )

    from_x, from_y, other_sums, other_ffn, (dq_a, own_a, give_a) = beside(
        always, self_back_first, parts_mid[1], parts_mid[2], sums, near_ffn[1], *back_operands
    )
    sums = sums + other_sums
    far_ffn = near_ffn[0] + other_ffn.astype(F32)
    from_xy, other_sums, other_ffn, other_a, (dq_b, own_b, give_b) = beside(
        always, self_back_second, parts_mid[3], sums, far_ffn[1].astype(LOW), give_a, *back_operands
    )
    sums = sums + other_sums
    piece_ffn = add_far(place, far_ffn, other_ffn)
    other_b = swap(give_b, "dp", 1, dp)
    dkv_s = jnp.concatenate(
        [
            (own.astype(F32) + other.astype(F32)).astype(LOW)
            for own, other in ((own_a, other_a), (own_b, other_b))
        ],
        2,
    )
    dq_s = jnp.concatenate([dq_a, dq_b], 1)
    dk_s, dv_s = dkv_s[0], dkv_s[1]
    keep_qkv, give_qkv = weight_grads(place, [(dq_s, x_own), (dk_s, x_own), (dv_s, x_own)])
    d_x = (grad_r1 + dot_nn(dq_s, wq) + dot_nn(dk_s, wk) + dot_nn(dv_s, wv)).astype(LOW)
    parts_qkv = chip_parts(place, keep_qkv, after(swap(give_qkv, "dp", 1, dp), d_x))

    def send_qkv(parts, rows, sums):
        return swap_chips(place, [None, *parts]), start_rows(rows), swap(sums, "dp", 1, dp)

    others_qkv, got_x, other_sums = beside(always, send_qkv, parts_qkv[1:], d_x, sums)
    sums = sums + other_sums
    others_mid = after([from_x, from_y, from_xy], others_qkv)
    total_mid = add_all(parts_mid[0], others_mid)
    total_qkv = add_all(parts_qkv[0], others_qkv)
    total = jnp.concatenate([total_qkv, total_mid], 0)
    near = near_parts(place, total, False)
    d_x = end_rows(got_x).astype(F32)
    d_mem = end_rows(got_mem).astype(F32)
    bit = 8
    while bit < dp:
        sums = sums + swap(sums, "dp", bit, dp)
        bit *= 2
    other, other_sums = after(
        (swap(near[1], "tensor", 1, slots), swap(sums, "tensor", 1, slots)), d_x, d_mem
    )
    sums = sums + other_sums
    far = near[0] + other.astype(F32)
    other, other_sums = after(
        (swap(far[1].astype(LOW), "tensor", 2, slots), swap(sums, "tensor", 2, slots)), out
    )
    sums = sums + other_sums
    piece = add_far(place, far, other)
    groups = [[first + d for d in range(8)] for first in range(0, dp, 8)]
    d_down, d_up = finish_ffn(lax.all_gather(piece_ffn, "dp", axis=0, axis_index_groups=groups))
    own, other = regather(place, after(piece, d_down, d_up))
    d_qkv, d_so, d_cq, d_ckv, d_co = finish(place, own, other, (3, 1, 1, 2, 1))
    return (
        out,
        d_x,
        d_mem,
        jnp.swapaxes(d_qkv, 1, 2),
        d_so[0],
        d_cq[0].T,
        jnp.swapaxes(d_ckv, 1, 2),
        d_co[0],
        d_up,
        d_down,
        sums[0:3],
        sums[3:6],
    )


def solution(mesh):
    rows = P(None, "dp", "tensor", None)
    in_specs = (
        P(None, "dp", None, None),
        P(None, "dp", None, None),
        rows,
        P(None, "dp"),
        P(None, "dp"),
        P(None, None, "tensor"),
        P("tensor", None),
        P(None, "tensor"),
        P(None, None, "tensor"),
        P("tensor", None),
        P(None, "tensor"),
        P("tensor", None),
        P(),
        P(),
    )
    out_specs = (
        rows,
        rows,
        rows,
        P(None, None, "tensor"),
        P("tensor", None),
        P(None, "tensor"),
        P(None, None, "tensor"),
        P("tensor", None),
        P(None, "tensor"),
        P("tensor", None),
        P(),
        P(),
    )
    return jax.shard_map(local, mesh=mesh, in_specs=in_specs, out_specs=out_specs, check_vma=False)
```

```python
import functools

import jax
import jax.numpy as jnp
from jax import lax
from jax.experimental import pallas as pl
from jax.experimental.pallas import tpu as pltpu
from jax.sharding import PartitionSpec as P

HEAD = 64
EPS = 1e-05
NEG = -1e30
LOW = jnp.bfloat16
F32 = jnp.float32
OWN_BLOCKS = ((0, 3), (1, 2))
MIB = 1024 * 1024


def dot_nn(left, right):
    return lax.dot_general(left, right, (((1,), (0,)), ((), ())), preferred_element_type=F32)


def dot_nt(left, right):
    return lax.dot_general(left, right, (((1,), (1,)), ((), ())), preferred_element_type=F32)


def dot_tn(left, right):
    return lax.dot_general(left, right, (((0,), (0,)), ((), ())), preferred_element_type=F32)


def cost(flops, size, trans=0):
    return pl.CostEstimate(flops=int(flops), bytes_accessed=int(size), transcendentals=int(trans))


def whole(shape):
    return pl.BlockSpec(shape, lambda *_: (0,) * len(shape), pipeline_mode=pl.Buffered(1))


def attend_forward(causal, info, query, keys_in, values_in):
    rows, width = query.shape
    key_rows = keys_in.shape[0]
    block = rows // 2
    pair = 2 * HEAD

    def kernel(info_ref, q_ref, k_ref, v_ref, o_ref, lse_ref):
        length = info_ref[1]

        def part(spot, block_id, extent):
            lane = lax.broadcasted_iota(jnp.int32, (block, pair), 1)
            limit = jnp.full((block, 1), length, jnp.int32)
            if causal:
                row = block_id * block + lax.broadcasted_iota(jnp.int32, (block, 1), 0)
                limit = jnp.minimum(limit, row + 1)
            allowed = lax.broadcasted_iota(jnp.int32, (block, extent), 1) < limit
            span = pl.ds(spot * block, block)
            q = q_ref[span, :]
            out, logs = None, None
            for side in range(2):
                mine = (lane >= HEAD) if side else (lane < HEAD)
                q_side = jnp.where(mine, q, 0).astype(LOW) * LOW(HEAD ** (-0.5))
                scores = jnp.where(allowed, dot_nt(q_side, k_ref[:extent, :]), NEG)
                peak = jnp.max(scores, -1, keepdims=True)
                weights = jnp.exp(scores - peak)
                total = jnp.sum(weights, -1, keepdims=True)
                mixed = dot_nn(weights.astype(LOW), v_ref[:extent, :]) / total
                log_total = peak + jnp.log(total)
                if side:
                    out = jnp.where(mine, mixed, out)
                    logs = jnp.where(mine, log_total, logs)
                else:
                    out, logs = mixed, jnp.broadcast_to(log_total, (block, pair))
            o_ref[span, :] = out.astype(LOW)
            lse_ref[span, :] = logs

        if causal:
            for variant in range(2):

                @pl.when(info_ref[0] == variant)
                def _():
                    for spot in range(2):
                        block_id = OWN_BLOCKS[variant][spot]
                        part(spot, block_id, (block_id + 1) * block)
        else:
            for spot in range(2):
                part(spot, 0, key_rows)

    column = pl.BlockSpec((rows, pair), lambda p, *_: (0, p))
    key_column = pl.BlockSpec((key_rows, pair), lambda p, *_: (0, p))
    share = 0.625 if causal else 1.0
    elements = width // HEAD * rows * key_rows * share
    return pl.pallas_call(
        kernel,
        out_shape=(
            jax.ShapeDtypeStruct((rows, width), LOW),
            jax.ShapeDtypeStruct((rows, width), F32),
        ),
        grid_spec=pltpu.PrefetchScalarGridSpec(
            num_scalar_prefetch=1,
            grid=(width // pair,),
            in_specs=[column, key_column, key_column],
            out_specs=[column, column],
        ),
        compiler_params=pltpu.CompilerParams(vmem_limit_bytes=48 * MIB),
        cost_estimate=cost(elements * 1024, 10 * MIB, elements),
    )(info, query, keys_in, values_in)


def attend_backward(causal, share_of, info, query, keys_in, values_in, out, logs, grad_out):
    rows, width = query.shape[0], query.shape[1] // share_of[1]
    skip = share_of[0] * width // (2 * HEAD)
    key_rows = keys_in.shape[0]
    block = rows // 2
    pair = 2 * HEAD

    def kernel(
        info_ref, q_ref, k_ref, v_ref, o_ref, lse_ref, g_ref,
        dq_ref, own_ref, give_ref, dk_acc, dv_acc,
    ):
        length = info_ref[1]
        dk_acc[...] = jnp.zeros_like(dk_acc)
        dv_acc[...] = jnp.zeros_like(dv_acc)

        def part(spot, block_id, extent):
            lane = lax.broadcasted_iota(jnp.int32, (block, pair), 1)
            limit = jnp.full((block, 1), length, jnp.int32)
            if causal:
                row = block_id * block + lax.broadcasted_iota(jnp.int32, (block, 1), 0)
                limit = jnp.minimum(limit, row + 1)
            allowed = lax.broadcasted_iota(jnp.int32, (block, extent), 1) < limit
            span = pl.ds(spot * block, block)
            q = q_ref[span, :]
            g = g_ref[span, :]
            along = g.astype(F32) * o_ref[span, :].astype(F32)
            dq = None
            for side in range(2):
                mine = (lane >= HEAD) if side else (lane < HEAD)
                q_side = jnp.where(mine, q, 0).astype(LOW) * LOW(HEAD ** (-0.5))
                g_side = jnp.where(mine, g, 0).astype(LOW)
                inner = jnp.sum(jnp.where(mine, along, 0.0), -1, keepdims=True)
                log_total = lse_ref[span, side * HEAD : side * HEAD + 1]
                scores = jnp.where(allowed, dot_nt(q_side, k_ref[:extent, :]), NEG)
                weights = jnp.exp(scores - log_total)
                dv_acc[:extent, :] += dot_tn(weights.astype(LOW), g_side)
                grad_w = dot_nt(g_side, v_ref[:extent, :])
                grad_s = (weights * (grad_w - inner)).astype(LOW)
                dk_acc[:extent, :] += dot_tn(grad_s, q_side)
                part_q = dot_nn(grad_s, k_ref[:extent, :])
                dq = jnp.where(mine, part_q, dq) if side else part_q
            dq_ref[span, :] = (dq * HEAD ** (-0.5)).astype(LOW)

        for variant in range(2):

            @pl.when(info_ref[0] == variant)
            def _():
                for spot in range(2):
                    block_id = OWN_BLOCKS[variant][spot]
                    part(spot, block_id, (block_id + 1) * block if causal else key_rows)
                for spot in range(2):
                    keep = slice(OWN_BLOCKS[variant][spot] * block, (OWN_BLOCKS[variant][spot] + 1) * block)
                    give = slice(OWN_BLOCKS[1 - variant][spot] * block, (OWN_BLOCKS[1 - variant][spot] + 1) * block)
                    span = slice(spot * block, (spot + 1) * block)
                    own_ref[0, span, :] = dk_acc[keep, :].astype(LOW)
                    own_ref[1, span, :] = dv_acc[keep, :].astype(LOW)
                    give_ref[0, span, :] = dk_acc[give, :].astype(LOW)
                    give_ref[1, span, :] = dv_acc[give, :].astype(LOW)

    column = pl.BlockSpec((rows, pair), lambda p, *_: (0, p + skip))
    key_column = pl.BlockSpec((key_rows, pair), lambda p, *_: (0, p + skip))
    single = pl.BlockSpec((rows, pair), lambda p, *_: (0, p))
    double = pl.BlockSpec((2, rows, pair), lambda p, *_: (0, 0, p))
    share = 0.625 if causal else 1.0
    elements = width // HEAD * rows * key_rows * share
    return pl.pallas_call(
        kernel,
        out_shape=(jax.ShapeDtypeStruct((rows, width), LOW),)
        + (jax.ShapeDtypeStruct((2, rows, width), LOW),) * 2,
        grid_spec=pltpu.PrefetchScalarGridSpec(
            num_scalar_prefetch=1,
            grid=(width // pair,),
            in_specs=[column, key_column, key_column, column, column, column],
            out_specs=[single, double, double],
            scratch_shapes=[pltpu.VMEM((key_rows, pair), F32), pltpu.VMEM((key_rows, pair), F32)],
        ),
        compiler_params=pltpu.CompilerParams(vmem_limit_bytes=48 * MIB),
        cost_estimate=cost(elements * 2560, 10 * MIB, elements),
    )(info, query, keys_in, values_in, out, logs, grad_out)


def normalize(resid):
    center = resid - jnp.mean(resid, -1, keepdims=True)
    rstd = lax.rsqrt(jnp.mean(center * center, -1, keepdims=True) + EPS)
    return center * rstd, rstd


def norm_back(grad, gain, normed, rstd):
    dn = grad * gain
    mean_dn = jnp.mean(dn, -1, keepdims=True)
    mean_dnn = jnp.mean(dn * normed, -1, keepdims=True)
    return rstd * (dn - mean_dn - normed * mean_dnn)


def row_sum(value):
    return jnp.sum(value, 0, keepdims=True)


def first_norm(attn, x_rows, w_out, w_query, gain, shift):
    rows, width = attn.shape
    block = min(256, rows)

    def kernel(o_ref, x_ref, wo_ref, wq_ref, g_ref, s_ref, n_ref, r_ref, h_ref, q_ref):
        normed, rstd = normalize(x_ref[...].astype(F32) + dot_nn(o_ref[...], wo_ref[...]))
        n_ref[...] = normed
        r_ref[...] = jnp.broadcast_to(rstd, r_ref.shape)
        low = (normed * g_ref[0:1, :] + s_ref[0:1, :]).astype(LOW)
        h_ref[...] = low
        q_ref[...] = dot_nt(low, wq_ref[...]).astype(LOW)

    row = pl.BlockSpec((block, width), lambda b: (b, 0))
    thin = pl.BlockSpec((block, 128), lambda b: (b, 0))
    return pl.pallas_call(
        kernel,
        grid=(rows // block,),
        out_shape=(
            jax.ShapeDtypeStruct((rows, width), F32),
            jax.ShapeDtypeStruct((rows, 128), F32),
            jax.ShapeDtypeStruct((rows, width), LOW),
            jax.ShapeDtypeStruct((rows, width), LOW),
        ),
        in_specs=[row, row, whole(w_out.shape), whole(w_query.shape), whole(gain.shape), whole(shift.shape)],
        out_specs=[row, thin, row, row],
        compiler_params=pltpu.CompilerParams(vmem_limit_bytes=40 * MIB),
        cost_estimate=cost(4 * rows * width * width, 8 * MIB),
    )(attn, x_rows, w_out, w_query, gain, shift)


def gelu_parts(u):
    t = 1.0 / (1.0 + (0.3275911 * 0.7071067811865476) * jnp.abs(u))
    bell = jnp.exp(-0.5 * u * u)
    poly = t * (0.254829592 + t * (-0.284496736 + t * (1.421413741 + t * (-1.453152027 + t * 1.061405429))))
    tail = 0.5 * poly * bell
    return jnp.where(u < 0, tail, 1.0 - tail), bell * 0.3989422804014327


def middle(normed_one, attn, grad_y, w_out, w_ffn, gain, shift):
    rows, width = attn.shape
    parts, _, part, _ = w_ffn.shape
    hidden = parts * part
    block = min(256, rows)
    step = min(768, hidden)

    def kernel(
        n0_ref, o_ref, y_ref, wo_ref, w_ref, g_ref, s_ref,
        out_ref, a_ref, du_ref, db3_ref, h2_ref, db2_ref, do_ref, dr2_ref, sums_ref, slope_ref,
    ):
        @pl.when(pl.program_id(0) == 0)
        def _():
            sums_ref[...] = jnp.zeros_like(sums_ref)

        def weight(which, start):
            return w_ref[start // part : (start + step) // part, which].reshape(step, width)

        h1 = n0_ref[...] * g_ref[0:1, :] + s_ref[0:1, :]
        n1, rstd1 = normalize(h1 + dot_nn(o_ref[...], wo_ref[...]))
        h2 = n1 * g_ref[1:2, :] + s_ref[1:2, :]
        h2_low = h2.astype(LOW)
        h2_ref[...] = h2_low
        branch = None
        for start in range(0, hidden, step):
            span = slice(start, start + step)
            u = dot_nt(h2_low, weight(0, start))
            share, density = gelu_parts(u)
            slope_ref[:, span] = share + u * density
            a = (u * share).astype(LOW)
            a_ref[:, span] = a
            term = dot_nn(a, weight(1, start))
            branch = term if branch is None else branch + term
        n2, rstd2 = normalize(h2 + branch)
        out_ref[...] = (n2 * g_ref[2:3, :] + s_ref[2:3, :]).astype(LOW)
        g = y_ref[...].astype(F32)
        sums_ref[2:3, :] += row_sum(g * n2)
        sums_ref[5:6, :] += row_sum(g)
        dr3 = norm_back(g, g_ref[2:3, :], n2, rstd2)
        db3 = dr3.astype(LOW)
        db3_ref[...] = db3
        dh2 = dr3
        for start in range(0, hidden, step):
            span = slice(start, start + step)
            du = (dot_nt(db3, weight(1, start)) * slope_ref[:, span]).astype(LOW)
            du_ref[:, span] = du
            dh2 = dh2 + dot_nn(du, weight(0, start))
        sums_ref[1:2, :] += row_sum(dh2 * n1)
        sums_ref[4:5, :] += row_sum(dh2)
        dr2 = norm_back(dh2, g_ref[1:2, :], n1, rstd1)
        dr2_ref[...] = dr2
        db2 = dr2.astype(LOW)
        db2_ref[...] = db2
        do_ref[...] = dot_nt(db2, wo_ref[...]).astype(LOW)

    row = pl.BlockSpec((block, width), lambda b: (b, 0))
    broad = pl.BlockSpec((block, hidden), lambda b: (b, 0))
    low_row = jax.ShapeDtypeStruct((rows, width), LOW)
    low_broad = jax.ShapeDtypeStruct((rows, hidden), LOW)
    return pl.pallas_call(
        kernel,
        grid=(rows // block,),
        out_shape=(
            low_row, low_broad, low_broad, low_row, low_row, low_row, low_row,
            jax.ShapeDtypeStruct((rows, width), F32),
            jax.ShapeDtypeStruct((8, width), F32),
        ),
        in_specs=[
            row, row, row, whole(w_out.shape), whole(w_ffn.shape), whole(gain.shape),
            whole(shift.shape),
        ],
        out_specs=[
            row, broad, broad, row, row, row, row, row,
            pl.BlockSpec((8, width), lambda b: (0, 0)),
        ],
        scratch_shapes=[pltpu.VMEM((block, hidden), F32)],
        compiler_params=pltpu.CompilerParams(vmem_limit_bytes=50 * MIB),
        cost_estimate=cost(rows * width * (8 * hidden + 4 * width), 24 * MIB, rows * hidden),
    )(normed_one, attn, grad_y, w_out, w_ffn, gain, shift)


def first_norm_back(grad_resid, grad_query, normed_one, rstd_one, w_query, w_out, gain):
    rows, width = grad_resid.shape
    block = min(256, rows)

    def kernel(dr2_ref, dq_ref, n_ref, r_ref, wq_ref, wo_ref, g_ref, dr1_ref, db1_ref, do_ref, sums_ref):
        @pl.when(pl.program_id(0) == 0)
        def _():
            sums_ref[...] = jnp.zeros_like(sums_ref)

        normed = n_ref[...]
        dh1 = dr2_ref[...] + dot_nn(dq_ref[...], wq_ref[...])
        sums_ref[0:1, :] += row_sum(dh1 * normed)
        sums_ref[3:4, :] += row_sum(dh1)
        dr1 = norm_back(dh1, g_ref[0:1, :], normed, r_ref[:, 0:1])
        dr1_ref[...] = dr1
        db1 = dr1.astype(LOW)
        db1_ref[...] = db1
        do_ref[...] = dot_nt(db1, wo_ref[...]).astype(LOW)

    row = pl.BlockSpec((block, width), lambda b: (b, 0))
    thin = pl.BlockSpec((block, 128), lambda b: (b, 0))
    low_row = jax.ShapeDtypeStruct((rows, width), LOW)
    return pl.pallas_call(
        kernel,
        grid=(rows // block,),
        out_shape=(
            jax.ShapeDtypeStruct((rows, width), F32), low_row, low_row,
            jax.ShapeDtypeStruct((8, width), F32),
        ),
        in_specs=[row, row, row, thin, whole(w_query.shape), whole(w_out.shape), whole(gain.shape)],
        out_specs=[row, row, row, pl.BlockSpec((8, width), lambda b: (0, 0))],
        compiler_params=pltpu.CompilerParams(vmem_limit_bytes=40 * MIB),
        cost_estimate=cost(4 * rows * width * width, 8 * MIB),
    )(grad_resid, grad_query, normed_one, rstd_one, w_query, w_out, gain)


def swap(value, axis, bit, size):
    return lax.ppermute(value, axis, [(d, d ^ bit) for d in range(size)])


def ordered(own, other, bit, axis):
    low = jnp.where(bit, other, own)
    high = jnp.where(bit, own, other)
    return jnp.concatenate([low, high], axis)


class Place:
    def __init__(self):
        self.dp = lax.axis_size("dp")
        self.tensor = lax.axis_size("tensor")
        index = lax.axis_index("dp")
        self.z = lax.axis_index("tensor")
        self.core = index & 1
        self.chip = (index >> 1) & 3


def after(value, *deps):
    return lax.optimization_barrier((value, deps))[0]


def beside(always, work, *operands):
    def nothing(*operands):
        return jax.tree.map(lambda leaf: jnp.zeros(leaf.shape, leaf.dtype), jax.eval_shape(work, *operands))

    return lax.optimization_barrier(
        lax.cond(always, work, nothing, *lax.optimization_barrier(operands))
    )


def piece_of(place, shard):
    count, rows, width = shard.shape
    return lax.dynamic_slice(
        shard,
        (0, place.chip * (rows // 4), place.core * (width // 2)),
        (count, rows // 4, width // 2),
    )


def near_pair(piece, far):
    return jnp.stack([piece, far])


def in_slots(near, far):
    return jnp.stack([near[0], far, near[1]])


def from_chips(place, got, *deps):
    others = [swap(got, "dp", 2 * r, place.dp) for r in range(1, 4)]
    if deps:
        others = after(others, *deps)
    return [got, *others]


def assemble(place, shard, mine, theirs):
    count, rows, width = shard.shape
    quarter, half, slots = rows // 4, width // 2, mine.shape[1] + 1

    def kernel(info_ref, shard_ref, mine_ref, theirs_ref, *out_refs):
        def fill(left, right):
            for t, out_ref in enumerate(out_refs):
                out_ref[0] = shard_ref[t]
                for r in range(1, slots):
                    out_ref[r, :, :half] = left[0, r - 1, t]
                    out_ref[r, :, half:] = right[0, r - 1, t]

        @pl.when(info_ref[0] == 0)
        def _():
            fill(mine_ref, theirs_ref)

        @pl.when(info_ref[0] == 1)
        def _():
            fill(theirs_ref, mine_ref)

    def spot(p, info):
        return (p ^ info[1], 0, 0, 0, 0)

    part = pl.BlockSpec((1, slots - 1, count, quarter, half), spot)
    outs = pl.pallas_call(
        kernel,
        out_shape=(jax.ShapeDtypeStruct((slots, rows, width), LOW),) * count,
        grid_spec=pltpu.PrefetchScalarGridSpec(
            num_scalar_prefetch=1,
            grid=(4,),
            in_specs=[pl.BlockSpec((count, quarter, width), lambda p, info: (0, p, 0)), part, part],
            out_specs=[pl.BlockSpec((slots, quarter, width), lambda p, info: (0, p, 0))] * count,
        ),
        compiler_params=pltpu.CompilerParams(vmem_limit_bytes=32 * MIB),
        cost_estimate=cost(0, 4 * count * slots * rows * width),
    )(jnp.stack([place.core, place.chip]).astype(jnp.int32), shard, mine, theirs)
    return [out.reshape(slots * rows, width) for out in outs]


def weight_grads(place, pairs):
    count = len(pairs)
    n, columns = pairs[0][0].shape
    width = pairs[0][1].shape[1]
    half = width // 2
    block = min(768, columns)
    steps = columns // block
    chunk = min(256, block)

    def kernel(info_ref, *refs):
        sides, (keep_ref, give_ref) = refs[: 2 * count], refs[2 * count :]
        keep = pl.multiple_of(info_ref[0] * half, 128)
        give = pl.multiple_of((1 - info_ref[0]) * half, 128)
        for t in range(count):

            @pl.when(pl.program_id(0) // steps == t)
            def _():
                g_ref, a_ref = sides[2 * t], sides[2 * t + 1]
                for start in range(0, block, chunk):
                    at = slice(start, start + chunk)
                    left = g_ref[:, at]
                    keep_ref[0, at, :] = dot_tn(left, a_ref[:, pl.ds(keep, half)]).astype(LOW)
                    give_ref[0, at, :] = dot_tn(left, a_ref[:, pl.ds(give, half)]).astype(LOW)

    def rows_spec(t):
        return pl.BlockSpec(
            (n, block), lambda g, info: (0, jnp.clip(g - t * steps, 0, steps - 1))
        )

    out = pl.BlockSpec((1, block, half), lambda g, info: (g // steps, g % steps, 0))
    in_specs, operands = [], []
    for t, (g, a) in enumerate(pairs):
        in_specs += [rows_spec(t), pl.BlockSpec((n, width), lambda g, info: (0, 0))]
        operands += [g, a]
    return pl.pallas_call(
        kernel,
        out_shape=(jax.ShapeDtypeStruct((count, columns, half), LOW),) * 2,
        grid_spec=pltpu.PrefetchScalarGridSpec(
            num_scalar_prefetch=1,
            grid=(count * steps,),
            in_specs=in_specs,
            out_specs=[out, out],
        ),
        compiler_params=pltpu.CompilerParams(vmem_limit_bytes=48 * MIB),
        cost_estimate=cost(2 * count * n * columns * width, 4 * count * columns * width),
    )(jnp.stack([place.core]).astype(jnp.int32), *operands)


def chip_parts(place, keep, other):
    count, rows, half = keep.shape
    slots = place.tensor
    quarter = rows // slots // 4

    def kernel(info_ref, keep_ref, other_ref, *part_refs):
        for r, part_ref in enumerate(part_refs):
            for z in range(slots):
                at = pl.multiple_of(4 * z * quarter + (info_ref[0] ^ r) * quarter, 16)
                span = pl.ds(at, quarter)
                total = keep_ref[0, span, :].astype(F32) + other_ref[0, span, :].astype(F32)
                part_ref[0, z] = total.astype(LOW)

    row = pl.BlockSpec((1, rows, half), lambda t, info: (t, 0, 0))
    part = pl.BlockSpec((1, slots, quarter, half), lambda t, info: (t, 0, 0, 0))
    return pl.pallas_call(
        kernel,
        out_shape=(jax.ShapeDtypeStruct((count, slots, quarter, half), LOW),) * 4,
        grid_spec=pltpu.PrefetchScalarGridSpec(
            num_scalar_prefetch=1, grid=(count,), in_specs=[row, row], out_specs=[part] * 4
        ),
        compiler_params=pltpu.CompilerParams(vmem_limit_bytes=32 * MIB),
        cost_estimate=cost(0, 6 * count * rows * half),
    )(jnp.stack([place.chip]).astype(jnp.int32), keep, other)


def swap_chips(place, parts):
    return [swap(parts[r], "dp", 2 * r, place.dp) for r in range(1, 4)]


def add_all(own, others):
    own = own.astype(F32)
    for other in others:
        own = own + other.astype(F32)
    return own


def near_parts(place, total, natural):
    def slot(r):
        if natural:
            return lax.dynamic_index_in_dim(total, place.z ^ r, 1, False)
        return total[:, r]

    stay, leave = jnp.stack([slot(0), slot(2)]), jnp.stack([slot(1), slot(3)])
    return stay, leave.astype(LOW)


def add_far(place, total, other):
    piece = total[0] + other.astype(F32)
    bit = 8
    while bit < place.dp:
        piece = piece + swap(piece.astype(LOW), "dp", bit, place.dp).astype(F32)
        bit *= 2
    return piece.astype(LOW)


def regather(place, piece, *deps):
    own = jnp.stack(from_chips(place, piece, *deps))
    return own, swap(own, "dp", 1, place.dp)


def finish(place, own, other, groups):
    _, count, quarter, half = own.shape
    rows, width = 4 * quarter, 2 * half

    def kernel(info_ref, own_ref, other_ref, *out_refs):
        core, chip = info_ref[0], info_ref[1]
        t = 0
        for group, out_ref in zip(groups, out_refs, strict=True):
            for g in range(group):
                for p in range(4):
                    at = slice(p * quarter, (p + 1) * quarter)
                    mine, theirs = own_ref[p ^ chip, t].astype(F32), other_ref[p ^ chip, t].astype(F32)
                    out_ref[g, at, :half] = jnp.where(core == 0, mine, theirs)
                    out_ref[g, at, half:] = jnp.where(core == 0, theirs, mine)
                t += 1

    shapes = [(group, rows, width) for group in groups]
    return pl.pallas_call(
        kernel,
        out_shape=[jax.ShapeDtypeStruct(shape, F32) for shape in shapes],
        grid_spec=pltpu.PrefetchScalarGridSpec(
            num_scalar_prefetch=1,
            grid=(1,),
            in_specs=[whole(own.shape), whole(own.shape)],
            out_specs=[whole(shape) for shape in shapes],
        ),
        compiler_params=pltpu.CompilerParams(vmem_limit_bytes=48 * MIB),
        cost_estimate=cost(0, 6 * count * rows * width),
    )(jnp.stack([place.core, place.chip]).astype(jnp.int32), own, other)


def finish_ffn(parts):
    _, _, quarter, half = parts.shape
    rows, width = 4 * quarter, 2 * half

    def kernel(parts_ref, down_ref, up_ref):
        for side in range(2):
            columns = slice(side * half, (side + 1) * half)
            for q in range(4):
                at = slice(q * quarter, (q + 1) * quarter)
                down_ref[at, columns] = parts_ref[2 * q + side, 0].astype(F32)
            full = jnp.concatenate([parts_ref[2 * q + side, 1] for q in range(4)], 0)
            up_ref[columns, :] = full.astype(F32).T

    return pl.pallas_call(
        kernel,
        out_shape=(jax.ShapeDtypeStruct((rows, width), F32), jax.ShapeDtypeStruct((width, rows), F32)),
        compiler_params=pltpu.CompilerParams(vmem_limit_bytes=32 * MIB),
        cost_estimate=cost(0, 12 * rows * width),
    )(parts)


def local(
    inputs, memory, cotangent, dec_len, mem_len,
    self_qkv, self_out, cross_q, cross_kv, cross_out, ffn_in, ffn_out, ln_gain, ln_bias,
):
    place = Place()
    dp, slots = place.dp, place.tensor
    axes = ("dp", "tensor")
    width = inputs.shape[3]
    length = inputs.shape[2]
    block = length // slots
    micro = place.z // 2
    owner = place.core == (place.z & 1)
    fetch_perm = [
        (d * slots + t, (d ^ 1) * slots + t)
        for d in range(dp)
        for t in range(slots)
        if d % 2 == t % 2
    ]
    spread = []
    for call in range(2):
        spread.append(
            [
                ((g + hh) * slots + s, (g + s % 2) * slots + OWN_BLOCKS[hh][(call + s // 2) % 2])
                for g in range(0, dp, 2)
                for s in range(slots)
                for hh in range(2)
            ]
        )
    collect = [[(dst, src) for src, dst in perm] for perm in spread]

    def fetch(value):
        mine = lax.dynamic_index_in_dim(value, micro, 0, False)[0]
        return jnp.where(owner, mine, lax.ppermute(mine, axes, fetch_perm))

    def own_rows(value):
        return jnp.concatenate(
            [
                lax.dynamic_slice_in_dim(value, place.core * block, block, 0),
                lax.dynamic_slice_in_dim(value, (3 - place.core) * block, block, 0),
            ],
            0,
        )

    def start_rows(value):
        return [
            lax.ppermute(
                lax.dynamic_slice_in_dim(value, ((call + micro) % 2) * block, block, 0), axes, spread[call]
            )
            for call in range(2)
        ]

    def end_rows(got):
        near = place.z // 2 == 0
        return jnp.stack([jnp.where(near, got[0], got[1]), jnp.where(near, got[1], got[0])])[:, None]

    def collect_rows(value):
        return [
            lax.ppermute(
                lax.dynamic_index_in_dim(value, (place.z // 2 + call) % 2, 0, False)[0], axes, collect[call]
            )
            for call in range(2)
        ]


    def flat(weights):
        return weights.reshape(-1, width)

    index = lax.axis_index("dp")
    at_ffn = ffn_out.shape[0] // dp
    piece_ffn = jnp.stack(
        [
            lax.dynamic_slice_in_dim(ffn_in, index * at_ffn, at_ffn, 1).T,
            lax.dynamic_slice_in_dim(ffn_out, index * at_ffn, at_ffn, 0),
        ]
    )
    shard_qkv = jnp.swapaxes(self_qkv, 1, 2)
    shard_mid = jnp.concatenate(
        [self_out[None], cross_q.T[None], jnp.swapaxes(cross_kv, 1, 2), cross_out[None]], 0
    )
    always = dec_len[0, 0] > 0
    pieces = jnp.concatenate([piece_of(place, shard_qkv), piece_of(place, shard_mid)], 0)
    lengths = jnp.stack([dec_len, mem_len], -1)

    def first_fetch(pieces, *values):
        far = swap(pieces, "tensor", 2, slots)
        x_all, mem_all, lens = (fetch(value) for value in values)
        return far, x_all, mem_all, own_rows(x_all), own_rows(mem_all), lens

    far, x_all, mem_all, x_own, mem_own, lens = beside(
        always, first_fetch, after(pieces, piece_ffn), inputs, memory, lengths
    )
    core = place.core.astype(jnp.int32)
    info_self = jnp.stack([core, lens[0]])
    info_cross = jnp.stack([core, lens[1]])
    got = in_slots(swap(near_pair(pieces, far), "tensor", 1, slots), far)
    w_ffn = lax.all_gather(after(piece_ffn, got), ("tensor", "dp"), axis=0)
    got_qkv = jnp.stack(from_chips(place, got[:, :3]))
    wq, wk, wv = assemble(place, shard_qkv, got_qkv, swap(got_qkv, "dp", 1, dp))

    def self_forward(got, rows, x_own, x_all, wq, wk, wv, info):
        query = dot_nt(x_own, wq).astype(LOW)
        key = dot_nt(x_all, wk).astype(LOW)
        value = dot_nt(x_all, wv).astype(LOW)
        return (
            swap_chips(place, [got] * 4),
            collect_rows(rows),
            (query, key, value),
            attend_forward(True, info, query, key, value),
        )

    others, got_y, (query_s, key_s, value_s), (attn_s, logs_s) = beside(
        always, self_forward, got[:, 3:], cotangent, x_own, x_all, wq, wk, wv, info_self
    )
    got_mid = jnp.stack([got[:, 3:], *others])
    w_so, w_cq, w_ck, w_cv, w_co = assemble(
        place, shard_mid, got_mid, swap(got_mid, "dp", 1, dp)
    )
    grad_y = jnp.concatenate(
        [jnp.where(micro == 0, got_y[0], got_y[1]), jnp.where(micro == 0, got_y[1], got_y[0])], 0
    )
    normed_one, rstd_one, h1_low, query_c = first_norm(
        attn_s, x_own, w_so, w_cq, ln_gain, ln_bias
    )
    key_c = dot_nt(mem_all, w_ck).astype(LOW)
    value_c = dot_nt(mem_all, w_cv).astype(LOW)
    attn_c, logs_c = attend_forward(False, info_cross, query_c, key_c, value_c)
    (out_rows, act, grad_pre, grad_b3, h2_low, grad_b2, grad_oc, grad_r2, sums_late) = middle(
        normed_one, attn_c, grad_y, w_co, w_ffn, ln_gain, ln_bias
    )

    keep_down, give_down = weight_grads(place, [(act, grad_b3)])

    def up_grads(give, *pair):
        return swap(give, "dp", 1, dp), weight_grads(place, [pair])

    other_down, (keep_up, give_up) = beside(always, up_grads, give_down, grad_pre, h2_low)
    other_up = swap(give_up, "dp", 1, dp)
    parts_down = chip_parts(place, keep_down, other_down)
    parts_up = chip_parts(place, keep_up, other_up)
    parts_ffn = [jnp.concatenate(pair, 0) for pair in zip(parts_down, parts_up, strict=True)]

    def cross_back(part_x, part_y, rows, *operands):
        return (
            swap(part_x, "dp", 2, dp),
            swap(part_y, "dp", 4, dp),
            start_rows(rows),
            attend_backward(False, (0, 1), *operands),
        )

    ffn_x, ffn_y, got_out, (dq_c, own_c, give_c) = beside(
        always, cross_back, parts_ffn[1], parts_ffn[2], out_rows,
        info_cross, query_c, key_c, value_c, attn_c, logs_c, grad_oc,
    )
    out = end_rows(got_out)
    own_c = (own_c.astype(F32) + swap(give_c, "dp", 1, dp).astype(F32)).astype(LOW)
    dk_c, dv_c = own_c[0], own_c[1]
    grad_r1, grad_b1, grad_os, sums_first = first_norm_back(
        grad_r2, dq_c, normed_one, rstd_one, w_cq, w_so, ln_gain
    )
    d_mem = (dot_nn(dk_c, w_ck) + dot_nn(dv_c, w_cv)).astype(LOW)

    def mid_grads(part, rows, *sides):
        return (
            swap(part, "dp", 6, dp),
            start_rows(rows),
            weight_grads(place, [(sides[2 * t], sides[2 * t + 1]) for t in range(5)]),
        )

    ffn_xy, got_mem, (keep_mid, give_mid) = beside(
        always, mid_grads, parts_ffn[3], d_mem,
        attn_s, grad_b1, dq_c, h1_low, dk_c, mem_own, dv_c, mem_own, attn_c, grad_b2,
    )
    total_ffn = add_all(parts_ffn[0], [ffn_x, ffn_y, ffn_xy])
    near_ffn = near_parts(place, total_ffn, True)
    parts_mid = chip_parts(place, keep_mid, swap(give_mid, "dp", 1, dp))
    sums = sums_late + sums_first
    back_operands = (info_self, query_s, key_s, value_s, attn_s, logs_s, grad_os)

    def self_back_first(part_x, part_y, sums, leave, *operands):
        return (
            swap(part_x, "dp", 2, dp),
            swap(part_y, "dp", 4, dp),
            swap(sums, "dp", 2, dp),
            swap(leave, "tensor", 1, slots),
            attend_backward(True, (0, 2), *operands),
        )

    def self_back_second(part_xy, sums, leave, give, *operands):
        return (
            swap(part_xy, "dp", 6, dp),
            swap(sums, "dp", 4, dp),
            swap(leave, "tensor", 2, slots),
            swap(give, "dp", 1, dp),
            attend_backward(True, (1, 2), *operands),
        )

    from_x, from_y, other_sums, other_ffn, (dq_a, own_a, give_a) = beside(
        always, self_back_first, parts_mid[1], parts_mid[2], sums, near_ffn[1], *back_operands
    )
    sums = sums + other_sums
    far_ffn = near_ffn[0] + other_ffn.astype(F32)
    from_xy, other_sums, other_ffn, other_a, (dq_b, own_b, give_b) = beside(
        always, self_back_second, parts_mid[3], sums, far_ffn[1].astype(LOW), give_a, *back_operands
    )
    sums = sums + other_sums
    piece_ffn = add_far(place, far_ffn, other_ffn)
    other_b = swap(give_b, "dp", 1, dp)
    dkv_s = jnp.concatenate(
        [
            (own.astype(F32) + other.astype(F32)).astype(LOW)
            for own, other in ((own_a, other_a), (own_b, other_b))
        ],
        2,
    )
    dq_s = jnp.concatenate([dq_a, dq_b], 1)
    dk_s, dv_s = dkv_s[0], dkv_s[1]
    keep_qkv, give_qkv = weight_grads(place, [(dq_s, x_own), (dk_s, x_own), (dv_s, x_own)])
    total_mid = add_all(parts_mid[0], [from_x, from_y, from_xy])
    near_mid = near_parts(place, total_mid, False)

    def input_grads(give, leave, sums, resid, *pairs):
        total = resid
        for t in range(3):
            total = total + dot_nn(pairs[t], pairs[3 + t])
        return (
            swap(give, "dp", 1, dp),
            swap(leave, "tensor", 1, slots),
            swap(sums, "dp", 1, dp),
            total.astype(LOW),
        )

    other_qkv, other, other_sums, d_x = beside(
        always, input_grads, give_qkv, near_mid[1], sums, grad_r1, dq_s, dk_s, dv_s, wq, wk, wv
    )
    sums = sums + other_sums
    bit = 8
    while bit < dp:
        sums = sums + swap(sums, "dp", bit, dp)
        bit *= 2
    far_mid = near_mid[0] + other.astype(F32)
    parts_qkv = chip_parts(place, keep_qkv, other_qkv)

    def send_qkv(parts, rows, leave):
        return (
            swap_chips(place, [None, *parts]),
            start_rows(rows),
            swap(leave, "tensor", 2, slots),
        )

    others_qkv, got_x, other = beside(
        always, send_qkv, parts_qkv[1:], d_x, far_mid[1].astype(LOW)
    )
    piece_mid = add_far(place, far_mid, other)
    near = near_parts(place, add_all(parts_qkv[0], others_qkv), False)
    d_x = end_rows(got_x).astype(F32)
    d_mem = end_rows(got_mem).astype(F32)
    other, other_sums = after(
        (swap(near[1], "tensor", 1, slots), swap(sums, "tensor", 1, slots)), d_x, d_mem
    )
    sums = sums + other_sums
    far = near[0] + other.astype(F32)
    other, other_sums = after(
        (swap(far[1].astype(LOW), "tensor", 2, slots), swap(sums, "tensor", 2, slots)), out
    )
    sums = sums + other_sums
    piece = jnp.concatenate([add_far(place, far, other), piece_mid], 0)
    groups = [[first + d for d in range(8)] for first in range(0, dp, 8)]
    d_down, d_up = finish_ffn(lax.all_gather(piece_ffn, "dp", axis=0, axis_index_groups=groups))
    own, other = regather(place, piece, d_down, d_up)
    d_qkv, d_so, d_cq, d_ckv, d_co = finish(place, own, other, (3, 1, 1, 2, 1))
    return (
        out,
        d_x,
        d_mem,
        jnp.swapaxes(d_qkv, 1, 2),
        d_so[0],
        d_cq[0].T,
        jnp.swapaxes(d_ckv, 1, 2),
        d_co[0],
        d_up,
        d_down,
        sums[0:3],
        sums[3:6],
    )


def solution(mesh):
    rows = P(None, "dp", "tensor", None)
    in_specs = (
        P(None, "dp", None, None),
        P(None, "dp", None, None),
        rows,
        P(None, "dp"),
        P(None, "dp"),
        P(None, None, "tensor"),
        P("tensor", None),
        P(None, "tensor"),
        P(None, None, "tensor"),
        P("tensor", None),
        P(None, "tensor"),
        P("tensor", None),
        P(),
        P(),
    )
    out_specs = (
        rows,
        rows,
        rows,
        P(None, None, "tensor"),
        P("tensor", None),
        P(None, "tensor"),
        P(None, None, "tensor"),
        P("tensor", None),
        P(None, "tensor"),
        P("tensor", None),
        P(),
        P(),
    )
    return jax.shard_map(local, mesh=mesh, in_specs=in_specs, out_specs=out_specs, check_vma=False)
```

```python
import functools

import jax
import jax.numpy as jnp
from jax import lax
from jax.experimental import pallas as pl
from jax.experimental.pallas import tpu as pltpu
from jax.sharding import PartitionSpec as P

HEAD = 64
EPS = 1e-05
NEG = -1e30
LOW = jnp.bfloat16
F32 = jnp.float32
OWN_BLOCKS = ((0, 3), (1, 2))
MIB = 1024 * 1024


def dot_nn(left, right):
    return lax.dot_general(left, right, (((1,), (0,)), ((), ())), preferred_element_type=F32)


def dot_nt(left, right):
    return lax.dot_general(left, right, (((1,), (1,)), ((), ())), preferred_element_type=F32)


def dot_tn(left, right):
    return lax.dot_general(left, right, (((0,), (0,)), ((), ())), preferred_element_type=F32)


def cost(flops, size, trans=0):
    return pl.CostEstimate(flops=int(flops), bytes_accessed=int(size), transcendentals=int(trans))


def whole(shape):
    return pl.BlockSpec(shape, lambda *_: (0,) * len(shape), pipeline_mode=pl.Buffered(1))


def attend_forward(causal, info, query, keys_in, values_in):
    rows, width = query.shape
    key_rows = keys_in.shape[0]
    block = rows // 2
    pair = 2 * HEAD

    def kernel(info_ref, q_ref, k_ref, v_ref, o_ref, lse_ref):
        length = info_ref[1]

        def part(spot, block_id, extent):
            lane = lax.broadcasted_iota(jnp.int32, (block, pair), 1)
            limit = jnp.full((block, 1), length, jnp.int32)
            if causal:
                row = block_id * block + lax.broadcasted_iota(jnp.int32, (block, 1), 0)
                limit = jnp.minimum(limit, row + 1)
            allowed = lax.broadcasted_iota(jnp.int32, (block, extent), 1) < limit
            span = pl.ds(spot * block, block)
            q = q_ref[span, :]
            out, logs = None, None
            for side in range(2):
                mine = (lane >= HEAD) if side else (lane < HEAD)
                q_side = jnp.where(mine, q, 0).astype(LOW) * LOW(HEAD ** (-0.5))
                scores = jnp.where(allowed, dot_nt(q_side, k_ref[:extent, :]), NEG)
                peak = jnp.max(scores, -1, keepdims=True)
                weights = jnp.exp(scores - peak)
                total = jnp.sum(weights, -1, keepdims=True)
                mixed = dot_nn(weights.astype(LOW), v_ref[:extent, :]) / total
                log_total = peak + jnp.log(total)
                if side:
                    out = jnp.where(mine, mixed, out)
                    logs = jnp.where(mine, log_total, logs)
                else:
                    out, logs = mixed, jnp.broadcast_to(log_total, (block, pair))
            o_ref[span, :] = out.astype(LOW)
            lse_ref[span, :] = logs

        if causal:
            for variant in range(2):

                @pl.when(info_ref[0] == variant)
                def _():
                    for spot in range(2):
                        block_id = OWN_BLOCKS[variant][spot]
                        part(spot, block_id, (block_id + 1) * block)
        else:
            for spot in range(2):
                part(spot, 0, key_rows)

    column = pl.BlockSpec((rows, pair), lambda p, *_: (0, p))
    key_column = pl.BlockSpec((key_rows, pair), lambda p, *_: (0, p))
    share = 0.625 if causal else 1.0
    elements = width // HEAD * rows * key_rows * share
    return pl.pallas_call(
        kernel,
        out_shape=(
            jax.ShapeDtypeStruct((rows, width), LOW),
            jax.ShapeDtypeStruct((rows, width), F32),
        ),
        grid_spec=pltpu.PrefetchScalarGridSpec(
            num_scalar_prefetch=1,
            grid=(width // pair,),
            in_specs=[column, key_column, key_column],
            out_specs=[column, column],
        ),
        compiler_params=pltpu.CompilerParams(vmem_limit_bytes=48 * MIB),
        cost_estimate=cost(elements * 1024, 10 * MIB, elements),
    )(info, query, keys_in, values_in)


def attend_backward(causal, share_of, info, query, keys_in, values_in, out, logs, grad_out):
    rows, width = query.shape[0], query.shape[1] // share_of[1]
    skip = share_of[0] * width // (2 * HEAD)
    key_rows = keys_in.shape[0]
    block = rows // 2
    pair = 2 * HEAD

    def kernel(
        info_ref, q_ref, k_ref, v_ref, o_ref, lse_ref, g_ref,
        dq_ref, dk_ref, dv_ref, give_ref, dk_acc, dv_acc,
    ):
        length = info_ref[1]
        dk_acc[...] = jnp.zeros_like(dk_acc)
        dv_acc[...] = jnp.zeros_like(dv_acc)

        def part(spot, block_id, extent):
            lane = lax.broadcasted_iota(jnp.int32, (block, pair), 1)
            limit = jnp.full((block, 1), length, jnp.int32)
            if causal:
                row = block_id * block + lax.broadcasted_iota(jnp.int32, (block, 1), 0)
                limit = jnp.minimum(limit, row + 1)
            allowed = lax.broadcasted_iota(jnp.int32, (block, extent), 1) < limit
            span = pl.ds(spot * block, block)
            q = q_ref[span, :]
            g = g_ref[span, :]
            along = g.astype(F32) * o_ref[span, :].astype(F32)
            dq = None
            for side in range(2):
                mine = (lane >= HEAD) if side else (lane < HEAD)
                q_side = jnp.where(mine, q, 0).astype(LOW) * LOW(HEAD ** (-0.5))
                g_side = jnp.where(mine, g, 0).astype(LOW)
                inner = jnp.sum(jnp.where(mine, along, 0.0), -1, keepdims=True)
                log_total = lse_ref[span, side * HEAD : side * HEAD + 1]
                scores = jnp.where(allowed, dot_nt(q_side, k_ref[:extent, :]), NEG)
                weights = jnp.exp(scores - log_total)
                dv_acc[:extent, :] += dot_tn(weights.astype(LOW), g_side)
                grad_w = dot_nt(g_side, v_ref[:extent, :])
                grad_s = (weights * (grad_w - inner)).astype(LOW)
                dk_acc[:extent, :] += dot_tn(grad_s, q_side)
                part_q = dot_nn(grad_s, k_ref[:extent, :])
                dq = jnp.where(mine, part_q, dq) if side else part_q
            dq_ref[span, :] = (dq * HEAD ** (-0.5)).astype(LOW)

        for variant in range(2):

            @pl.when(info_ref[0] == variant)
            def _():
                for spot in range(2):
                    block_id = OWN_BLOCKS[variant][spot]
                    part(spot, block_id, (block_id + 1) * block if causal else key_rows)
                for spot in range(2):
                    keep = slice(OWN_BLOCKS[variant][spot] * block, (OWN_BLOCKS[variant][spot] + 1) * block)
                    give = slice(OWN_BLOCKS[1 - variant][spot] * block, (OWN_BLOCKS[1 - variant][spot] + 1) * block)
                    span = slice(spot * block, (spot + 1) * block)
                    dk_ref[span, :] = dk_acc[keep, :].astype(LOW)
                    dv_ref[span, :] = dv_acc[keep, :].astype(LOW)
                    give_ref[0, span, :] = dk_acc[give, :].astype(LOW)
                    give_ref[1, span, :] = dv_acc[give, :].astype(LOW)

    column = pl.BlockSpec((rows, pair), lambda p, *_: (0, p + skip))
    key_column = pl.BlockSpec((key_rows, pair), lambda p, *_: (0, p + skip))
    single = pl.BlockSpec((rows, pair), lambda p, *_: (0, p))
    double = pl.BlockSpec((2, rows, pair), lambda p, *_: (0, 0, p))
    share = 0.625 if causal else 1.0
    elements = width // HEAD * rows * key_rows * share
    return pl.pallas_call(
        kernel,
        out_shape=(jax.ShapeDtypeStruct((rows, width), LOW),) * 3
        + (jax.ShapeDtypeStruct((2, rows, width), LOW),),
        grid_spec=pltpu.PrefetchScalarGridSpec(
            num_scalar_prefetch=1,
            grid=(width // pair,),
            in_specs=[column, key_column, key_column, column, column, column],
            out_specs=[single, single, single, double],
            scratch_shapes=[pltpu.VMEM((key_rows, pair), F32), pltpu.VMEM((key_rows, pair), F32)],
        ),
        compiler_params=pltpu.CompilerParams(vmem_limit_bytes=48 * MIB),
        cost_estimate=cost(elements * 2560, 10 * MIB, elements),
    )(info, query, keys_in, values_in, out, logs, grad_out)


def normalize(resid):
    center = resid - jnp.mean(resid, -1, keepdims=True)
    rstd = lax.rsqrt(jnp.mean(center * center, -1, keepdims=True) + EPS)
    return center * rstd, rstd


def norm_back(grad, gain, normed, rstd):
    dn = grad * gain
    mean_dn = jnp.mean(dn, -1, keepdims=True)
    mean_dnn = jnp.mean(dn * normed, -1, keepdims=True)
    return rstd * (dn - mean_dn - normed * mean_dnn)


def row_sum(value):
    return jnp.sum(value, 0, keepdims=True)


def first_norm(attn, x_rows, w_out, w_query, gain, shift):
    rows, width = attn.shape
    block = min(256, rows)

    def kernel(o_ref, x_ref, wo_ref, wq_ref, g_ref, s_ref, n_ref, r_ref, h_ref, q_ref):
        normed, rstd = normalize(x_ref[...].astype(F32) + dot_nn(o_ref[...], wo_ref[...]))
        n_ref[...] = normed
        r_ref[...] = jnp.broadcast_to(rstd, r_ref.shape)
        low = (normed * g_ref[0:1, :] + s_ref[0:1, :]).astype(LOW)
        h_ref[...] = low
        q_ref[...] = dot_nt(low, wq_ref[...]).astype(LOW)

    row = pl.BlockSpec((block, width), lambda b: (b, 0))
    thin = pl.BlockSpec((block, 128), lambda b: (b, 0))
    return pl.pallas_call(
        kernel,
        grid=(rows // block,),
        out_shape=(
            jax.ShapeDtypeStruct((rows, width), F32),
            jax.ShapeDtypeStruct((rows, 128), F32),
            jax.ShapeDtypeStruct((rows, width), LOW),
            jax.ShapeDtypeStruct((rows, width), LOW),
        ),
        in_specs=[row, row, whole(w_out.shape), whole(w_query.shape), whole(gain.shape), whole(shift.shape)],
        out_specs=[row, thin, row, row],
        compiler_params=pltpu.CompilerParams(vmem_limit_bytes=40 * MIB),
        cost_estimate=cost(4 * rows * width * width, 8 * MIB),
    )(attn, x_rows, w_out, w_query, gain, shift)


def gelu_parts(u):
    t = 1.0 / (1.0 + (0.3275911 * 0.7071067811865476) * jnp.abs(u))
    bell = jnp.exp(-0.5 * u * u)
    poly = t * (0.254829592 + t * (-0.284496736 + t * (1.421413741 + t * (-1.453152027 + t * 1.061405429))))
    tail = 0.5 * poly * bell
    return jnp.where(u < 0, tail, 1.0 - tail), bell * 0.3989422804014327


def middle(normed_one, attn, grad_y, w_out, w_ffn, gain, shift):
    rows, width = attn.shape
    parts, _, part, _ = w_ffn.shape
    hidden = parts * part
    block = min(256, rows)
    step = min(768, hidden)

    def kernel(
        n0_ref, o_ref, y_ref, wo_ref, w_ref, g_ref, s_ref,
        out_ref, a_ref, du_ref, db3_ref, h2_ref, db2_ref, do_ref, dr2_ref, sums_ref, slope_ref,
    ):
        @pl.when(pl.program_id(0) == 0)
        def _():
            sums_ref[...] = jnp.zeros_like(sums_ref)

        def weight(which, start):
            return w_ref[start // part : (start + step) // part, which].reshape(step, width)

        h1 = n0_ref[...] * g_ref[0:1, :] + s_ref[0:1, :]
        n1, rstd1 = normalize(h1 + dot_nn(o_ref[...], wo_ref[...]))
        h2 = n1 * g_ref[1:2, :] + s_ref[1:2, :]
        h2_low = h2.astype(LOW)
        h2_ref[...] = h2_low
        branch = None
        for start in range(0, hidden, step):
            span = slice(start, start + step)
            u = dot_nt(h2_low, weight(0, start))
            share, density = gelu_parts(u)
            slope_ref[:, span] = share + u * density
            a = (u * share).astype(LOW)
            a_ref[:, span] = a
            term = dot_nn(a, weight(1, start))
            branch = term if branch is None else branch + term
        n2, rstd2 = normalize(h2 + branch)
        out_ref[...] = (n2 * g_ref[2:3, :] + s_ref[2:3, :]).astype(LOW)
        g = y_ref[...].astype(F32)
        sums_ref[2:3, :] += row_sum(g * n2)
        sums_ref[5:6, :] += row_sum(g)
        dr3 = norm_back(g, g_ref[2:3, :], n2, rstd2)
        db3 = dr3.astype(LOW)
        db3_ref[...] = db3
        dh2 = dr3
        for start in range(0, hidden, step):
            span = slice(start, start + step)
            du = (dot_nt(db3, weight(1, start)) * slope_ref[:, span]).astype(LOW)
            du_ref[:, span] = du
            dh2 = dh2 + dot_nn(du, weight(0, start))
        sums_ref[1:2, :] += row_sum(dh2 * n1)
        sums_ref[4:5, :] += row_sum(dh2)
        dr2 = norm_back(dh2, g_ref[1:2, :], n1, rstd1)
        dr2_ref[...] = dr2
        db2 = dr2.astype(LOW)
        db2_ref[...] = db2
        do_ref[...] = dot_nt(db2, wo_ref[...]).astype(LOW)

    row = pl.BlockSpec((block, width), lambda b: (b, 0))
    broad = pl.BlockSpec((block, hidden), lambda b: (b, 0))
    low_row = jax.ShapeDtypeStruct((rows, width), LOW)
    low_broad = jax.ShapeDtypeStruct((rows, hidden), LOW)
    return pl.pallas_call(
        kernel,
        grid=(rows // block,),
        out_shape=(
            low_row, low_broad, low_broad, low_row, low_row, low_row, low_row,
            jax.ShapeDtypeStruct((rows, width), F32),
            jax.ShapeDtypeStruct((8, width), F32),
        ),
        in_specs=[
            row, row, row, whole(w_out.shape), whole(w_ffn.shape), whole(gain.shape),
            whole(shift.shape),
        ],
        out_specs=[
            row, broad, broad, row, row, row, row, row,
            pl.BlockSpec((8, width), lambda b: (0, 0)),
        ],
        scratch_shapes=[pltpu.VMEM((block, hidden), F32)],
        compiler_params=pltpu.CompilerParams(vmem_limit_bytes=50 * MIB),
        cost_estimate=cost(rows * width * (8 * hidden + 4 * width), 24 * MIB, rows * hidden),
    )(normed_one, attn, grad_y, w_out, w_ffn, gain, shift)


def first_norm_back(grad_resid, grad_query, normed_one, rstd_one, w_query, w_out, gain):
    rows, width = grad_resid.shape
    block = min(256, rows)

    def kernel(dr2_ref, dq_ref, n_ref, r_ref, wq_ref, wo_ref, g_ref, dr1_ref, db1_ref, do_ref, sums_ref):
        @pl.when(pl.program_id(0) == 0)
        def _():
            sums_ref[...] = jnp.zeros_like(sums_ref)

        normed = n_ref[...]
        dh1 = dr2_ref[...] + dot_nn(dq_ref[...], wq_ref[...])
        sums_ref[0:1, :] += row_sum(dh1 * normed)
        sums_ref[3:4, :] += row_sum(dh1)
        dr1 = norm_back(dh1, g_ref[0:1, :], normed, r_ref[:, 0:1])
        dr1_ref[...] = dr1
        db1 = dr1.astype(LOW)
        db1_ref[...] = db1
        do_ref[...] = dot_nt(db1, wo_ref[...]).astype(LOW)

    row = pl.BlockSpec((block, width), lambda b: (b, 0))
    thin = pl.BlockSpec((block, 128), lambda b: (b, 0))
    low_row = jax.ShapeDtypeStruct((rows, width), LOW)
    return pl.pallas_call(
        kernel,
        grid=(rows // block,),
        out_shape=(
            jax.ShapeDtypeStruct((rows, width), F32), low_row, low_row,
            jax.ShapeDtypeStruct((8, width), F32),
        ),
        in_specs=[row, row, row, thin, whole(w_query.shape), whole(w_out.shape), whole(gain.shape)],
        out_specs=[row, row, row, pl.BlockSpec((8, width), lambda b: (0, 0))],
        compiler_params=pltpu.CompilerParams(vmem_limit_bytes=40 * MIB),
        cost_estimate=cost(4 * rows * width * width, 8 * MIB),
    )(grad_resid, grad_query, normed_one, rstd_one, w_query, w_out, gain)


def swap(value, axis, bit, size):
    return lax.ppermute(value, axis, [(d, d ^ bit) for d in range(size)])


def ordered(own, other, bit, axis):
    low = jnp.where(bit, other, own)
    high = jnp.where(bit, own, other)
    return jnp.concatenate([low, high], axis)


class Place:
    def __init__(self):
        self.dp = lax.axis_size("dp")
        self.tensor = lax.axis_size("tensor")
        index = lax.axis_index("dp")
        self.z = lax.axis_index("tensor")
        self.core = index & 1
        self.chip = (index >> 1) & 3


def after(value, *deps):
    return lax.optimization_barrier((value, deps))[0]


def beside(always, work, *operands):
    def nothing(*operands):
        return jax.tree.map(lambda leaf: jnp.zeros(leaf.shape, leaf.dtype), jax.eval_shape(work, *operands))

    return lax.optimization_barrier(
        lax.cond(always, work, nothing, *lax.optimization_barrier(operands))
    )


def piece_of(place, shard):
    count, rows, width = shard.shape
    return lax.dynamic_slice(
        shard,
        (0, place.chip * (rows // 4), place.core * (width // 2)),
        (count, rows // 4, width // 2),
    )


def near_pair(piece, far):
    return jnp.stack([piece, far])


def in_slots(near, far):
    return jnp.stack([near[0], far, near[1]])


def from_chips(place, got, *deps):
    others = [swap(got, "dp", 2 * r, place.dp) for r in range(1, 4)]
    if deps:
        others = after(others, *deps)
    return [got, *others]


def assemble(place, shard, mine, theirs):
    count, rows, width = shard.shape
    quarter, half, slots = rows // 4, width // 2, mine.shape[1] + 1

    def kernel(info_ref, shard_ref, mine_ref, theirs_ref, *out_refs):
        def fill(left, right):
            for t, out_ref in enumerate(out_refs):
                out_ref[0] = shard_ref[t]
                for r in range(1, slots):
                    out_ref[r, :, :half] = left[0, r - 1, t]
                    out_ref[r, :, half:] = right[0, r - 1, t]

        @pl.when(info_ref[0] == 0)
        def _():
            fill(mine_ref, theirs_ref)

        @pl.when(info_ref[0] == 1)
        def _():
            fill(theirs_ref, mine_ref)

    def spot(p, info):
        return (p ^ info[1], 0, 0, 0, 0)

    part = pl.BlockSpec((1, slots - 1, count, quarter, half), spot)
    outs = pl.pallas_call(
        kernel,
        out_shape=(jax.ShapeDtypeStruct((slots, rows, width), LOW),) * count,
        grid_spec=pltpu.PrefetchScalarGridSpec(
            num_scalar_prefetch=1,
            grid=(4,),
            in_specs=[pl.BlockSpec((count, quarter, width), lambda p, info: (0, p, 0)), part, part],
            out_specs=[pl.BlockSpec((slots, quarter, width), lambda p, info: (0, p, 0))] * count,
        ),
        compiler_params=pltpu.CompilerParams(vmem_limit_bytes=32 * MIB),
        cost_estimate=cost(0, 4 * count * slots * rows * width),
    )(jnp.stack([place.core, place.chip]).astype(jnp.int32), shard, mine, theirs)
    return [out.reshape(slots * rows, width) for out in outs]


def weight_grads(place, pairs):
    count = len(pairs)
    n, columns = pairs[0][0].shape
    width = pairs[0][1].shape[1]
    half = width // 2
    block = min(768, columns)
    steps = columns // block
    chunk = 256 if block % 256 == 0 else block

    def kernel(info_ref, *refs):
        sides, (keep_ref, give_ref) = refs[: 2 * count], refs[2 * count :]
        keep = pl.multiple_of(info_ref[0] * half, 128)
        give = pl.multiple_of((1 - info_ref[0]) * half, 128)
        for t in range(count):

            @pl.when(pl.program_id(0) // steps == t)
            def _():
                g_ref, a_ref = sides[2 * t], sides[2 * t + 1]
                for start in range(0, block, chunk):
                    at = slice(start, start + chunk)
                    left = g_ref[:, at]
                    keep_ref[0, at, :] = dot_tn(left, a_ref[:, pl.ds(keep, half)]).astype(LOW)
                    give_ref[0, at, :] = dot_tn(left, a_ref[:, pl.ds(give, half)]).astype(LOW)

    def rows_spec(t):
        return pl.BlockSpec(
            (n, block), lambda g, info: (0, jnp.clip(g - t * steps, 0, steps - 1))
        )

    out = pl.BlockSpec((1, block, half), lambda g, info: (g // steps, g % steps, 0))
    in_specs, operands = [], []
    for t, (g, a) in enumerate(pairs):
        in_specs += [rows_spec(t), pl.BlockSpec((n, width), lambda g, info: (0, 0))]
        operands += [g, a]
    return pl.pallas_call(
        kernel,
        out_shape=(jax.ShapeDtypeStruct((count, columns, half), LOW),) * 2,
        grid_spec=pltpu.PrefetchScalarGridSpec(
            num_scalar_prefetch=1,
            grid=(count * steps,),
            in_specs=in_specs,
            out_specs=[out, out],
        ),
        compiler_params=pltpu.CompilerParams(vmem_limit_bytes=48 * MIB),
        cost_estimate=cost(2 * count * n * columns * width, 4 * count * columns * width),
    )(jnp.stack([place.core]).astype(jnp.int32), *operands)


def chip_parts(place, keep, other, groups):
    count, rows, half = keep.shape
    slots = place.tensor
    quarter = rows // slots // 4

    def kernel(info_ref, keep_ref, other_ref, *part_refs):
        for group, part_ref in zip(groups, part_refs, strict=True):
            for at, r in enumerate(group):
                for z in range(slots):
                    start = pl.multiple_of(4 * z * quarter + (info_ref[0] ^ r) * quarter, 16)
                    span = pl.ds(start, quarter)
                    value = keep_ref[0, span, :].astype(F32) + other_ref[0, span, :].astype(F32)
                    part_ref[at, z] = value.astype(LOW)

    row = pl.BlockSpec((1, rows, half), lambda t, info: (t, 0, 0))
    return pl.pallas_call(
        kernel,
        out_shape=[
            jax.ShapeDtypeStruct((count * len(group), slots, quarter, half), LOW) for group in groups
        ],
        grid_spec=pltpu.PrefetchScalarGridSpec(
            num_scalar_prefetch=1,
            grid=(count,),
            in_specs=[row, row],
            out_specs=[
                pl.BlockSpec((len(group), slots, quarter, half), lambda t, info: (t, 0, 0, 0))
                for group in groups
            ],
        ),
        compiler_params=pltpu.CompilerParams(vmem_limit_bytes=32 * MIB),
        cost_estimate=cost(0, 6 * count * rows * half),
    )(jnp.stack([place.chip]).astype(jnp.int32), keep, other)


EACH = ((0,), (1,), (2,), (3,))


def input_grad(resid, halves, weights):
    rows, width = resid.shape
    block = min(256, rows)
    half = width // 2

    def kernel(r_ref, *refs):
        out_ref = refs[-1]
        total = r_ref[...]
        for t in range(len(weights)):
            for side in range(2):
                w = refs[len(halves) + t][side * half : (side + 1) * half, :]
                total = total + dot_nn(refs[2 * t + side][...], w)
        out_ref[...] = total.astype(LOW)

    row = pl.BlockSpec((block, width), lambda b: (b, 0))
    return pl.pallas_call(
        kernel,
        grid=(rows // block,),
        out_shape=jax.ShapeDtypeStruct((rows, width), LOW),
        in_specs=[row]
        + [pl.BlockSpec((block, half), lambda b: (b, 0))] * len(halves)
        + [whole((width, width))] * len(weights),
        out_specs=row,
        compiler_params=pltpu.CompilerParams(vmem_limit_bytes=40 * MIB),
        cost_estimate=cost(2 * len(weights) * rows * width * width, 8 * MIB),
    )(resid, *halves, *weights)


def swap_chips(place, parts):
    return [swap(parts[r], "dp", 2 * r, place.dp) for r in range(1, 4)]


def add_all(own, others):
    own = own.astype(F32)
    for other in others:
        own = own + other.astype(F32)
    return own


def near_parts(place, total, natural):
    def slot(r):
        if natural:
            return lax.dynamic_index_in_dim(total, place.z ^ r, 1, False)
        return total[:, r]

    stay, leave = jnp.stack([slot(0), slot(2)]), jnp.stack([slot(1), slot(3)])
    return stay, leave.astype(LOW)


def add_far(place, total, other):
    piece = total[0] + other.astype(F32)
    bit = 8
    while bit < place.dp:
        piece = piece + swap(piece.astype(LOW), "dp", bit, place.dp).astype(F32)
        bit *= 2
    return piece.astype(LOW)


def regather(place, piece, *deps):
    own = jnp.stack(from_chips(place, piece, *deps))
    return own, swap(own, "dp", 1, place.dp)


def finish(place, own, other, groups):
    _, count, quarter, half = own.shape
    rows, width = 4 * quarter, 2 * half

    def kernel(info_ref, own_ref, other_ref, *out_refs):
        core, chip = info_ref[0], info_ref[1]
        t = 0
        for group, out_ref in zip(groups, out_refs, strict=True):
            for g in range(group):
                for p in range(4):
                    at = slice(p * quarter, (p + 1) * quarter)
                    mine, theirs = own_ref[p ^ chip, t].astype(F32), other_ref[p ^ chip, t].astype(F32)
                    out_ref[g, at, :half] = jnp.where(core == 0, mine, theirs)
                    out_ref[g, at, half:] = jnp.where(core == 0, theirs, mine)
                t += 1

    shapes = [(group, rows, width) for group in groups]
    return pl.pallas_call(
        kernel,
        out_shape=[jax.ShapeDtypeStruct(shape, F32) for shape in shapes],
        grid_spec=pltpu.PrefetchScalarGridSpec(
            num_scalar_prefetch=1,
            grid=(1,),
            in_specs=[whole(own.shape), whole(own.shape)],
            out_specs=[whole(shape) for shape in shapes],
        ),
        compiler_params=pltpu.CompilerParams(vmem_limit_bytes=48 * MIB),
        cost_estimate=cost(0, 6 * count * rows * width),
    )(jnp.stack([place.core, place.chip]).astype(jnp.int32), own, other)


def finish_ffn(parts):
    _, _, quarter, half = parts.shape
    rows, width = 4 * quarter, 2 * half

    def kernel(parts_ref, down_ref, up_ref):
        for side in range(2):
            columns = slice(side * half, (side + 1) * half)
            for q in range(4):
                at = slice(q * quarter, (q + 1) * quarter)
                down_ref[at, columns] = parts_ref[2 * q + side, 0].astype(F32)
            full = jnp.concatenate([parts_ref[2 * q + side, 1] for q in range(4)], 0)
            up_ref[columns, :] = full.astype(F32).T

    return pl.pallas_call(
        kernel,
        out_shape=(jax.ShapeDtypeStruct((rows, width), F32), jax.ShapeDtypeStruct((width, rows), F32)),
        compiler_params=pltpu.CompilerParams(vmem_limit_bytes=32 * MIB),
        cost_estimate=cost(0, 12 * rows * width),
    )(parts)


def local(
    inputs, memory, cotangent, dec_len, mem_len,
    self_qkv, self_out, cross_q, cross_kv, cross_out, ffn_in, ffn_out, ln_gain, ln_bias,
):
    place = Place()
    dp, slots = place.dp, place.tensor
    axes = ("dp", "tensor")
    width = inputs.shape[3]
    length = inputs.shape[2]
    block = length // slots
    micro = place.z // 2
    owner = place.core == (place.z & 1)
    fetch_perm = [
        (d * slots + t, (d ^ 1) * slots + t)
        for d in range(dp)
        for t in range(slots)
        if d % 2 == t % 2
    ]
    spread = []
    for call in range(2):
        spread.append(
            [
                ((g + hh) * slots + s, (g + s % 2) * slots + OWN_BLOCKS[hh][(call + s // 2) % 2])
                for g in range(0, dp, 2)
                for s in range(slots)
                for hh in range(2)
            ]
        )
    collect = [[(dst, src) for src, dst in perm] for perm in spread]

    def fetch(value):
        mine = lax.dynamic_index_in_dim(value, micro, 0, False)[0]
        return jnp.where(owner, mine, lax.ppermute(mine, axes, fetch_perm))

    def own_rows(value):
        return jnp.concatenate(
            [
                lax.dynamic_slice_in_dim(value, place.core * block, block, 0),
                lax.dynamic_slice_in_dim(value, (3 - place.core) * block, block, 0),
            ],
            0,
        )

    def start_rows(value):
        return [
            lax.ppermute(
                lax.dynamic_slice_in_dim(value, ((call + micro) % 2) * block, block, 0), axes, spread[call]
            )
            for call in range(2)
        ]

    def end_rows(got):
        near = place.z // 2 == 0
        return jnp.stack([jnp.where(near, got[0], got[1]), jnp.where(near, got[1], got[0])])[:, None]

    def collect_rows(value):
        return [
            lax.ppermute(
                lax.dynamic_index_in_dim(value, (place.z // 2 + call) % 2, 0, False)[0], axes, collect[call]
            )
            for call in range(2)
        ]


    def flat(weights):
        return weights.reshape(-1, width)

    index = lax.axis_index("dp")
    at_ffn = ffn_out.shape[0] // dp
    piece_ffn = jnp.stack(
        [
            lax.dynamic_slice_in_dim(ffn_in, index * at_ffn, at_ffn, 1).T,
            lax.dynamic_slice_in_dim(ffn_out, index * at_ffn, at_ffn, 0),
        ]
    )
    shard_qkv = jnp.swapaxes(self_qkv, 1, 2)
    shard_mid = jnp.concatenate(
        [self_out[None], cross_q.T[None], jnp.swapaxes(cross_kv, 1, 2), cross_out[None]], 0
    )
    always = dec_len[0, 0] > 0
    pieces = jnp.concatenate([piece_of(place, shard_qkv), piece_of(place, shard_mid)], 0)
    lengths = jnp.stack([dec_len, mem_len], -1)

    def first_fetch(pieces, *values):
        far = swap(pieces, "tensor", 2, slots)
        x_all, mem_all, lens = (fetch(value) for value in values)
        return far, x_all, mem_all, own_rows(x_all), own_rows(mem_all), lens

    far, x_all, mem_all, x_own, mem_own, lens = beside(
        always, first_fetch, after(pieces, piece_ffn), inputs, memory, lengths
    )
    core = place.core.astype(jnp.int32)
    info_self = jnp.stack([core, lens[0]])
    info_cross = jnp.stack([core, lens[1]])
    got = in_slots(swap(near_pair(pieces, far), "tensor", 1, slots), far)
    w_ffn = lax.all_gather(after(piece_ffn, got), ("tensor", "dp"), axis=0)
    got_qkv = jnp.stack(from_chips(place, got[:, :3]))
    wq, wk, wv = assemble(place, shard_qkv, got_qkv, swap(got_qkv, "dp", 1, dp))

    def self_forward(got, rows, x_own, x_all, wq, wk, wv, info):
        query = dot_nt(x_own, wq).astype(LOW)
        key = dot_nt(x_all, wk).astype(LOW)
        value = dot_nt(x_all, wv).astype(LOW)
        return (
            swap_chips(place, [got] * 4),
            collect_rows(rows),
            (query, key, value),
            attend_forward(True, info, query, key, value),
        )

    others, got_y, (query_s, key_s, value_s), (attn_s, logs_s) = beside(
        always, self_forward, got[:, 3:], cotangent, x_own, x_all, wq, wk, wv, info_self
    )
    got_mid = jnp.stack([got[:, 3:], *others])
    w_so, w_cq, w_ck, w_cv, w_co = assemble(
        place, shard_mid, got_mid, swap(got_mid, "dp", 1, dp)
    )
    grad_y = jnp.concatenate(
        [jnp.where(micro == 0, got_y[0], got_y[1]), jnp.where(micro == 0, got_y[1], got_y[0])], 0
    )
    normed_one, rstd_one, h1_low, query_c = first_norm(
        attn_s, x_own, w_so, w_cq, ln_gain, ln_bias
    )
    key_c = dot_nt(mem_all, w_ck).astype(LOW)
    value_c = dot_nt(mem_all, w_cv).astype(LOW)
    attn_c, logs_c = attend_forward(False, info_cross, query_c, key_c, value_c)
    (out_rows, act, grad_pre, grad_b3, h2_low, grad_b2, grad_oc, grad_r2, sums_late) = middle(
        normed_one, attn_c, grad_y, w_co, w_ffn, ln_gain, ln_bias
    )

    keep_down, give_down = weight_grads(place, [(act, grad_b3)])

    def up_grads(give, *pair):
        return swap(give, "dp", 1, dp), weight_grads(place, [pair])

    other_down, (keep_up, give_up) = beside(always, up_grads, give_down, grad_pre, h2_low)
    other_up = swap(give_up, "dp", 1, dp)
    own_down, on_down, first_down = chip_parts(place, keep_down, other_down, ((0,), (2,), (1, 3)))
    own_up, on_up, first_up = chip_parts(place, keep_up, other_up, ((0,), (1,), (2, 3)))

    def cross_back(first_down, first_up, rows, *operands):
        return (
            swap(first_down, "dp", 2, dp),
            swap(first_up, "dp", 4, dp),
            start_rows(rows),
            attend_backward(False, (0, 1), *operands),
        )

    from_down, from_up, got_out, (dq_c, dk_c, dv_c, give_c) = beside(
        always, cross_back, first_down, first_up, out_rows,
        info_cross, query_c, key_c, value_c, attn_c, logs_c, grad_oc,
    )

    def in_chip(own, other):
        return (own.astype(F32) + other.astype(F32)).astype(LOW)

    other_c = swap(give_c, "dp", 1, dp)
    dk_c, dv_c = in_chip(dk_c, other_c[0]), in_chip(dv_c, other_c[1])
    grad_r1, grad_b1, grad_os, sums_first = first_norm_back(
        grad_r2, dq_c, normed_one, rstd_one, w_cq, w_so, ln_gain
    )
    d_mem = (dot_nn(dk_c, w_ck) + dot_nn(dv_c, w_cv)).astype(LOW)

    def mid_grads(down, up, rows, *sides):
        return (
            swap(down, "dp", 4, dp),
            swap(up, "dp", 2, dp),
            start_rows(rows),
            weight_grads(place, [(sides[2 * t], sides[2 * t + 1]) for t in range(5)]),
        )

    on_down, on_up = in_chip(on_down[0], from_down[1]), in_chip(on_up[0], from_up[1])
    last_down, last_up, got_mem, (keep_mid, give_mid) = beside(
        always, mid_grads, on_down, on_up, d_mem,
        attn_s, grad_b1, dq_c, h1_low, dk_c, mem_own, dv_c, mem_own, attn_c, grad_b2,
    )
    total_ffn = jnp.stack(
        [
            add_all(own_down[0], [from_down[0], last_down]),
            add_all(own_up[0], [from_up[0], last_up]),
        ]
    )
    near_ffn = near_parts(place, total_ffn, True)
    parts_mid = chip_parts(place, keep_mid, swap(give_mid, "dp", 1, dp), EACH)
    sums = sums_late + sums_first
    back_operands = (info_self, query_s, key_s, value_s, attn_s, logs_s, grad_os)

    def self_back_first(part_x, part_y, sums, leave, *operands):
        return (
            swap(part_x, "dp", 2, dp),
            swap(part_y, "dp", 4, dp),
            swap(sums, "dp", 2, dp),
            swap(leave, "tensor", 1, slots),
            attend_backward(True, (0, 2), *operands),
        )

    def self_back_second(part_xy, sums, leave, give, *operands):
        return (
            swap(part_xy, "dp", 6, dp),
            swap(sums, "dp", 4, dp),
            swap(leave, "tensor", 2, slots),
            swap(give, "dp", 1, dp),
            attend_backward(True, (1, 2), *operands),
        )

    from_x, from_y, other_sums, other_ffn, (dq_a, dk_a, dv_a, give_a) = beside(
        always, self_back_first, parts_mid[1], parts_mid[2], sums, near_ffn[1], *back_operands
    )
    sums = sums + other_sums
    far_ffn = near_ffn[0] + other_ffn.astype(F32)
    from_xy, other_sums, other_ffn, other_a, (dq_b, dk_b, dv_b, give_b) = beside(
        always, self_back_second, parts_mid[3], sums, far_ffn[1].astype(LOW), give_a, *back_operands
    )
    sums = sums + other_sums
    piece_ffn = add_far(place, far_ffn, other_ffn)
    other_b = swap(give_b, "dp", 1, dp)
    halves = (
        dq_a, dq_b, in_chip(dk_a, other_a[0]), in_chip(dk_b, other_b[0]),
        in_chip(dv_a, other_a[1]), in_chip(dv_b, other_b[1]),
    )
    keep_qkv, give_qkv = weight_grads(place, [(side, x_own) for side in halves])
    keep_qkv, give_qkv = (grad.reshape(3, width, -1) for grad in (keep_qkv, give_qkv))
    total_mid = add_all(parts_mid[0], [from_x, from_y, from_xy])
    near_mid = near_parts(place, total_mid, False)

    def input_grads(give, leave, sums, resid, *operands):
        return (
            swap(give, "dp", 1, dp),
            swap(leave, "tensor", 1, slots),
            swap(sums, "dp", 1, dp),
            input_grad(resid, operands[:6], operands[6:]),
        )

    other_qkv, other, other_sums, d_x = beside(
        always, input_grads, give_qkv, near_mid[1], sums, grad_r1, *halves, wq, wk, wv
    )
    sums = sums + other_sums
    bit = 8
    while bit < dp:
        sums = sums + swap(sums, "dp", bit, dp)
        bit *= 2
    far_mid = near_mid[0] + other.astype(F32)
    parts_qkv = chip_parts(place, keep_qkv, other_qkv, EACH)

    def send_qkv(parts, rows, leave):
        return (
            swap_chips(place, [None, *parts]),
            start_rows(rows),
            swap(leave, "tensor", 2, slots),
        )

    others_qkv, got_x, other = beside(
        always, send_qkv, parts_qkv[1:], d_x, far_mid[1].astype(LOW)
    )
    piece_mid = add_far(place, far_mid, other)
    near = near_parts(place, add_all(parts_qkv[0], others_qkv), False)
    d_x = end_rows(got_x).astype(F32)
    d_mem = end_rows(after(got_mem, others_qkv)).astype(F32)
    out = end_rows(after(got_out, others_qkv))
    other, other_sums = after(
        (swap(near[1], "tensor", 1, slots), swap(sums, "tensor", 1, slots)), d_x, d_mem
    )
    sums = sums + other_sums
    far = near[0] + other.astype(F32)
    other, other_sums = after(
        (swap(far[1].astype(LOW), "tensor", 2, slots), swap(sums, "tensor", 2, slots)), out
    )
    sums = sums + other_sums
    piece = jnp.concatenate([add_far(place, far, other), piece_mid], 0)
    groups = [[first + d for d in range(8)] for first in range(0, dp, 8)]
    d_down, d_up = finish_ffn(lax.all_gather(piece_ffn, "dp", axis=0, axis_index_groups=groups))
    own, other = regather(place, piece, d_down, d_up)
    d_qkv, d_so, d_cq, d_ckv, d_co = finish(place, own, other, (3, 1, 1, 2, 1))
    return (
        out,
        d_x,
        d_mem,
        jnp.swapaxes(d_qkv, 1, 2),
        d_so[0],
        d_cq[0].T,
        jnp.swapaxes(d_ckv, 1, 2),
        d_co[0],
        d_up,
        d_down,
        sums[0:3],
        sums[3:6],
    )


def solution(mesh):
    rows = P(None, "dp", "tensor", None)
    in_specs = (
        P(None, "dp", None, None),
        P(None, "dp", None, None),
        rows,
        P(None, "dp"),
        P(None, "dp"),
        P(None, None, "tensor"),
        P("tensor", None),
        P(None, "tensor"),
        P(None, None, "tensor"),
        P("tensor", None),
        P(None, "tensor"),
        P("tensor", None),
        P(),
        P(),
    )
    out_specs = (
        rows,
        rows,
        rows,
        P(None, None, "tensor"),
        P("tensor", None),
        P(None, "tensor"),
        P(None, None, "tensor"),
        P("tensor", None),
        P(None, "tensor"),
        P("tensor", None),
        P(),
        P(),
    )
    return jax.shard_map(local, mesh=mesh, in_specs=in_specs, out_specs=out_specs, check_vma=False)
```

```python
import functools

import jax
import jax.numpy as jnp
from jax import lax
from jax.experimental import pallas as pl
from jax.experimental.pallas import tpu as pltpu
from jax.sharding import PartitionSpec as P

HEAD = 64
EPS = 1e-05
NEG = -1e30
LOW = jnp.bfloat16
F32 = jnp.float32
OWN_BLOCKS = ((0, 3), (1, 2))
MIB = 1024 * 1024


def dot_nn(left, right):
    return lax.dot_general(left, right, (((1,), (0,)), ((), ())), preferred_element_type=F32)


def dot_nt(left, right):
    return lax.dot_general(left, right, (((1,), (1,)), ((), ())), preferred_element_type=F32)


def dot_tn(left, right):
    return lax.dot_general(left, right, (((0,), (0,)), ((), ())), preferred_element_type=F32)


def cost(flops, size, trans=0):
    return pl.CostEstimate(flops=int(flops), bytes_accessed=int(size), transcendentals=int(trans))


def whole(shape):
    return pl.BlockSpec(shape, lambda *_: (0,) * len(shape), pipeline_mode=pl.Buffered(1))


def attend_forward(causal, info, query, keys_in, values_in):
    rows, width = query.shape
    key_rows = keys_in.shape[0]
    block = rows // 2
    pair = 2 * HEAD

    def kernel(info_ref, q_ref, k_ref, v_ref, o_ref, lse_ref):
        length = info_ref[1]

        def part(spot, block_id, extent):
            lane = lax.broadcasted_iota(jnp.int32, (block, pair), 1)
            limit = jnp.full((block, 1), length, jnp.int32)
            if causal:
                row = block_id * block + lax.broadcasted_iota(jnp.int32, (block, 1), 0)
                limit = jnp.minimum(limit, row + 1)
            allowed = lax.broadcasted_iota(jnp.int32, (block, extent), 1) < limit
            span = pl.ds(spot * block, block)
            q = q_ref[span, :]
            out, logs = None, None
            for side in range(2):
                mine = (lane >= HEAD) if side else (lane < HEAD)
                q_side = jnp.where(mine, q, 0).astype(LOW) * LOW(HEAD ** (-0.5))
                scores = jnp.where(allowed, dot_nt(q_side, k_ref[:extent, :]), NEG)
                peak = jnp.max(scores, -1, keepdims=True)
                weights = jnp.exp(scores - peak)
                total = jnp.sum(weights, -1, keepdims=True)
                mixed = dot_nn(weights.astype(LOW), v_ref[:extent, :]) / total
                log_total = peak + jnp.log(total)
                if side:
                    out = jnp.where(mine, mixed, out)
                    logs = jnp.where(mine, log_total, logs)
                else:
                    out, logs = mixed, jnp.broadcast_to(log_total, (block, pair))
            o_ref[span, :] = out.astype(LOW)
            lse_ref[span, :] = logs

        if causal:
            for variant in range(2):

                @pl.when(info_ref[0] == variant)
                def _():
                    for spot in range(2):
                        block_id = OWN_BLOCKS[variant][spot]
                        part(spot, block_id, (block_id + 1) * block)
        else:
            for spot in range(2):
                part(spot, 0, key_rows)

    column = pl.BlockSpec((rows, pair), lambda p, *_: (0, p))
    key_column = pl.BlockSpec((key_rows, pair), lambda p, *_: (0, p))
    share = 0.625 if causal else 1.0
    elements = width // HEAD * rows * key_rows * share
    return pl.pallas_call(
        kernel,
        out_shape=(
            jax.ShapeDtypeStruct((rows, width), LOW),
            jax.ShapeDtypeStruct((rows, width), F32),
        ),
        grid_spec=pltpu.PrefetchScalarGridSpec(
            num_scalar_prefetch=1,
            grid=(width // pair,),
            in_specs=[column, key_column, key_column],
            out_specs=[column, column],
        ),
        compiler_params=pltpu.CompilerParams(vmem_limit_bytes=48 * MIB),
        cost_estimate=cost(elements * 1024, 10 * MIB, elements),
    )(info, query, keys_in, values_in)


def attend_backward(causal, share_of, info, query, keys_in, values_in, out, logs, grad_out):
    rows, width = query.shape[0], query.shape[1] // share_of[1]
    skip = share_of[0] * width // (2 * HEAD)
    key_rows = keys_in.shape[0]
    block = rows // 2
    pair = 2 * HEAD

    def kernel(
        info_ref, q_ref, k_ref, v_ref, o_ref, lse_ref, g_ref,
        dq_ref, dk_ref, dv_ref, give_ref, dk_acc, dv_acc,
    ):
        length = info_ref[1]
        dk_acc[...] = jnp.zeros_like(dk_acc)
        dv_acc[...] = jnp.zeros_like(dv_acc)

        def part(spot, block_id, extent):
            lane = lax.broadcasted_iota(jnp.int32, (block, pair), 1)
            limit = jnp.full((block, 1), length, jnp.int32)
            if causal:
                row = block_id * block + lax.broadcasted_iota(jnp.int32, (block, 1), 0)
                limit = jnp.minimum(limit, row + 1)
            allowed = lax.broadcasted_iota(jnp.int32, (block, extent), 1) < limit
            span = pl.ds(spot * block, block)
            q = q_ref[span, :]
            g = g_ref[span, :]
            along = g.astype(F32) * o_ref[span, :].astype(F32)
            dq = None
            for side in range(2):
                mine = (lane >= HEAD) if side else (lane < HEAD)
                q_side = jnp.where(mine, q, 0).astype(LOW) * LOW(HEAD ** (-0.5))
                g_side = jnp.where(mine, g, 0).astype(LOW)
                inner = jnp.sum(jnp.where(mine, along, 0.0), -1, keepdims=True)
                log_total = lse_ref[span, side * HEAD : side * HEAD + 1]
                scores = jnp.where(allowed, dot_nt(q_side, k_ref[:extent, :]), NEG)
                weights = jnp.exp(scores - log_total)
                dv_acc[:extent, :] += dot_tn(weights.astype(LOW), g_side)
                grad_w = dot_nt(g_side, v_ref[:extent, :])
                grad_s = (weights * (grad_w - inner)).astype(LOW)
                dk_acc[:extent, :] += dot_tn(grad_s, q_side)
                part_q = dot_nn(grad_s, k_ref[:extent, :])
                dq = jnp.where(mine, part_q, dq) if side else part_q
            dq_ref[span, :] = (dq * HEAD ** (-0.5)).astype(LOW)

        for variant in range(2):

            @pl.when(info_ref[0] == variant)
            def _():
                for spot in range(2):
                    block_id = OWN_BLOCKS[variant][spot]
                    part(spot, block_id, (block_id + 1) * block if causal else key_rows)
                for spot in range(2):
                    keep = slice(OWN_BLOCKS[variant][spot] * block, (OWN_BLOCKS[variant][spot] + 1) * block)
                    give = slice(OWN_BLOCKS[1 - variant][spot] * block, (OWN_BLOCKS[1 - variant][spot] + 1) * block)
                    span = slice(spot * block, (spot + 1) * block)
                    dk_ref[span, :] = dk_acc[keep, :].astype(LOW)
                    dv_ref[span, :] = dv_acc[keep, :].astype(LOW)
                    give_ref[0, span, :] = dk_acc[give, :].astype(LOW)
                    give_ref[1, span, :] = dv_acc[give, :].astype(LOW)

    column = pl.BlockSpec((rows, pair), lambda p, *_: (0, p + skip))
    key_column = pl.BlockSpec((key_rows, pair), lambda p, *_: (0, p + skip))
    single = pl.BlockSpec((rows, pair), lambda p, *_: (0, p))
    double = pl.BlockSpec((2, rows, pair), lambda p, *_: (0, 0, p))
    share = 0.625 if causal else 1.0
    elements = width // HEAD * rows * key_rows * share
    return pl.pallas_call(
        kernel,
        out_shape=(jax.ShapeDtypeStruct((rows, width), LOW),) * 3
        + (jax.ShapeDtypeStruct((2, rows, width), LOW),),
        grid_spec=pltpu.PrefetchScalarGridSpec(
            num_scalar_prefetch=1,
            grid=(width // pair,),
            in_specs=[column, key_column, key_column, column, column, column],
            out_specs=[single, single, single, double],
            scratch_shapes=[pltpu.VMEM((key_rows, pair), F32), pltpu.VMEM((key_rows, pair), F32)],
        ),
        compiler_params=pltpu.CompilerParams(vmem_limit_bytes=48 * MIB),
        cost_estimate=cost(elements * 2560, 10 * MIB, elements),
    )(info, query, keys_in, values_in, out, logs, grad_out)


def normalize(resid):
    center = resid - jnp.mean(resid, -1, keepdims=True)
    rstd = lax.rsqrt(jnp.mean(center * center, -1, keepdims=True) + EPS)
    return center * rstd, rstd


def norm_back(grad, gain, normed, rstd):
    dn = grad * gain
    mean_dn = jnp.mean(dn, -1, keepdims=True)
    mean_dnn = jnp.mean(dn * normed, -1, keepdims=True)
    return rstd * (dn - mean_dn - normed * mean_dnn)


def row_sum(value):
    return jnp.sum(value, 0, keepdims=True)


def first_norm(attn, x_rows, w_out, w_query, gain, shift):
    rows, width = attn.shape
    block = min(256, rows)

    def kernel(o_ref, x_ref, wo_ref, wq_ref, g_ref, s_ref, n_ref, r_ref, h_ref, q_ref):
        normed, rstd = normalize(x_ref[...].astype(F32) + dot_nn(o_ref[...], wo_ref[...]))
        n_ref[...] = normed
        r_ref[...] = jnp.broadcast_to(rstd, r_ref.shape)
        low = (normed * g_ref[0:1, :] + s_ref[0:1, :]).astype(LOW)
        h_ref[...] = low
        q_ref[...] = dot_nt(low, wq_ref[...]).astype(LOW)

    row = pl.BlockSpec((block, width), lambda b: (b, 0))
    thin = pl.BlockSpec((block, 128), lambda b: (b, 0))
    return pl.pallas_call(
        kernel,
        grid=(rows // block,),
        out_shape=(
            jax.ShapeDtypeStruct((rows, width), F32),
            jax.ShapeDtypeStruct((rows, 128), F32),
            jax.ShapeDtypeStruct((rows, width), LOW),
            jax.ShapeDtypeStruct((rows, width), LOW),
        ),
        in_specs=[row, row, whole(w_out.shape), whole(w_query.shape), whole(gain.shape), whole(shift.shape)],
        out_specs=[row, thin, row, row],
        compiler_params=pltpu.CompilerParams(vmem_limit_bytes=40 * MIB),
        cost_estimate=cost(4 * rows * width * width, 8 * MIB),
    )(attn, x_rows, w_out, w_query, gain, shift)


def gelu_parts(u):
    t = 1.0 / (1.0 + (0.3275911 * 0.7071067811865476) * jnp.abs(u))
    bell = jnp.exp(-0.5 * u * u)
    poly = t * (0.254829592 + t * (-0.284496736 + t * (1.421413741 + t * (-1.453152027 + t * 1.061405429))))
    tail = 0.5 * poly * bell
    return jnp.where(u < 0, tail, 1.0 - tail), bell * 0.3989422804014327


def middle(normed_one, attn, grad_y, w_out, w_ffn, gain, shift):
    rows, width = attn.shape
    parts, _, part, _ = w_ffn.shape
    hidden = parts * part
    block = min(256, rows)
    step = min(768, hidden)

    def kernel(
        n0_ref, o_ref, y_ref, wo_ref, w_ref, g_ref, s_ref,
        out_ref, a_ref, du_ref, db3_ref, h2_ref, db2_ref, do_ref, dr2_ref, sums_ref, slope_ref,
    ):
        @pl.when(pl.program_id(0) == 0)
        def _():
            sums_ref[...] = jnp.zeros_like(sums_ref)

        def weight(which, start):
            return w_ref[start // part : (start + step) // part, which].reshape(step, width)

        h1 = n0_ref[...] * g_ref[0:1, :] + s_ref[0:1, :]
        n1, rstd1 = normalize(h1 + dot_nn(o_ref[...], wo_ref[...]))
        h2 = n1 * g_ref[1:2, :] + s_ref[1:2, :]
        h2_low = h2.astype(LOW)
        h2_ref[...] = h2_low
        branch = None
        for start in range(0, hidden, step):
            span = slice(start, start + step)
            u = dot_nt(h2_low, weight(0, start))
            share, density = gelu_parts(u)
            slope_ref[:, span] = share + u * density
            a = (u * share).astype(LOW)
            a_ref[:, span] = a
            term = dot_nn(a, weight(1, start))
            branch = term if branch is None else branch + term
        n2, rstd2 = normalize(h2 + branch)
        out_ref[...] = (n2 * g_ref[2:3, :] + s_ref[2:3, :]).astype(LOW)
        g = y_ref[...].astype(F32)
        sums_ref[2:3, :] += row_sum(g * n2)
        sums_ref[5:6, :] += row_sum(g)
        dr3 = norm_back(g, g_ref[2:3, :], n2, rstd2)
        db3 = dr3.astype(LOW)
        db3_ref[...] = db3
        dh2 = dr3
        for start in range(0, hidden, step):
            span = slice(start, start + step)
            du = (dot_nt(db3, weight(1, start)) * slope_ref[:, span]).astype(LOW)
            du_ref[:, span] = du
            dh2 = dh2 + dot_nn(du, weight(0, start))
        sums_ref[1:2, :] += row_sum(dh2 * n1)
        sums_ref[4:5, :] += row_sum(dh2)
        dr2 = norm_back(dh2, g_ref[1:2, :], n1, rstd1)
        dr2_ref[...] = dr2
        db2 = dr2.astype(LOW)
        db2_ref[...] = db2
        do_ref[...] = dot_nt(db2, wo_ref[...]).astype(LOW)

    row = pl.BlockSpec((block, width), lambda b: (b, 0))
    broad = pl.BlockSpec((block, hidden), lambda b: (b, 0))
    low_row = jax.ShapeDtypeStruct((rows, width), LOW)
    low_broad = jax.ShapeDtypeStruct((rows, hidden), LOW)
    return pl.pallas_call(
        kernel,
        grid=(rows // block,),
        out_shape=(
            low_row, low_broad, low_broad, low_row, low_row, low_row, low_row,
            jax.ShapeDtypeStruct((rows, width), F32),
            jax.ShapeDtypeStruct((8, width), F32),
        ),
        in_specs=[
            row, row, row, whole(w_out.shape), whole(w_ffn.shape), whole(gain.shape),
            whole(shift.shape),
        ],
        out_specs=[
            row, broad, broad, row, row, row, row, row,
            pl.BlockSpec((8, width), lambda b: (0, 0)),
        ],
        scratch_shapes=[pltpu.VMEM((block, hidden), F32)],
        compiler_params=pltpu.CompilerParams(vmem_limit_bytes=50 * MIB),
        cost_estimate=cost(rows * width * (8 * hidden + 4 * width), 24 * MIB, rows * hidden),
    )(normed_one, attn, grad_y, w_out, w_ffn, gain, shift)


def first_norm_back(grad_resid, grad_query, normed_one, rstd_one, w_query, w_out, gain):
    rows, width = grad_resid.shape
    block = min(256, rows)

    def kernel(dr2_ref, dq_ref, n_ref, r_ref, wq_ref, wo_ref, g_ref, dr1_ref, db1_ref, do_ref, sums_ref):
        @pl.when(pl.program_id(0) == 0)
        def _():
            sums_ref[...] = jnp.zeros_like(sums_ref)

        normed = n_ref[...]
        dh1 = dr2_ref[...] + dot_nn(dq_ref[...], wq_ref[...])
        sums_ref[0:1, :] += row_sum(dh1 * normed)
        sums_ref[3:4, :] += row_sum(dh1)
        dr1 = norm_back(dh1, g_ref[0:1, :], normed, r_ref[:, 0:1])
        dr1_ref[...] = dr1
        db1 = dr1.astype(LOW)
        db1_ref[...] = db1
        do_ref[...] = dot_nt(db1, wo_ref[...]).astype(LOW)

    row = pl.BlockSpec((block, width), lambda b: (b, 0))
    thin = pl.BlockSpec((block, 128), lambda b: (b, 0))
    low_row = jax.ShapeDtypeStruct((rows, width), LOW)
    return pl.pallas_call(
        kernel,
        grid=(rows // block,),
        out_shape=(
            jax.ShapeDtypeStruct((rows, width), F32), low_row, low_row,
            jax.ShapeDtypeStruct((8, width), F32),
        ),
        in_specs=[row, row, row, thin, whole(w_query.shape), whole(w_out.shape), whole(gain.shape)],
        out_specs=[row, row, row, pl.BlockSpec((8, width), lambda b: (0, 0))],
        compiler_params=pltpu.CompilerParams(vmem_limit_bytes=40 * MIB),
        cost_estimate=cost(4 * rows * width * width, 8 * MIB),
    )(grad_resid, grad_query, normed_one, rstd_one, w_query, w_out, gain)


def swap(value, axis, bit, size):
    return lax.ppermute(value, axis, [(d, d ^ bit) for d in range(size)])


def ordered(own, other, bit, axis):
    low = jnp.where(bit, other, own)
    high = jnp.where(bit, own, other)
    return jnp.concatenate([low, high], axis)


class Place:
    def __init__(self):
        self.dp = lax.axis_size("dp")
        self.tensor = lax.axis_size("tensor")
        index = lax.axis_index("dp")
        self.z = lax.axis_index("tensor")
        self.core = index & 1
        self.chip = (index >> 1) & 3


def after(value, *deps):
    return lax.optimization_barrier((value, deps))[0]


def beside(always, work, *operands):
    def nothing(*operands):
        return jax.tree.map(lambda leaf: jnp.zeros(leaf.shape, leaf.dtype), jax.eval_shape(work, *operands))

    return lax.optimization_barrier(
        lax.cond(always, work, nothing, *lax.optimization_barrier(operands))
    )


def piece_of(place, shard):
    count, rows, width = shard.shape
    return lax.dynamic_slice(
        shard,
        (0, place.chip * (rows // 4), place.core * (width // 2)),
        (count, rows // 4, width // 2),
    )


def near_pair(piece, far):
    return jnp.stack([piece, far])


def in_slots(near, far):
    return jnp.stack([near[0], far, near[1]])


def from_chips(place, got, *deps):
    others = [swap(got, "dp", 2 * r, place.dp) for r in range(1, 4)]
    if deps:
        others = after(others, *deps)
    return [got, *others]


def assemble(place, shard, mine, theirs):
    count, rows, width = shard.shape
    quarter, half, slots = rows // 4, width // 2, mine.shape[1] + 1

    def kernel(info_ref, shard_ref, mine_ref, theirs_ref, *out_refs):
        def fill(left, right):
            for t, out_ref in enumerate(out_refs):
                out_ref[0] = shard_ref[t]
                for r in range(1, slots):
                    out_ref[r, :, :half] = left[0, r - 1, t]
                    out_ref[r, :, half:] = right[0, r - 1, t]

        @pl.when(info_ref[0] == 0)
        def _():
            fill(mine_ref, theirs_ref)

        @pl.when(info_ref[0] == 1)
        def _():
            fill(theirs_ref, mine_ref)

    def spot(p, info):
        return (p ^ info[1], 0, 0, 0, 0)

    part = pl.BlockSpec((1, slots - 1, count, quarter, half), spot)
    outs = pl.pallas_call(
        kernel,
        out_shape=(jax.ShapeDtypeStruct((slots, rows, width), LOW),) * count,
        grid_spec=pltpu.PrefetchScalarGridSpec(
            num_scalar_prefetch=1,
            grid=(4,),
            in_specs=[pl.BlockSpec((count, quarter, width), lambda p, info: (0, p, 0)), part, part],
            out_specs=[pl.BlockSpec((slots, quarter, width), lambda p, info: (0, p, 0))] * count,
        ),
        compiler_params=pltpu.CompilerParams(vmem_limit_bytes=32 * MIB),
        cost_estimate=cost(0, 4 * count * slots * rows * width),
    )(jnp.stack([place.core, place.chip]).astype(jnp.int32), shard, mine, theirs)
    return [out.reshape(slots * rows, width) for out in outs]


def weight_grads(place, pairs):
    count = len(pairs)
    n, columns = pairs[0][0].shape
    width = pairs[0][1].shape[1]
    half = width // 2
    block = min(768, columns)
    steps = columns // block
    chunk = 256 if block % 256 == 0 else block

    def kernel(info_ref, *refs):
        sides, (keep_ref, give_ref) = refs[: 2 * count], refs[2 * count :]
        keep = pl.multiple_of(info_ref[0] * half, 128)
        give = pl.multiple_of((1 - info_ref[0]) * half, 128)
        for t in range(count):

            @pl.when(pl.program_id(0) // steps == t)
            def _():
                g_ref, a_ref = sides[2 * t], sides[2 * t + 1]
                for start in range(0, block, chunk):
                    at = slice(start, start + chunk)
                    left = g_ref[:, at]
                    keep_ref[0, at, :] = dot_tn(left, a_ref[:, pl.ds(keep, half)]).astype(LOW)
                    give_ref[0, at, :] = dot_tn(left, a_ref[:, pl.ds(give, half)]).astype(LOW)

    def rows_spec(t):
        return pl.BlockSpec(
            (n, block), lambda g, info: (0, jnp.clip(g - t * steps, 0, steps - 1))
        )

    out = pl.BlockSpec((1, block, half), lambda g, info: (g // steps, g % steps, 0))
    in_specs, operands = [], []
    for t, (g, a) in enumerate(pairs):
        in_specs += [rows_spec(t), pl.BlockSpec((n, width), lambda g, info: (0, 0))]
        operands += [g, a]
    return pl.pallas_call(
        kernel,
        out_shape=(jax.ShapeDtypeStruct((count, columns, half), LOW),) * 2,
        grid_spec=pltpu.PrefetchScalarGridSpec(
            num_scalar_prefetch=1,
            grid=(count * steps,),
            in_specs=in_specs,
            out_specs=[out, out],
        ),
        compiler_params=pltpu.CompilerParams(vmem_limit_bytes=48 * MIB),
        cost_estimate=cost(2 * count * n * columns * width, 4 * count * columns * width),
    )(jnp.stack([place.core]).astype(jnp.int32), *operands)


def chip_parts(place, keep, other, groups):
    count, rows, half = keep.shape
    slots = place.tensor
    quarter = rows // slots // 4

    def kernel(info_ref, keep_ref, other_ref, *part_refs):
        for group, part_ref in zip(groups, part_refs, strict=True):
            for at, r in enumerate(group):
                for z in range(slots):
                    start = pl.multiple_of(4 * z * quarter + (info_ref[0] ^ r) * quarter, 16)
                    span = pl.ds(start, quarter)
                    value = keep_ref[0, span, :].astype(F32) + other_ref[0, span, :].astype(F32)
                    part_ref[at, z] = value.astype(LOW)

    row = pl.BlockSpec((1, rows, half), lambda t, info: (t, 0, 0))
    return pl.pallas_call(
        kernel,
        out_shape=[
            jax.ShapeDtypeStruct((count * len(group), slots, quarter, half), LOW) for group in groups
        ],
        grid_spec=pltpu.PrefetchScalarGridSpec(
            num_scalar_prefetch=1,
            grid=(count,),
            in_specs=[row, row],
            out_specs=[
                pl.BlockSpec((len(group), slots, quarter, half), lambda t, info: (t, 0, 0, 0))
                for group in groups
            ],
        ),
        compiler_params=pltpu.CompilerParams(vmem_limit_bytes=32 * MIB),
        cost_estimate=cost(0, 6 * count * rows * half),
    )(jnp.stack([place.chip]).astype(jnp.int32), keep, other)


EACH = ((0,), (1,), (2,), (3,))


def in_chip_sums(owns, others):
    rows, width = owns[0].shape
    block = min(256, rows)

    def kernel(*refs):
        ins, outs = refs[: -len(owns)], refs[-len(owns) :]
        for at, out_ref in enumerate(outs):
            other = ins[len(owns) + at // 2][at % 2]
            out_ref[...] = (ins[at][...].astype(F32) + other.astype(F32)).astype(LOW)

    row = pl.BlockSpec((block, width), lambda b: (b, 0))
    return pl.pallas_call(
        kernel,
        grid=(rows // block,),
        out_shape=[jax.ShapeDtypeStruct((rows, width), LOW)] * len(owns),
        in_specs=[row] * len(owns)
        + [pl.BlockSpec((2, block, width), lambda b: (0, b, 0))] * len(others),
        out_specs=[row] * len(owns),
        compiler_params=pltpu.CompilerParams(vmem_limit_bytes=32 * MIB),
        cost_estimate=cost(0, 6 * len(owns) * rows * width),
    )(*owns, *others)


def memory_grad(dk, dv, other, w_key, w_value):
    rows, width = dk.shape
    block = min(256, rows)

    def kernel(dk_ref, dv_ref, other_ref, wk_ref, wv_ref, k_ref, v_ref, out_ref):
        k = (dk_ref[...].astype(F32) + other_ref[0].astype(F32)).astype(LOW)
        v = (dv_ref[...].astype(F32) + other_ref[1].astype(F32)).astype(LOW)
        k_ref[...] = k
        v_ref[...] = v
        out_ref[...] = (dot_nn(k, wk_ref[...]) + dot_nn(v, wv_ref[...])).astype(LOW)

    row = pl.BlockSpec((block, width), lambda b: (b, 0))
    return pl.pallas_call(
        kernel,
        grid=(rows // block,),
        out_shape=[jax.ShapeDtypeStruct((rows, width), LOW)] * 3,
        in_specs=[
            row, row, pl.BlockSpec((2, block, width), lambda b: (0, b, 0)),
            whole(w_key.shape), whole(w_value.shape),
        ],
        out_specs=[row] * 3,
        compiler_params=pltpu.CompilerParams(vmem_limit_bytes=40 * MIB),
        cost_estimate=cost(4 * rows * width * width, 8 * MIB),
    )(dk, dv, other, w_key, w_value)


def input_grad(resid, halves, weights):
    rows, width = resid.shape
    block = min(256, rows)
    half = width // 2

    def kernel(r_ref, *refs):
        out_ref = refs[-1]
        total = r_ref[...]
        for t in range(len(weights)):
            for side in range(2):
                w = refs[len(halves) + t][side * half : (side + 1) * half, :]
                total = total + dot_nn(refs[2 * t + side][...], w)
        out_ref[...] = total.astype(LOW)

    row = pl.BlockSpec((block, width), lambda b: (b, 0))
    return pl.pallas_call(
        kernel,
        grid=(rows // block,),
        out_shape=jax.ShapeDtypeStruct((rows, width), LOW),
        in_specs=[row]
        + [pl.BlockSpec((block, half), lambda b: (b, 0))] * len(halves)
        + [whole((width, width))] * len(weights),
        out_specs=row,
        compiler_params=pltpu.CompilerParams(vmem_limit_bytes=40 * MIB),
        cost_estimate=cost(2 * len(weights) * rows * width * width, 8 * MIB),
    )(resid, *halves, *weights)


def swap_chips(place, parts):
    return [swap(parts[r], "dp", 2 * r, place.dp) for r in range(1, 4)]


def add_all(own, others):
    own = own.astype(F32)
    for other in others:
        own = own + other.astype(F32)
    return own


def near_parts(place, total, natural):
    def slot(r):
        if natural:
            return lax.dynamic_index_in_dim(total, place.z ^ r, 1, False)
        return total[:, r]

    stay, leave = jnp.stack([slot(0), slot(2)]), jnp.stack([slot(1), slot(3)])
    return stay, leave.astype(LOW)


def add_far(place, total, other):
    piece = total[0] + other.astype(F32)
    bit = 8
    while bit < place.dp:
        piece = piece + swap(piece.astype(LOW), "dp", bit, place.dp).astype(F32)
        bit *= 2
    return piece.astype(LOW)


def regather(place, piece, *deps):
    own = jnp.stack(from_chips(place, piece, *deps))
    return own, swap(own, "dp", 1, place.dp)


def finish(place, own, other, groups):
    _, count, quarter, half = own.shape
    rows, width = 4 * quarter, 2 * half

    def kernel(info_ref, own_ref, other_ref, *out_refs):
        core, chip = info_ref[0], info_ref[1]
        t = 0
        for group, out_ref in zip(groups, out_refs, strict=True):
            for g in range(group):
                for p in range(4):
                    at = slice(p * quarter, (p + 1) * quarter)
                    mine, theirs = own_ref[p ^ chip, t].astype(F32), other_ref[p ^ chip, t].astype(F32)
                    out_ref[g, at, :half] = jnp.where(core == 0, mine, theirs)
                    out_ref[g, at, half:] = jnp.where(core == 0, theirs, mine)
                t += 1

    shapes = [(group, rows, width) for group in groups]
    return pl.pallas_call(
        kernel,
        out_shape=[jax.ShapeDtypeStruct(shape, F32) for shape in shapes],
        grid_spec=pltpu.PrefetchScalarGridSpec(
            num_scalar_prefetch=1,
            grid=(1,),
            in_specs=[whole(own.shape), whole(own.shape)],
            out_specs=[whole(shape) for shape in shapes],
        ),
        compiler_params=pltpu.CompilerParams(vmem_limit_bytes=48 * MIB),
        cost_estimate=cost(0, 6 * count * rows * width),
    )(jnp.stack([place.core, place.chip]).astype(jnp.int32), own, other)


def finish_ffn(parts):
    _, _, quarter, half = parts.shape
    rows, width = 4 * quarter, 2 * half

    def kernel(parts_ref, down_ref, up_ref):
        for side in range(2):
            columns = slice(side * half, (side + 1) * half)
            for q in range(4):
                at = slice(q * quarter, (q + 1) * quarter)
                down_ref[at, columns] = parts_ref[2 * q + side, 0].astype(F32)
            full = jnp.concatenate([parts_ref[2 * q + side, 1] for q in range(4)], 0)
            up_ref[columns, :] = full.astype(F32).T

    return pl.pallas_call(
        kernel,
        out_shape=(jax.ShapeDtypeStruct((rows, width), F32), jax.ShapeDtypeStruct((width, rows), F32)),
        compiler_params=pltpu.CompilerParams(vmem_limit_bytes=32 * MIB),
        cost_estimate=cost(0, 12 * rows * width),
    )(parts)


def local(
    inputs, memory, cotangent, dec_len, mem_len,
    self_qkv, self_out, cross_q, cross_kv, cross_out, ffn_in, ffn_out, ln_gain, ln_bias,
):
    place = Place()
    dp, slots = place.dp, place.tensor
    axes = ("dp", "tensor")
    width = inputs.shape[3]
    length = inputs.shape[2]
    block = length // slots
    micro = place.z // 2
    owner = place.core == (place.z & 1)
    fetch_perm = [
        (d * slots + t, (d ^ 1) * slots + t)
        for d in range(dp)
        for t in range(slots)
        if d % 2 == t % 2
    ]
    spread = []
    for call in range(2):
        spread.append(
            [
                ((g + hh) * slots + s, (g + s % 2) * slots + OWN_BLOCKS[hh][(call + s // 2) % 2])
                for g in range(0, dp, 2)
                for s in range(slots)
                for hh in range(2)
            ]
        )
    collect = [[(dst, src) for src, dst in perm] for perm in spread]

    def fetch(value):
        mine = lax.dynamic_index_in_dim(value, micro, 0, False)[0]
        return jnp.where(owner, mine, lax.ppermute(mine, axes, fetch_perm))

    def own_rows(value):
        return jnp.concatenate(
            [
                lax.dynamic_slice_in_dim(value, place.core * block, block, 0),
                lax.dynamic_slice_in_dim(value, (3 - place.core) * block, block, 0),
            ],
            0,
        )

    def start_rows(value):
        return [
            lax.ppermute(
                lax.dynamic_slice_in_dim(value, ((call + micro) % 2) * block, block, 0), axes, spread[call]
            )
            for call in range(2)
        ]

    def end_rows(got):
        near = place.z // 2 == 0
        return jnp.stack([jnp.where(near, got[0], got[1]), jnp.where(near, got[1], got[0])])[:, None]

    def collect_rows(value):
        return [
            lax.ppermute(
                lax.dynamic_index_in_dim(value, (place.z // 2 + call) % 2, 0, False)[0], axes, collect[call]
            )
            for call in range(2)
        ]


    def flat(weights):
        return weights.reshape(-1, width)

    index = lax.axis_index("dp")
    at_ffn = ffn_out.shape[0] // dp
    piece_ffn = jnp.stack(
        [
            lax.dynamic_slice_in_dim(ffn_in, index * at_ffn, at_ffn, 1).T,
            lax.dynamic_slice_in_dim(ffn_out, index * at_ffn, at_ffn, 0),
        ]
    )
    shard_qkv = jnp.swapaxes(self_qkv, 1, 2)
    shard_mid = jnp.concatenate(
        [self_out[None], cross_q.T[None], jnp.swapaxes(cross_kv, 1, 2), cross_out[None]], 0
    )
    always = dec_len[0, 0] > 0
    pieces = jnp.concatenate([piece_of(place, shard_qkv), piece_of(place, shard_mid)], 0)
    lengths = jnp.stack([dec_len, mem_len], -1)

    def first_fetch(pieces, *values):
        far = swap(pieces, "tensor", 2, slots)
        x_all, mem_all, lens = (fetch(value) for value in values)
        return far, x_all, mem_all, own_rows(x_all), own_rows(mem_all), lens

    far, x_all, mem_all, x_own, mem_own, lens = beside(
        always, first_fetch, after(pieces, piece_ffn), inputs, memory, lengths
    )
    core = place.core.astype(jnp.int32)
    info_self = jnp.stack([core, lens[0]])
    info_cross = jnp.stack([core, lens[1]])
    got = in_slots(swap(near_pair(pieces, far), "tensor", 1, slots), far)
    w_ffn = lax.all_gather(after(piece_ffn, got), ("tensor", "dp"), axis=0)
    got_qkv = jnp.stack(from_chips(place, got[:, :3]))
    wq, wk, wv = assemble(place, shard_qkv, got_qkv, swap(got_qkv, "dp", 1, dp))

    def self_forward(got, rows, x_own, x_all, wq, wk, wv, info):
        query = dot_nt(x_own, wq).astype(LOW)
        key = dot_nt(x_all, wk).astype(LOW)
        value = dot_nt(x_all, wv).astype(LOW)
        return (
            swap_chips(place, [got] * 4),
            collect_rows(rows),
            (query, key, value),
            attend_forward(True, info, query, key, value),
        )

    others, got_y, (query_s, key_s, value_s), (attn_s, logs_s) = beside(
        always, self_forward, got[:, 3:], cotangent, x_own, x_all, wq, wk, wv, info_self
    )
    got_mid = jnp.stack([got[:, 3:], *others])
    w_so, w_cq, w_ck, w_cv, w_co = assemble(
        place, shard_mid, got_mid, swap(got_mid, "dp", 1, dp)
    )
    grad_y = jnp.concatenate(
        [jnp.where(micro == 0, got_y[0], got_y[1]), jnp.where(micro == 0, got_y[1], got_y[0])], 0
    )
    normed_one, rstd_one, h1_low, query_c = first_norm(
        attn_s, x_own, w_so, w_cq, ln_gain, ln_bias
    )
    key_c = dot_nt(mem_all, w_ck).astype(LOW)
    value_c = dot_nt(mem_all, w_cv).astype(LOW)
    attn_c, logs_c = attend_forward(False, info_cross, query_c, key_c, value_c)
    (out_rows, act, grad_pre, grad_b3, h2_low, grad_b2, grad_oc, grad_r2, sums_late) = middle(
        normed_one, attn_c, grad_y, w_co, w_ffn, ln_gain, ln_bias
    )

    keep_down, give_down = weight_grads(place, [(act, grad_b3)])

    def up_grads(give, *pair):
        return swap(give, "dp", 1, dp), weight_grads(place, [pair])

    other_down, (keep_up, give_up) = beside(always, up_grads, give_down, grad_pre, h2_low)
    other_up = swap(give_up, "dp", 1, dp)
    own_down, on_down, first_down = chip_parts(place, keep_down, other_down, ((0,), (2,), (1, 3)))
    own_up, on_up, first_up = chip_parts(place, keep_up, other_up, ((0,), (1,), (2, 3)))

    def cross_back(first_down, first_up, rows, *operands):
        return (
            swap(first_down, "dp", 2, dp),
            swap(first_up, "dp", 4, dp),
            start_rows(rows),
            attend_backward(False, (0, 1), *operands),
        )

    from_down, from_up, got_out, (dq_c, dk_c, dv_c, give_c) = beside(
        always, cross_back, first_down, first_up, out_rows,
        info_cross, query_c, key_c, value_c, attn_c, logs_c, grad_oc,
    )

    def in_chip(own, other):
        return (own.astype(F32) + other.astype(F32)).astype(LOW)

    other_c = swap(give_c, "dp", 1, dp)
    grad_r1, grad_b1, grad_os, sums_first = first_norm_back(
        grad_r2, dq_c, normed_one, rstd_one, w_cq, w_so, ln_gain
    )
    dk_c, dv_c, d_mem = memory_grad(dk_c, dv_c, other_c, w_ck, w_cv)

    def mid_grads(down, up, rows, *sides):
        return (
            swap(down, "dp", 4, dp),
            swap(up, "dp", 2, dp),
            start_rows(rows),
            weight_grads(place, [(sides[2 * t], sides[2 * t + 1]) for t in range(5)]),
        )

    on_down, on_up = in_chip(on_down[0], from_down[1]), in_chip(on_up[0], from_up[1])
    last_down, last_up, got_mem, (keep_mid, give_mid) = beside(
        always, mid_grads, on_down, on_up, d_mem,
        attn_s, grad_b1, dq_c, h1_low, dk_c, mem_own, dv_c, mem_own, attn_c, grad_b2,
    )
    total_ffn = jnp.stack(
        [
            add_all(own_down[0], [from_down[0], last_down]),
            add_all(own_up[0], [from_up[0], last_up]),
        ]
    )
    near_ffn = near_parts(place, total_ffn, True)
    parts_mid = chip_parts(place, keep_mid, swap(give_mid, "dp", 1, dp), EACH)
    sums = sums_late + sums_first
    back_operands = (info_self, query_s, key_s, value_s, attn_s, logs_s, grad_os)

    def self_back_first(part_x, part_y, sums, leave, *operands):
        return (
            swap(part_x, "dp", 2, dp),
            swap(part_y, "dp", 4, dp),
            swap(sums, "dp", 2, dp),
            swap(leave, "tensor", 1, slots),
            attend_backward(True, (0, 2), *operands),
        )

    def self_back_second(part_xy, sums, leave, give, *operands):
        return (
            swap(part_xy, "dp", 6, dp),
            swap(sums, "dp", 4, dp),
            swap(leave, "tensor", 2, slots),
            swap(give, "dp", 1, dp),
            attend_backward(True, (1, 2), *operands),
        )

    from_x, from_y, other_sums, other_ffn, (dq_a, dk_a, dv_a, give_a) = beside(
        always, self_back_first, parts_mid[1], parts_mid[2], sums, near_ffn[1], *back_operands
    )
    sums = sums + other_sums
    far_ffn = near_ffn[0] + other_ffn.astype(F32)
    from_xy, other_sums, other_ffn, other_a, (dq_b, dk_b, dv_b, give_b) = beside(
        always, self_back_second, parts_mid[3], sums, far_ffn[1].astype(LOW), give_a, *back_operands
    )
    sums = sums + other_sums
    piece_ffn = add_far(place, far_ffn, other_ffn)
    other_b = swap(give_b, "dp", 1, dp)
    dk_a, dv_a, dk_b, dv_b = in_chip_sums((dk_a, dv_a, dk_b, dv_b), (other_a, other_b))
    halves = (dq_a, dq_b, dk_a, dk_b, dv_a, dv_b)
    keep_qkv, give_qkv = weight_grads(place, [(side, x_own) for side in halves])
    keep_qkv, give_qkv = (grad.reshape(3, width, -1) for grad in (keep_qkv, give_qkv))
    total_mid = add_all(parts_mid[0], [from_x, from_y, from_xy])
    near_mid = near_parts(place, total_mid, False)

    def input_grads(give, leave, sums, resid, *operands):
        return (
            swap(give, "dp", 1, dp),
            swap(leave, "tensor", 1, slots),
            swap(sums, "dp", 1, dp),
            input_grad(resid, operands[:6], operands[6:]),
        )

    other_qkv, other, other_sums, d_x = beside(
        always, input_grads, give_qkv, near_mid[1], sums, grad_r1, *halves, wq, wk, wv
    )
    sums = sums + other_sums
    bit = 8
    while bit < dp:
        sums = sums + swap(sums, "dp", bit, dp)
        bit *= 2
    far_mid = near_mid[0] + other.astype(F32)
    parts_qkv = chip_parts(place, keep_qkv, other_qkv, EACH)

    def send_qkv(parts, rows, leave):
        return (
            swap_chips(place, [None, *parts]),
            start_rows(rows),
            swap(leave, "tensor", 2, slots),
        )

    others_qkv, got_x, other = beside(
        always, send_qkv, parts_qkv[1:], d_x, far_mid[1].astype(LOW)
    )
    piece_mid = add_far(place, far_mid, other)
    near = near_parts(place, add_all(parts_qkv[0], others_qkv), False)
    d_x = end_rows(got_x).astype(F32)
    d_mem = end_rows(after(got_mem, others_qkv)).astype(F32)
    out = end_rows(after(got_out, others_qkv))
    other, other_sums = after(
        (swap(near[1], "tensor", 1, slots), swap(sums, "tensor", 1, slots)), d_x, d_mem
    )
    sums = sums + other_sums
    far = near[0] + other.astype(F32)
    other, other_sums = after(
        (swap(far[1].astype(LOW), "tensor", 2, slots), swap(sums, "tensor", 2, slots)), out
    )
    sums = sums + other_sums
    piece = jnp.concatenate([add_far(place, far, other), piece_mid], 0)
    groups = [[first + d for d in range(8)] for first in range(0, dp, 8)]
    d_down, d_up = finish_ffn(lax.all_gather(piece_ffn, "dp", axis=0, axis_index_groups=groups))
    own, other = regather(place, piece, d_down, d_up)
    d_qkv, d_so, d_cq, d_ckv, d_co = finish(place, own, other, (3, 1, 1, 2, 1))
    return (
        out,
        d_x,
        d_mem,
        jnp.swapaxes(d_qkv, 1, 2),
        d_so[0],
        d_cq[0].T,
        jnp.swapaxes(d_ckv, 1, 2),
        d_co[0],
        d_up,
        d_down,
        sums[0:3],
        sums[3:6],
    )


def solution(mesh):
    rows = P(None, "dp", "tensor", None)
    in_specs = (
        P(None, "dp", None, None),
        P(None, "dp", None, None),
        rows,
        P(None, "dp"),
        P(None, "dp"),
        P(None, None, "tensor"),
        P("tensor", None),
        P(None, "tensor"),
        P(None, None, "tensor"),
        P("tensor", None),
        P(None, "tensor"),
        P("tensor", None),
        P(),
        P(),
    )
    out_specs = (
        rows,
        rows,
        rows,
        P(None, None, "tensor"),
        P("tensor", None),
        P(None, "tensor"),
        P(None, None, "tensor"),
        P("tensor", None),
        P(None, "tensor"),
        P("tensor", None),
        P(),
        P(),
    )
    return jax.shard_map(local, mesh=mesh, in_specs=in_specs, out_specs=out_specs, check_vma=False)
```

```python
import functools

import jax
import jax.numpy as jnp
from jax import lax
from jax.experimental import pallas as pl
from jax.experimental.pallas import tpu as pltpu
from jax.sharding import PartitionSpec as P

HEAD = 64
EPS = 1e-05
NEG = -1e30
LOW = jnp.bfloat16
F32 = jnp.float32
OWN_BLOCKS = ((0, 3), (1, 2))
MIB = 1024 * 1024


def dot_nn(left, right):
    return lax.dot_general(left, right, (((1,), (0,)), ((), ())), preferred_element_type=F32)


def dot_nt(left, right):
    return lax.dot_general(left, right, (((1,), (1,)), ((), ())), preferred_element_type=F32)


def dot_tn(left, right):
    return lax.dot_general(left, right, (((0,), (0,)), ((), ())), preferred_element_type=F32)


def cost(flops, size, trans=0):
    return pl.CostEstimate(flops=int(flops), bytes_accessed=int(size), transcendentals=int(trans))


def whole(shape):
    return pl.BlockSpec(shape, lambda *_: (0,) * len(shape), pipeline_mode=pl.Buffered(1))


def attend_forward(causal, info, query, keys_in, values_in):
    rows, width = query.shape
    key_rows = keys_in.shape[0]
    block = rows // 2
    pair = 2 * HEAD

    def kernel(info_ref, q_ref, k_ref, v_ref, o_ref, lse_ref):
        length = info_ref[1]

        def part(spot, block_id, extent):
            lane = lax.broadcasted_iota(jnp.int32, (block, pair), 1)
            limit = jnp.full((block, 1), length, jnp.int32)
            if causal:
                row = block_id * block + lax.broadcasted_iota(jnp.int32, (block, 1), 0)
                limit = jnp.minimum(limit, row + 1)
            allowed = lax.broadcasted_iota(jnp.int32, (block, extent), 1) < limit
            span = pl.ds(spot * block, block)
            q = q_ref[span, :]
            out, logs = None, None
            for side in range(2):
                mine = (lane >= HEAD) if side else (lane < HEAD)
                q_side = jnp.where(mine, q, 0).astype(LOW) * LOW(HEAD ** (-0.5))
                scores = jnp.where(allowed, dot_nt(q_side, k_ref[:extent, :]), NEG)
                peak = jnp.max(scores, -1, keepdims=True)
                weights = jnp.exp(scores - peak)
                total = jnp.sum(weights, -1, keepdims=True)
                mixed = dot_nn(weights.astype(LOW), v_ref[:extent, :]) / total
                log_total = peak + jnp.log(total)
                if side:
                    out = jnp.where(mine, mixed, out)
                    logs = jnp.where(mine, log_total, logs)
                else:
                    out, logs = mixed, jnp.broadcast_to(log_total, (block, pair))
            o_ref[span, :] = out.astype(LOW)
            lse_ref[span, :] = logs

        if causal:
            for variant in range(2):

                @pl.when(info_ref[0] == variant)
                def _():
                    for spot in range(2):
                        block_id = OWN_BLOCKS[variant][spot]
                        part(spot, block_id, (block_id + 1) * block)
        else:
            for spot in range(2):
                part(spot, 0, key_rows)

    column = pl.BlockSpec((rows, pair), lambda p, *_: (0, p))
    key_column = pl.BlockSpec((key_rows, pair), lambda p, *_: (0, p))
    share = 0.625 if causal else 1.0
    elements = width // HEAD * rows * key_rows * share
    return pl.pallas_call(
        kernel,
        out_shape=(
            jax.ShapeDtypeStruct((rows, width), LOW),
            jax.ShapeDtypeStruct((rows, width), F32),
        ),
        grid_spec=pltpu.PrefetchScalarGridSpec(
            num_scalar_prefetch=1,
            grid=(width // pair,),
            in_specs=[column, key_column, key_column],
            out_specs=[column, column],
        ),
        compiler_params=pltpu.CompilerParams(vmem_limit_bytes=48 * MIB),
        cost_estimate=cost(elements * 1024, 10 * MIB, elements),
    )(info, query, keys_in, values_in)


def attend_backward(causal, share_of, info, query, keys_in, values_in, out, logs, grad_out):
    rows, width = query.shape[0], query.shape[1] // share_of[1]
    skip = share_of[0] * width // (2 * HEAD)
    key_rows = keys_in.shape[0]
    block = rows // 2
    pair = 2 * HEAD

    def kernel(
        info_ref, q_ref, k_ref, v_ref, o_ref, lse_ref, g_ref,
        dq_ref, dk_ref, dv_ref, give_ref, dk_acc, dv_acc,
    ):
        length = info_ref[1]
        dk_acc[...] = jnp.zeros_like(dk_acc)
        dv_acc[...] = jnp.zeros_like(dv_acc)

        def part(spot, block_id, extent):
            lane = lax.broadcasted_iota(jnp.int32, (block, pair), 1)
            limit = jnp.full((block, 1), length, jnp.int32)
            if causal:
                row = block_id * block + lax.broadcasted_iota(jnp.int32, (block, 1), 0)
                limit = jnp.minimum(limit, row + 1)
            allowed = lax.broadcasted_iota(jnp.int32, (block, extent), 1) < limit
            span = pl.ds(spot * block, block)
            q = q_ref[span, :]
            g = g_ref[span, :]
            along = g.astype(F32) * o_ref[span, :].astype(F32)
            dq = None
            for side in range(2):
                mine = (lane >= HEAD) if side else (lane < HEAD)
                q_side = jnp.where(mine, q, 0).astype(LOW) * LOW(HEAD ** (-0.5))
                g_side = jnp.where(mine, g, 0).astype(LOW)
                inner = jnp.sum(jnp.where(mine, along, 0.0), -1, keepdims=True)
                log_total = lse_ref[span, side * HEAD : side * HEAD + 1]
                scores = jnp.where(allowed, dot_nt(q_side, k_ref[:extent, :]), NEG)
                weights = jnp.exp(scores - log_total)
                dv_acc[:extent, :] += dot_tn(weights.astype(LOW), g_side)
                grad_w = dot_nt(g_side, v_ref[:extent, :])
                grad_s = (weights * (grad_w - inner)).astype(LOW)
                dk_acc[:extent, :] += dot_tn(grad_s, q_side)
                part_q = dot_nn(grad_s, k_ref[:extent, :])
                dq = jnp.where(mine, part_q, dq) if side else part_q
            dq_ref[span, :] = (dq * HEAD ** (-0.5)).astype(LOW)

        for variant in range(2):

            @pl.when(info_ref[0] == variant)
            def _():
                for spot in range(2):
                    block_id = OWN_BLOCKS[variant][spot]
                    part(spot, block_id, (block_id + 1) * block if causal else key_rows)
                for spot in range(2):
                    keep = slice(OWN_BLOCKS[variant][spot] * block, (OWN_BLOCKS[variant][spot] + 1) * block)
                    give = slice(OWN_BLOCKS[1 - variant][spot] * block, (OWN_BLOCKS[1 - variant][spot] + 1) * block)
                    span = slice(spot * block, (spot + 1) * block)
                    dk_ref[span, :] = dk_acc[keep, :].astype(LOW)
                    dv_ref[span, :] = dv_acc[keep, :].astype(LOW)
                    give_ref[0, span, :] = dk_acc[give, :].astype(LOW)
                    give_ref[1, span, :] = dv_acc[give, :].astype(LOW)

    column = pl.BlockSpec((rows, pair), lambda p, *_: (0, p + skip))
    key_column = pl.BlockSpec((key_rows, pair), lambda p, *_: (0, p + skip))
    single = pl.BlockSpec((rows, pair), lambda p, *_: (0, p))
    double = pl.BlockSpec((2, rows, pair), lambda p, *_: (0, 0, p))
    share = 0.625 if causal else 1.0
    elements = width // HEAD * rows * key_rows * share
    return pl.pallas_call(
        kernel,
        out_shape=(jax.ShapeDtypeStruct((rows, width), LOW),) * 3
        + (jax.ShapeDtypeStruct((2, rows, width), LOW),),
        grid_spec=pltpu.PrefetchScalarGridSpec(
            num_scalar_prefetch=1,
            grid=(width // pair,),
            in_specs=[column, key_column, key_column, column, column, column],
            out_specs=[single, single, single, double],
            scratch_shapes=[pltpu.VMEM((key_rows, pair), F32), pltpu.VMEM((key_rows, pair), F32)],
        ),
        compiler_params=pltpu.CompilerParams(vmem_limit_bytes=48 * MIB),
        cost_estimate=cost(elements * 2560, 10 * MIB, elements),
    )(info, query, keys_in, values_in, out, logs, grad_out)


def normalize(resid):
    center = resid - jnp.mean(resid, -1, keepdims=True)
    rstd = lax.rsqrt(jnp.mean(center * center, -1, keepdims=True) + EPS)
    return center * rstd, rstd


def norm_back(grad, gain, normed, rstd):
    dn = grad * gain
    mean_dn = jnp.mean(dn, -1, keepdims=True)
    mean_dnn = jnp.mean(dn * normed, -1, keepdims=True)
    return rstd * (dn - mean_dn - normed * mean_dnn)


def row_sum(value):
    return jnp.sum(value, 0, keepdims=True)


def first_norm(attn, x_rows, w_out, w_query, gain, shift):
    rows, width = attn.shape
    block = min(256, rows)

    def kernel(o_ref, x_ref, wo_ref, wq_ref, g_ref, s_ref, n_ref, r_ref, h_ref, q_ref):
        normed, rstd = normalize(x_ref[...].astype(F32) + dot_nn(o_ref[...], wo_ref[...]))
        n_ref[...] = normed
        r_ref[...] = jnp.broadcast_to(rstd, r_ref.shape)
        low = (normed * g_ref[0:1, :] + s_ref[0:1, :]).astype(LOW)
        h_ref[...] = low
        q_ref[...] = dot_nt(low, wq_ref[...]).astype(LOW)

    row = pl.BlockSpec((block, width), lambda b: (b, 0))
    thin = pl.BlockSpec((block, 128), lambda b: (b, 0))
    return pl.pallas_call(
        kernel,
        grid=(rows // block,),
        out_shape=(
            jax.ShapeDtypeStruct((rows, width), F32),
            jax.ShapeDtypeStruct((rows, 128), F32),
            jax.ShapeDtypeStruct((rows, width), LOW),
            jax.ShapeDtypeStruct((rows, width), LOW),
        ),
        in_specs=[row, row, whole(w_out.shape), whole(w_query.shape), whole(gain.shape), whole(shift.shape)],
        out_specs=[row, thin, row, row],
        compiler_params=pltpu.CompilerParams(vmem_limit_bytes=40 * MIB),
        cost_estimate=cost(4 * rows * width * width, 8 * MIB),
    )(attn, x_rows, w_out, w_query, gain, shift)


def gelu_parts(u):
    t = 1.0 / (1.0 + (0.3275911 * 0.7071067811865476) * jnp.abs(u))
    bell = jnp.exp(-0.5 * u * u)
    poly = t * (0.254829592 + t * (-0.284496736 + t * (1.421413741 + t * (-1.453152027 + t * 1.061405429))))
    tail = 0.5 * poly * bell
    return jnp.where(u < 0, tail, 1.0 - tail), bell * 0.3989422804014327


def middle(normed_one, attn, grad_y, w_out, w_ffn, gain, shift):
    rows, width = attn.shape
    parts, _, part, _ = w_ffn.shape
    hidden = parts * part
    block = min(256, rows)
    step = min(768, hidden)

    def kernel(
        n0_ref, o_ref, y_ref, wo_ref, w_ref, g_ref, s_ref,
        out_ref, a_ref, du_ref, db3_ref, h2_ref, db2_ref, do_ref, dr2_ref, sums_ref, slope_ref,
    ):
        @pl.when(pl.program_id(0) == 0)
        def _():
            sums_ref[...] = jnp.zeros_like(sums_ref)

        def weight(which, start):
            return w_ref[start // part : (start + step) // part, which].reshape(step, width)

        h1 = n0_ref[...] * g_ref[0:1, :] + s_ref[0:1, :]
        n1, rstd1 = normalize(h1 + dot_nn(o_ref[...], wo_ref[...]))
        h2 = n1 * g_ref[1:2, :] + s_ref[1:2, :]
        h2_low = h2.astype(LOW)
        h2_ref[...] = h2_low
        branch = None
        for start in range(0, hidden, step):
            span = slice(start, start + step)
            u = dot_nt(h2_low, weight(0, start))
            share, density = gelu_parts(u)
            slope_ref[:, span] = share + u * density
            a = (u * share).astype(LOW)
            a_ref[:, span] = a
            term = dot_nn(a, weight(1, start))
            branch = term if branch is None else branch + term
        n2, rstd2 = normalize(h2 + branch)
        out_ref[...] = (n2 * g_ref[2:3, :] + s_ref[2:3, :]).astype(LOW)
        g = y_ref[...].astype(F32)
        sums_ref[2:3, :] += row_sum(g * n2)
        sums_ref[5:6, :] += row_sum(g)
        dr3 = norm_back(g, g_ref[2:3, :], n2, rstd2)
        db3 = dr3.astype(LOW)
        db3_ref[...] = db3
        dh2 = dr3
        for start in range(0, hidden, step):
            span = slice(start, start + step)
            du = (dot_nt(db3, weight(1, start)) * slope_ref[:, span]).astype(LOW)
            du_ref[:, span] = du
            dh2 = dh2 + dot_nn(du, weight(0, start))
        sums_ref[1:2, :] += row_sum(dh2 * n1)
        sums_ref[4:5, :] += row_sum(dh2)
        dr2 = norm_back(dh2, g_ref[1:2, :], n1, rstd1)
        dr2_ref[...] = dr2
        db2 = dr2.astype(LOW)
        db2_ref[...] = db2
        do_ref[...] = dot_nt(db2, wo_ref[...]).astype(LOW)

    row = pl.BlockSpec((block, width), lambda b: (b, 0))
    broad = pl.BlockSpec((block, hidden), lambda b: (b, 0))
    low_row = jax.ShapeDtypeStruct((rows, width), LOW)
    low_broad = jax.ShapeDtypeStruct((rows, hidden), LOW)
    return pl.pallas_call(
        kernel,
        grid=(rows // block,),
        out_shape=(
            low_row, low_broad, low_broad, low_row, low_row, low_row, low_row,
            jax.ShapeDtypeStruct((rows, width), F32),
            jax.ShapeDtypeStruct((8, width), F32),
        ),
        in_specs=[
            row, row, row, whole(w_out.shape), whole(w_ffn.shape), whole(gain.shape),
            whole(shift.shape),
        ],
        out_specs=[
            row, broad, broad, row, row, row, row, row,
            pl.BlockSpec((8, width), lambda b: (0, 0)),
        ],
        scratch_shapes=[pltpu.VMEM((block, hidden), F32)],
        compiler_params=pltpu.CompilerParams(vmem_limit_bytes=50 * MIB),
        cost_estimate=cost(rows * width * (8 * hidden + 4 * width), 24 * MIB, rows * hidden),
    )(normed_one, attn, grad_y, w_out, w_ffn, gain, shift)


def first_norm_back(grad_resid, grad_query, normed_one, rstd_one, w_query, w_out, gain):
    rows, width = grad_resid.shape
    block = min(256, rows)

    def kernel(dr2_ref, dq_ref, n_ref, r_ref, wq_ref, wo_ref, g_ref, dr1_ref, db1_ref, do_ref, sums_ref):
        @pl.when(pl.program_id(0) == 0)
        def _():
            sums_ref[...] = jnp.zeros_like(sums_ref)

        normed = n_ref[...]
        dh1 = dr2_ref[...] + dot_nn(dq_ref[...], wq_ref[...])
        sums_ref[0:1, :] += row_sum(dh1 * normed)
        sums_ref[3:4, :] += row_sum(dh1)
        dr1 = norm_back(dh1, g_ref[0:1, :], normed, r_ref[:, 0:1])
        dr1_ref[...] = dr1
        db1 = dr1.astype(LOW)
        db1_ref[...] = db1
        do_ref[...] = dot_nt(db1, wo_ref[...]).astype(LOW)

    row = pl.BlockSpec((block, width), lambda b: (b, 0))
    thin = pl.BlockSpec((block, 128), lambda b: (b, 0))
    low_row = jax.ShapeDtypeStruct((rows, width), LOW)
    return pl.pallas_call(
        kernel,
        grid=(rows // block,),
        out_shape=(
            jax.ShapeDtypeStruct((rows, width), F32), low_row, low_row,
            jax.ShapeDtypeStruct((8, width), F32),
        ),
        in_specs=[row, row, row, thin, whole(w_query.shape), whole(w_out.shape), whole(gain.shape)],
        out_specs=[row, row, row, pl.BlockSpec((8, width), lambda b: (0, 0))],
        compiler_params=pltpu.CompilerParams(vmem_limit_bytes=40 * MIB),
        cost_estimate=cost(4 * rows * width * width, 8 * MIB),
    )(grad_resid, grad_query, normed_one, rstd_one, w_query, w_out, gain)


def swap(value, axis, bit, size):
    return lax.ppermute(value, axis, [(d, d ^ bit) for d in range(size)])


def ordered(own, other, bit, axis):
    low = jnp.where(bit, other, own)
    high = jnp.where(bit, own, other)
    return jnp.concatenate([low, high], axis)


class Place:
    def __init__(self):
        self.dp = lax.axis_size("dp")
        self.tensor = lax.axis_size("tensor")
        index = lax.axis_index("dp")
        self.z = lax.axis_index("tensor")
        self.core = index & 1
        self.chip = (index >> 1) & 3


def after(value, *deps):
    return lax.optimization_barrier((value, deps))[0]


def beside(always, work, *operands):
    def nothing(*operands):
        return jax.tree.map(lambda leaf: jnp.zeros(leaf.shape, leaf.dtype), jax.eval_shape(work, *operands))

    return lax.optimization_barrier(
        lax.cond(always, work, nothing, *lax.optimization_barrier(operands))
    )


def piece_of(place, shard):
    count, rows, width = shard.shape
    return lax.dynamic_slice(
        shard,
        (0, place.chip * (rows // 4), place.core * (width // 2)),
        (count, rows // 4, width // 2),
    )


def near_pair(piece, far):
    return jnp.stack([piece, far])


def in_slots(near, far):
    return jnp.stack([near[0], far, near[1]])


def from_chips(place, got, *deps):
    others = [swap(got, "dp", 2 * r, place.dp) for r in range(1, 4)]
    if deps:
        others = after(others, *deps)
    return [got, *others]


def assemble(place, shard, mine, theirs):
    count, rows, width = shard.shape
    quarter, half, slots = rows // 4, width // 2, mine.shape[1] + 1

    def kernel(info_ref, shard_ref, mine_ref, theirs_ref, *out_refs):
        def fill(left, right):
            for t, out_ref in enumerate(out_refs):
                out_ref[0] = shard_ref[t]
                for r in range(1, slots):
                    out_ref[r, :, :half] = left[0, r - 1, t]
                    out_ref[r, :, half:] = right[0, r - 1, t]

        @pl.when(info_ref[0] == 0)
        def _():
            fill(mine_ref, theirs_ref)

        @pl.when(info_ref[0] == 1)
        def _():
            fill(theirs_ref, mine_ref)

    def spot(p, info):
        return (p ^ info[1], 0, 0, 0, 0)

    part = pl.BlockSpec((1, slots - 1, count, quarter, half), spot)
    outs = pl.pallas_call(
        kernel,
        out_shape=(jax.ShapeDtypeStruct((slots, rows, width), LOW),) * count,
        grid_spec=pltpu.PrefetchScalarGridSpec(
            num_scalar_prefetch=1,
            grid=(4,),
            in_specs=[pl.BlockSpec((count, quarter, width), lambda p, info: (0, p, 0)), part, part],
            out_specs=[pl.BlockSpec((slots, quarter, width), lambda p, info: (0, p, 0))] * count,
        ),
        compiler_params=pltpu.CompilerParams(vmem_limit_bytes=32 * MIB),
        cost_estimate=cost(0, 4 * count * slots * rows * width),
    )(jnp.stack([place.core, place.chip]).astype(jnp.int32), shard, mine, theirs)
    return [out.reshape(slots * rows, width) for out in outs]


def weight_grads(place, pairs):
    count = len(pairs)
    n, columns = pairs[0][0].shape
    width = pairs[0][1].shape[1]
    half = width // 2
    block = min(768, columns)
    steps = columns // block
    chunk = 256 if block % 256 == 0 else block

    def kernel(info_ref, *refs):
        sides, (keep_ref, give_ref) = refs[: 2 * count], refs[2 * count :]
        keep = pl.multiple_of(info_ref[0] * half, 128)
        give = pl.multiple_of((1 - info_ref[0]) * half, 128)
        for t in range(count):

            @pl.when(pl.program_id(0) // steps == t)
            def _():
                g_ref, a_ref = sides[2 * t], sides[2 * t + 1]
                for start in range(0, block, chunk):
                    at = slice(start, start + chunk)
                    left = g_ref[:, at]
                    keep_ref[0, at, :] = dot_tn(left, a_ref[:, pl.ds(keep, half)]).astype(LOW)
                    give_ref[0, at, :] = dot_tn(left, a_ref[:, pl.ds(give, half)]).astype(LOW)

    def rows_spec(t):
        return pl.BlockSpec(
            (n, block), lambda g, info: (0, jnp.clip(g - t * steps, 0, steps - 1))
        )

    out = pl.BlockSpec((1, block, half), lambda g, info: (g // steps, g % steps, 0))
    in_specs, operands = [], []
    for t, (g, a) in enumerate(pairs):
        in_specs += [rows_spec(t), pl.BlockSpec((n, width), lambda g, info: (0, 0))]
        operands += [g, a]
    return pl.pallas_call(
        kernel,
        out_shape=(jax.ShapeDtypeStruct((count, columns, half), LOW),) * 2,
        grid_spec=pltpu.PrefetchScalarGridSpec(
            num_scalar_prefetch=1,
            grid=(count * steps,),
            in_specs=in_specs,
            out_specs=[out, out],
        ),
        compiler_params=pltpu.CompilerParams(vmem_limit_bytes=48 * MIB),
        cost_estimate=cost(2 * count * n * columns * width, 4 * count * columns * width),
    )(jnp.stack([place.core]).astype(jnp.int32), *operands)


def chip_parts(place, keep, other, groups):
    count, rows, half = keep.shape
    slots = place.tensor
    quarter = rows // slots // 4

    def kernel(info_ref, keep_ref, other_ref, *part_refs):
        for group, part_ref in zip(groups, part_refs, strict=True):
            for at, r in enumerate(group):
                for z in range(slots):
                    start = pl.multiple_of(4 * z * quarter + (info_ref[0] ^ r) * quarter, 16)
                    span = pl.ds(start, quarter)
                    value = keep_ref[0, span, :].astype(F32) + other_ref[0, span, :].astype(F32)
                    part_ref[at, z] = value.astype(LOW)

    row = pl.BlockSpec((1, rows, half), lambda t, info: (t, 0, 0))
    return pl.pallas_call(
        kernel,
        out_shape=[
            jax.ShapeDtypeStruct((count * len(group), slots, quarter, half), LOW) for group in groups
        ],
        grid_spec=pltpu.PrefetchScalarGridSpec(
            num_scalar_prefetch=1,
            grid=(count,),
            in_specs=[row, row],
            out_specs=[
                pl.BlockSpec((len(group), slots, quarter, half), lambda t, info: (t, 0, 0, 0))
                for group in groups
            ],
        ),
        compiler_params=pltpu.CompilerParams(vmem_limit_bytes=32 * MIB),
        cost_estimate=cost(0, 6 * count * rows * half),
    )(jnp.stack([place.chip]).astype(jnp.int32), keep, other)


EACH = ((0,), (1,), (2,), (3,))


def in_chip_sums(owns, others):
    rows, width = owns[0].shape
    block = min(256, rows)

    def kernel(*refs):
        ins, outs = refs[: -len(owns)], refs[-len(owns) :]
        for at, out_ref in enumerate(outs):
            other = ins[len(owns) + at // 2][at % 2]
            out_ref[...] = (ins[at][...].astype(F32) + other.astype(F32)).astype(LOW)

    row = pl.BlockSpec((block, width), lambda b: (b, 0))
    return pl.pallas_call(
        kernel,
        grid=(rows // block,),
        out_shape=[jax.ShapeDtypeStruct((rows, width), LOW)] * len(owns),
        in_specs=[row] * len(owns)
        + [pl.BlockSpec((2, block, width), lambda b: (0, b, 0))] * len(others),
        out_specs=[row] * len(owns),
        compiler_params=pltpu.CompilerParams(vmem_limit_bytes=32 * MIB),
        cost_estimate=cost(0, 6 * len(owns) * rows * width),
    )(*owns, *others)


def memory_grad(dk, dv, other, w_key, w_value):
    rows, width = dk.shape
    block = min(256, rows)

    def kernel(dk_ref, dv_ref, other_ref, wk_ref, wv_ref, k_ref, v_ref, out_ref):
        k = (dk_ref[...].astype(F32) + other_ref[0].astype(F32)).astype(LOW)
        v = (dv_ref[...].astype(F32) + other_ref[1].astype(F32)).astype(LOW)
        k_ref[...] = k
        v_ref[...] = v
        out_ref[...] = (dot_nn(k, wk_ref[...]) + dot_nn(v, wv_ref[...])).astype(LOW)

    row = pl.BlockSpec((block, width), lambda b: (b, 0))
    return pl.pallas_call(
        kernel,
        grid=(rows // block,),
        out_shape=[jax.ShapeDtypeStruct((rows, width), LOW)] * 3,
        in_specs=[
            row, row, pl.BlockSpec((2, block, width), lambda b: (0, b, 0)),
            whole(w_key.shape), whole(w_value.shape),
        ],
        out_specs=[row] * 3,
        compiler_params=pltpu.CompilerParams(vmem_limit_bytes=40 * MIB),
        cost_estimate=cost(4 * rows * width * width, 8 * MIB),
    )(dk, dv, other, w_key, w_value)


def input_grad(resid, halves, weights):
    rows, width = resid.shape
    block = min(256, rows)
    half = width // 2

    def kernel(r_ref, *refs):
        out_ref = refs[-1]
        total = r_ref[...]
        for t in range(len(weights)):
            for side in range(2):
                w = refs[len(halves) + t][side * half : (side + 1) * half, :]
                total = total + dot_nn(refs[2 * t + side][...], w)
        out_ref[...] = total.astype(LOW)

    row = pl.BlockSpec((block, width), lambda b: (b, 0))
    return pl.pallas_call(
        kernel,
        grid=(rows // block,),
        out_shape=jax.ShapeDtypeStruct((rows, width), LOW),
        in_specs=[row]
        + [pl.BlockSpec((block, half), lambda b: (b, 0))] * len(halves)
        + [whole((width, width))] * len(weights),
        out_specs=row,
        compiler_params=pltpu.CompilerParams(vmem_limit_bytes=40 * MIB),
        cost_estimate=cost(2 * len(weights) * rows * width * width, 8 * MIB),
    )(resid, *halves, *weights)


def swap_chips(place, parts):
    return [swap(parts[r], "dp", 2 * r, place.dp) for r in range(1, 4)]


def add_all(own, others):
    own = own.astype(F32)
    for other in others:
        own = own + other.astype(F32)
    return own


def near_parts(place, total, natural):
    def slot(r):
        if natural:
            return lax.dynamic_index_in_dim(total, place.z ^ r, 1, False)
        return total[:, r]

    stay, leave = jnp.stack([slot(0), slot(2)]), jnp.stack([slot(1), slot(3)])
    return stay, leave.astype(LOW)


def add_far(place, total, other):
    piece = total[0] + other.astype(F32)
    bit = 8
    while bit < place.dp:
        piece = piece + swap(piece.astype(LOW), "dp", bit, place.dp).astype(F32)
        bit *= 2
    return piece.astype(LOW)


def regather(place, piece, *deps):
    own = jnp.stack(from_chips(place, piece, *deps))
    return own, swap(own, "dp", 1, place.dp)


def finish(place, own, other, groups):
    _, count, quarter, half = own.shape
    rows, width = 4 * quarter, 2 * half

    def kernel(info_ref, own_ref, other_ref, *out_refs):
        core, chip = info_ref[0], info_ref[1]
        t = 0
        for group, out_ref in zip(groups, out_refs, strict=True):
            for g in range(group):
                for p in range(4):
                    at = slice(p * quarter, (p + 1) * quarter)
                    mine, theirs = own_ref[p ^ chip, t].astype(F32), other_ref[p ^ chip, t].astype(F32)
                    out_ref[g, at, :half] = jnp.where(core == 0, mine, theirs)
                    out_ref[g, at, half:] = jnp.where(core == 0, theirs, mine)
                t += 1

    shapes = [(group, rows, width) for group in groups]
    return pl.pallas_call(
        kernel,
        out_shape=[jax.ShapeDtypeStruct(shape, F32) for shape in shapes],
        grid_spec=pltpu.PrefetchScalarGridSpec(
            num_scalar_prefetch=1,
            grid=(1,),
            in_specs=[whole(own.shape), whole(own.shape)],
            out_specs=[whole(shape) for shape in shapes],
        ),
        compiler_params=pltpu.CompilerParams(vmem_limit_bytes=48 * MIB),
        cost_estimate=cost(0, 6 * count * rows * width),
    )(jnp.stack([place.core, place.chip]).astype(jnp.int32), own, other)


def finish_ffn(parts):
    _, _, quarter, half = parts.shape
    rows, width = 4 * quarter, 2 * half

    def kernel(parts_ref, down_ref, up_ref):
        for side in range(2):
            columns = slice(side * half, (side + 1) * half)
            for q in range(4):
                at = slice(q * quarter, (q + 1) * quarter)
                down_ref[at, columns] = parts_ref[2 * q + side, 0].astype(F32)
            full = jnp.concatenate([parts_ref[2 * q + side, 1] for q in range(4)], 0)
            up_ref[columns, :] = full.astype(F32).T

    return pl.pallas_call(
        kernel,
        out_shape=(jax.ShapeDtypeStruct((rows, width), F32), jax.ShapeDtypeStruct((width, rows), F32)),
        compiler_params=pltpu.CompilerParams(vmem_limit_bytes=32 * MIB),
        cost_estimate=cost(0, 12 * rows * width),
    )(parts)


def local(
    inputs, memory, cotangent, dec_len, mem_len,
    self_qkv, self_out, cross_q, cross_kv, cross_out, ffn_in, ffn_out, ln_gain, ln_bias,
):
    place = Place()
    dp, slots = place.dp, place.tensor
    axes = ("dp", "tensor")
    width = inputs.shape[3]
    length = inputs.shape[2]
    block = length // slots
    micro = place.z // 2
    owner = place.core == (place.z & 1)
    fetch_perm = [
        (d * slots + t, (d ^ 1) * slots + t)
        for d in range(dp)
        for t in range(slots)
        if d % 2 == t % 2
    ]
    spread = []
    for call in range(2):
        spread.append(
            [
                ((g + hh) * slots + s, (g + s % 2) * slots + OWN_BLOCKS[hh][(call + s // 2) % 2])
                for g in range(0, dp, 2)
                for s in range(slots)
                for hh in range(2)
            ]
        )
    collect = [[(dst, src) for src, dst in perm] for perm in spread]

    def fetch(value):
        mine = lax.dynamic_index_in_dim(value, micro, 0, False)[0]
        return jnp.where(owner, mine, lax.ppermute(mine, axes, fetch_perm))

    def own_rows(value):
        return jnp.concatenate(
            [
                lax.dynamic_slice_in_dim(value, place.core * block, block, 0),
                lax.dynamic_slice_in_dim(value, (3 - place.core) * block, block, 0),
            ],
            0,
        )

    def start_row(value, call):
        mine = lax.dynamic_slice_in_dim(value, ((call + micro) % 2) * block, block, 0)
        return lax.ppermute(mine, axes, spread[call])

    def start_rows(value):
        return [start_row(value, call) for call in range(2)]

    def end_rows(got):
        near = place.z // 2 == 0
        return jnp.stack([jnp.where(near, got[0], got[1]), jnp.where(near, got[1], got[0])])[:, None]

    def collect_rows(value):
        return [
            lax.ppermute(
                lax.dynamic_index_in_dim(value, (place.z // 2 + call) % 2, 0, False)[0], axes, collect[call]
            )
            for call in range(2)
        ]


    def flat(weights):
        return weights.reshape(-1, width)

    index = lax.axis_index("dp")
    at_ffn = ffn_out.shape[0] // dp
    piece_ffn = jnp.stack(
        [
            lax.dynamic_slice_in_dim(ffn_in, index * at_ffn, at_ffn, 1).T,
            lax.dynamic_slice_in_dim(ffn_out, index * at_ffn, at_ffn, 0),
        ]
    )
    shard_qkv = jnp.swapaxes(self_qkv, 1, 2)
    shard_mid = jnp.concatenate(
        [self_out[None], cross_q.T[None], jnp.swapaxes(cross_kv, 1, 2), cross_out[None]], 0
    )
    always = dec_len[0, 0] > 0
    pieces = jnp.concatenate([piece_of(place, shard_qkv), piece_of(place, shard_mid)], 0)
    lengths = jnp.stack([dec_len, mem_len], -1)

    def first_fetch(pieces, *values):
        far = swap(pieces, "tensor", 2, slots)
        x_all, mem_all, lens = (fetch(value) for value in values)
        return far, x_all, mem_all, own_rows(x_all), own_rows(mem_all), lens

    far, x_all, mem_all, x_own, mem_own, lens = beside(
        always, first_fetch, after(pieces, piece_ffn), inputs, memory, lengths
    )
    core = place.core.astype(jnp.int32)
    info_self = jnp.stack([core, lens[0]])
    info_cross = jnp.stack([core, lens[1]])
    got = in_slots(swap(near_pair(pieces, far), "tensor", 1, slots), far)
    w_ffn = lax.all_gather(after(piece_ffn, got), ("tensor", "dp"), axis=0)
    got_qkv = jnp.stack(from_chips(place, got[:, :3]))
    wq, wk, wv = assemble(place, shard_qkv, got_qkv, swap(got_qkv, "dp", 1, dp))

    def self_forward(got, rows, x_own, x_all, wq, wk, wv, info):
        query = dot_nt(x_own, wq).astype(LOW)
        key = dot_nt(x_all, wk).astype(LOW)
        value = dot_nt(x_all, wv).astype(LOW)
        return (
            swap_chips(place, [got] * 4),
            collect_rows(rows),
            (query, key, value),
            attend_forward(True, info, query, key, value),
        )

    others, got_y, (query_s, key_s, value_s), (attn_s, logs_s) = beside(
        always, self_forward, got[:, 3:], cotangent, x_own, x_all, wq, wk, wv, info_self
    )
    got_mid = jnp.stack([got[:, 3:], *others])
    w_so, w_cq, w_ck, w_cv, w_co = assemble(
        place, shard_mid, got_mid, swap(got_mid, "dp", 1, dp)
    )
    grad_y = jnp.concatenate(
        [jnp.where(micro == 0, got_y[0], got_y[1]), jnp.where(micro == 0, got_y[1], got_y[0])], 0
    )
    normed_one, rstd_one, h1_low, query_c = first_norm(
        attn_s, x_own, w_so, w_cq, ln_gain, ln_bias
    )
    key_c = dot_nt(mem_all, w_ck).astype(LOW)
    value_c = dot_nt(mem_all, w_cv).astype(LOW)
    attn_c, logs_c = attend_forward(False, info_cross, query_c, key_c, value_c)
    (out_rows, act, grad_pre, grad_b3, h2_low, grad_b2, grad_oc, grad_r2, sums_late) = middle(
        normed_one, attn_c, grad_y, w_co, w_ffn, ln_gain, ln_bias
    )

    keep_down, give_down = weight_grads(place, [(act, grad_b3)])

    def up_grads(give, *pair):
        return swap(give, "dp", 1, dp), weight_grads(place, [pair])

    other_down, (keep_up, give_up) = beside(always, up_grads, give_down, grad_pre, h2_low)
    other_up = swap(give_up, "dp", 1, dp)
    own_down, on_down, first_down = chip_parts(place, keep_down, other_down, ((0,), (2,), (1, 3)))
    own_up, on_up, first_up = chip_parts(place, keep_up, other_up, ((0,), (1,), (2, 3)))

    def cross_back(first_down, first_up, rows, *operands):
        return (
            swap(first_down, "dp", 2, dp),
            swap(first_up, "dp", 4, dp),
            start_row(rows, 0),
            attend_backward(False, (0, 1), *operands),
        )

    from_down, from_up, out_first, (dq_c, dk_c, dv_c, give_c) = beside(
        always, cross_back, first_down, first_up, out_rows,
        info_cross, query_c, key_c, value_c, attn_c, logs_c, grad_oc,
    )

    def in_chip(own, other):
        return (own.astype(F32) + other.astype(F32)).astype(LOW)

    other_c = swap(give_c, "dp", 1, dp)
    grad_r1, grad_b1, grad_os, sums_first = first_norm_back(
        grad_r2, dq_c, normed_one, rstd_one, w_cq, w_so, ln_gain
    )
    dk_c, dv_c, d_mem = memory_grad(dk_c, dv_c, other_c, w_ck, w_cv)

    def mid_grads(down, up, rows, *sides):
        return (
            swap(down, "dp", 4, dp),
            swap(up, "dp", 2, dp),
            start_rows(rows),
            weight_grads(place, [(sides[2 * t], sides[2 * t + 1]) for t in range(5)]),
        )

    on_down, on_up = in_chip(on_down[0], from_down[1]), in_chip(on_up[0], from_up[1])
    last_down, last_up, got_mem, (keep_mid, give_mid) = beside(
        always, mid_grads, on_down, on_up, d_mem,
        attn_s, grad_b1, dq_c, h1_low, dk_c, mem_own, dv_c, mem_own, attn_c, grad_b2,
    )
    total_ffn = jnp.stack(
        [
            add_all(own_down[0], [from_down[0], last_down]),
            add_all(own_up[0], [from_up[0], last_up]),
        ]
    )
    near_ffn = near_parts(place, total_ffn, True)
    parts_mid = chip_parts(place, keep_mid, swap(give_mid, "dp", 1, dp), EACH)
    sums = sums_late + sums_first
    back_operands = (info_self, query_s, key_s, value_s, attn_s, logs_s, grad_os)

    def self_back_first(part_x, part_y, sums, leave, *operands):
        return (
            swap(part_x, "dp", 2, dp),
            swap(part_y, "dp", 4, dp),
            swap(sums, "dp", 2, dp),
            swap(leave, "tensor", 1, slots),
            attend_backward(True, (0, 2), *operands),
        )

    def self_back_second(rows, part_xy, sums, leave, give, *operands):
        return (
            start_row(rows, 1),
            swap(part_xy, "dp", 6, dp),
            swap(sums, "dp", 4, dp),
            swap(leave, "tensor", 2, slots),
            swap(give, "dp", 1, dp),
            attend_backward(True, (1, 2), *operands),
        )

    from_x, from_y, other_sums, other_ffn, (dq_a, dk_a, dv_a, give_a) = beside(
        always, self_back_first, parts_mid[1], parts_mid[2], sums, near_ffn[1], *back_operands
    )
    sums = sums + other_sums
    far_ffn = near_ffn[0] + other_ffn.astype(F32)
    out_second, from_xy, other_sums, other_ffn, other_a, (dq_b, dk_b, dv_b, give_b) = beside(
        always, self_back_second, out_rows, parts_mid[3], sums, far_ffn[1].astype(LOW), give_a, *back_operands
    )
    sums = sums + other_sums
    piece_ffn = add_far(place, far_ffn, other_ffn)
    other_b = swap(give_b, "dp", 1, dp)
    dk_a, dv_a, dk_b, dv_b = in_chip_sums((dk_a, dv_a, dk_b, dv_b), (other_a, other_b))
    halves = (dq_a, dq_b, dk_a, dk_b, dv_a, dv_b)
    keep_qkv, give_qkv = weight_grads(place, [(side, x_own) for side in halves])
    keep_qkv, give_qkv = (grad.reshape(3, width, -1) for grad in (keep_qkv, give_qkv))
    total_mid = add_all(parts_mid[0], [from_x, from_y, from_xy])
    near_mid = near_parts(place, total_mid, False)

    def input_grads(give, leave, sums, resid, *operands):
        return (
            swap(give, "dp", 1, dp),
            swap(leave, "tensor", 1, slots),
            swap(sums, "dp", 1, dp),
            input_grad(resid, operands[:6], operands[6:]),
        )

    other_qkv, other, other_sums, d_x = beside(
        always, input_grads, give_qkv, near_mid[1], sums, grad_r1, *halves, wq, wk, wv
    )
    sums = sums + other_sums
    bit = 8
    while bit < dp:
        sums = sums + swap(sums, "dp", bit, dp)
        bit *= 2
    far_mid = near_mid[0] + other.astype(F32)
    parts_qkv = chip_parts(place, keep_qkv, other_qkv, EACH)

    def send_qkv(parts, rows, leave):
        return (
            swap_chips(place, [None, *parts]),
            start_rows(rows),
            swap(leave, "tensor", 2, slots),
        )

    others_qkv, got_x, other = beside(
        always, send_qkv, parts_qkv[1:], d_x, far_mid[1].astype(LOW)
    )
    piece_mid = add_far(place, far_mid, other)
    near = near_parts(place, add_all(parts_qkv[0], others_qkv), False)
    d_x = end_rows(got_x).astype(F32)
    d_mem = end_rows(after(got_mem, others_qkv)).astype(F32)
    out = end_rows(after([out_first, out_second], others_qkv))
    other, other_sums = after(
        (swap(near[1], "tensor", 1, slots), swap(sums, "tensor", 1, slots)), d_x, d_mem
    )
    sums = sums + other_sums
    far = near[0] + other.astype(F32)
    other, other_sums = after(
        (swap(far[1].astype(LOW), "tensor", 2, slots), swap(sums, "tensor", 2, slots)), out
    )
    sums = sums + other_sums
    piece = jnp.concatenate([add_far(place, far, other), piece_mid], 0)
    groups = [[first + d for d in range(8)] for first in range(0, dp, 8)]
    d_down, d_up = finish_ffn(lax.all_gather(piece_ffn, "dp", axis=0, axis_index_groups=groups))
    own, other = regather(place, piece, d_down, d_up)
    d_qkv, d_so, d_cq, d_ckv, d_co = finish(place, own, other, (3, 1, 1, 2, 1))
    return (
        out,
        d_x,
        d_mem,
        jnp.swapaxes(d_qkv, 1, 2),
        d_so[0],
        d_cq[0].T,
        jnp.swapaxes(d_ckv, 1, 2),
        d_co[0],
        d_up,
        d_down,
        sums[0:3],
        sums[3:6],
    )


def solution(mesh):
    rows = P(None, "dp", "tensor", None)
    in_specs = (
        P(None, "dp", None, None),
        P(None, "dp", None, None),
        rows,
        P(None, "dp"),
        P(None, "dp"),
        P(None, None, "tensor"),
        P("tensor", None),
        P(None, "tensor"),
        P(None, None, "tensor"),
        P("tensor", None),
        P(None, "tensor"),
        P("tensor", None),
        P(),
        P(),
    )
    out_specs = (
        rows,
        rows,
        rows,
        P(None, None, "tensor"),
        P("tensor", None),
        P(None, "tensor"),
        P(None, None, "tensor"),
        P("tensor", None),
        P(None, "tensor"),
        P("tensor", None),
        P(),
        P(),
    )
    return jax.shard_map(local, mesh=mesh, in_specs=in_specs, out_specs=out_specs, check_vma=False)
```
